32 devices in a mesh: wide: 16 (over z, y, core), narrow: 2 (over x).
Axes of the slice: x: 2, y: 2, z: 4, core: 2. Of those that a mesh axis runs over, the one named last changes fastest.
Arguments:
- target: bfloat16 [16, 512, 512], P('wide', 'narrow'), may hold values from -6 to 6
- memory: bfloat16 [16, 512, 512], P('wide', 'narrow'), may hold values from -6 to 6
- target_lens: int32 [16, 8], P('wide'), may hold values from 1 to 384, as said below
- source_lens: int32 [16, 8], P('wide'), may hold values from 1 to 384, as said below
- self_in: bfloat16 [512, 1536], replicated, may hold values from -0.25 to 0.25
- self_out: bfloat16 [512, 512], replicated, may hold values from -1 to 1
- cross_q: bfloat16 [512, 512], replicated, may hold values from -0.25 to 0.25
- cross_kv: bfloat16 [512, 1024], replicated, may hold values from -0.25 to 0.25
- cross_out: bfloat16 [512, 512], replicated, may hold values from -1 to 1
- ffn_in: bfloat16 [512, 2048], replicated, may hold values from -0.25 to 0.25
- ffn_in_bias: float32 [2048], replicated, may hold values from -3 to 3
- ffn_out: bfloat16 [2048, 512], replicated, may hold values from -0.125 to 0.125
- ffn_out_bias: float32 [512], replicated, may hold values from -3 to 3
- norm_gain: float32 [3, 512], replicated, may hold values from 0.1 to 1.9
- norm_bias: float32 [3, 512], replicated, may hold values from -3 to 3
- cotangent: bfloat16 [16, 512, 512], P('wide', 'narrow'), may hold values from -6 to 6
Outputs:
- output: bfloat16 [16, 512, 512], P('wide', 'narrow')
- target_grad: float32 [16, 512, 512], P('wide', 'narrow')
- memory_grad: float32 [16, 512, 512], P('wide', 'narrow')
- self_in_grad: float32 [512, 1536], P('narrow')
- self_out_grad: float32 [512, 512], P('narrow')
- cross_q_grad: float32 [512, 512], P('narrow')
- cross_kv_grad: float32 [512, 1024], P('narrow')
- cross_out_grad: float32 [512, 512], P('narrow')
- ffn_in_grad: float32 [512, 2048], P('narrow')
- ffn_in_bias_grad: float32 [2048], P('narrow')
- ffn_out_grad: float32 [2048, 512], P('narrow')
- ffn_out_bias_grad: float32 [512], P('narrow')
- norm_gain_grad: float32 [3, 512], P(None, 'narrow')
- norm_bias_grad: float32 [3, 512], P(None, 'narrow')
The draws below stay inside these ranges and needn't reach their ends.
Inputs may be any that keep to these rules, and one draw needn't show every extreme that they name: `target_lens`: row b holds 8 target documents in order with these lengths; positions after their sum are padding. Target document j attends to source document j. `source_lens`: row b holds 8 source documents in order with these lengths; positions after their sum are padding.
All inputs are finite; a program needn't handle non-finite values.
Results may differ from the reference program's by a relative error of at most 0.025.
Values may be sent and summed in bfloat16 or wider, within the bound.
No kernel may reach another device: no remote copies, remote signals or barrier semaphores. Data moves between devices by JAX's collectives and lax.ppermute only.
A program may use at most 128 MiB of HBM per device.

```python
import math
import jax
import jax.numpy as jnp
from jax import lax

D = 512
HEADS = 8
HEAD_DIM = 64
FF = 2048
SEQ = 256
NSEG = 8
ROW = 512
BATCH = 16


def long_slot(key):
    return jax.random.randint(key, (BATCH, 1), 0, NSEG)


def document_lengths(key, slot):
    remain = SEQ // 2
    scores = jax.random.randint(key, (BATCH, remain - 1), 0, 1 << 20) * remain + jnp.arange(remain - 1, dtype=jnp.int32)[None, :]
    _, picked = lax.top_k(scores, NSEG - 1)
    cuts = jnp.sort(picked.astype(jnp.int32) + 1, axis=-1)
    bounds = jnp.concatenate([jnp.zeros((BATCH, 1), jnp.int32), cuts, jnp.full((BATCH, 1), remain, jnp.int32)], axis=-1)
    pieces = bounds[:, 1:] - bounds[:, :-1]
    shorts = pieces[:, :NSEG - 1]
    column = jnp.zeros((BATCH, 1), jnp.int32)
    before = jnp.concatenate([shorts, column], axis=-1)
    after = jnp.concatenate([column, shorts], axis=-1)
    places = jnp.arange(NSEG, dtype=jnp.int32)[None, :]
    longest = jnp.full((BATCH, NSEG), ROW - remain, jnp.int32)
    lengths = jnp.where(places < slot, before, jnp.where(places == slot, longest, after))
    return lengths.astype(jnp.int32)


def draw_target_lens(key, part):
    slot = long_slot(key)
    key = jax.random.fold_in(key, 1)
    return document_lengths(key, slot)


def draw_source_lens(key, part):
    slot = long_slot(key)
    key = jax.random.fold_in(key, 2)
    return document_lengths(key, slot)


def level_of(rng, dims, split, low, top_value):
    loudness, own = 1.0, jax.random.fold_in(rng, 6)
    for dim, shards_of in split:
        draws = jnp.exp(jax.random.uniform(jax.random.fold_in(own, dim), (shards_of,), jnp.float32, low / len(split), top_value / len(split)))
        loudness = loudness * jnp.repeat(draws, dims[dim] // shards_of).reshape([-1 if axis == dim else 1 for axis in range(len(dims))])
    return loudness


def centred(rng, shape, scale, most, cuts=(), kind=jnp.bfloat16):
    level = level_of(rng, shape, cuts, -0.22, 0.18) if cuts else 1.0
    drawn = jax.random.normal(rng, shape, jnp.float32) * scale * level
    return jnp.minimum(jnp.maximum(drawn, -most), most).astype(kind)


def setup_inputs(seed: int = 0) -> dict:
    seeds = jax.random.split(jax.random.key(seed), 17)
    target = centred(seeds[0], (BATCH, ROW, D), 1.0, 6.0, ((0, 16), (1, 2)))
    memory = centred(seeds[1], (BATCH, ROW, D), 1.0, 6.0, ((0, 16), (1, 2)))
    target_lens = draw_target_lens(jax.random.fold_in(seeds[16], 71), 0)
    source_lens = draw_source_lens(jax.random.fold_in(seeds[16], 71), 0)
    self_in = centred(seeds[4], (D, 3 * D), D ** -0.5, 0.25)
    self_out = centred(seeds[5], (D, D), (D // 16) ** -0.5, 1.0)
    cross_q = centred(seeds[6], (D, D), D ** -0.5, 0.25)
    cross_kv = centred(seeds[7], (D, 2 * D), D ** -0.5, 0.25)
    cross_out = centred(seeds[8], (D, D), (D // 16) ** -0.5, 1.0)
    ffn_in = centred(seeds[9], (D, FF), D ** -0.5, 0.25)
    ffn_in_bias = centred(seeds[10], (FF,), 0.5, 3.0, (), jnp.float32)
    ffn_out = centred(seeds[11], (FF, D), FF ** -0.5, 0.125)
    ffn_out_bias = centred(seeds[12], (D,), 0.5, 3.0, (), jnp.float32)
    norm_gain = jnp.clip(1.0 + 0.18 * jax.random.normal(seeds[13], (3, D), jnp.float32), 0.1, 1.9)
    norm_bias = centred(seeds[14], (3, D), 0.5, 3.0, (), jnp.float32)
    cotangent = centred(seeds[15], (BATCH, ROW, D), 1.0, 6.0, ((0, 16), (1, 2)))
    return dict(target=target, memory=memory, target_lens=target_lens, source_lens=source_lens, self_in=self_in, self_out=self_out, cross_q=cross_q, cross_kv=cross_kv, cross_out=cross_out, ffn_in=ffn_in, ffn_in_bias=ffn_in_bias, ffn_out=ffn_out, ffn_out_bias=ffn_out_bias, norm_gain=norm_gain, norm_bias=norm_bias, cotangent=cotangent)


EPSILON = 1e-05
MASKED = -1e+30
HIGHEST = lax.Precision.HIGHEST

@jax.custom_vjp
def low(v):
    return lax.optimization_barrier(v.astype(jnp.bfloat16)).astype(jnp.float32)

@jax.custom_vjp
def low_back(v):
    return v

def low_keep(v):
    return (low(v), None)

def low_pass(kept, grad):
    return (grad,)

def back_keep(v):
    return (v, None)

def back_low(kept, grad):
    return (low(grad),)
low.defvjp(low_keep, low_pass)
low_back.defvjp(back_keep, back_low)

def segment_ids(doc_lens, length):
    ends = jnp.cumsum(doc_lens, axis=-1)
    places = jnp.arange(length, dtype=jnp.int32)
    return lax.optimization_barrier(jnp.sum((places[:, None] >= ends[..., None, :]).astype(jnp.int32), axis=-1))

def layer_norm(values, gain, shift):
    centre = values - lax.optimization_barrier(jnp.mean(values, axis=-1, keepdims=True))
    spread = lax.optimization_barrier(jnp.mean(centre * centre, axis=-1, keepdims=True))
    return centre * lax.rsqrt(spread + EPSILON) * gain + shift

def matmul(left, right):
    return jnp.dot(left, right, precision=HIGHEST)

def both_low(values):
    return low(low_back(values))

def attend(queries, keys, values, query_seg, key_seg, causal):
    length, feat_width = queries.shape
    block_len = math.gcd(length, 512)
    key_heads = keys.reshape(length, HEADS, HEAD_DIM)
    value_heads = values.reshape(length, HEADS, HEAD_DIM)
    key_pos = jnp.arange(length, dtype=jnp.int32)

    def one_block(operands):
        query_blk, seg_blk, pos_blk = operands
        query_heads = query_blk.reshape(block_len, HEADS, HEAD_DIM)
        raw_scores = low_back(jnp.einsum('qhd,khd->hqk', query_heads, key_heads, precision=HIGHEST))
        visible = seg_blk[:, None] == key_seg[None, :]
        if causal:
            visible = visible & (key_pos[None, :] <= pos_blk[:, None])
        scores = jnp.where(visible[None], raw_scores * HEAD_DIM ** (-0.5), MASKED)
        attention = jax.nn.softmax(scores, axis=-1)
        mixture = jnp.einsum('hqk,khd->qhd', low(attention), value_heads, precision=HIGHEST)
        return mixture.reshape(block_len, feat_width)
    block_count = length // block_len
    blocks = lax.map(jax.checkpoint(one_block), (queries.reshape(block_count, block_len, feat_width), query_seg.reshape(block_count, block_len), key_pos.reshape(block_count, block_len)))
    return blocks.reshape(length, feat_width)

def decoder_layer(inputs, memory_row, params, target_seg, source_seg):
    self_in, self_out, cross_q, cross_kv, cross_out, ffn_in, ffn_in_bias, ffn_out, ffn_out_bias, norm_gain, norm_bias = params
    feat_width = inputs.shape[1]
    triple = both_low(matmul(inputs, self_in))
    self_mix = attend(triple[:, :feat_width], triple[:, feat_width:2 * feat_width], triple[:, 2 * feat_width:], target_seg, target_seg, True)
    first = layer_norm(inputs + low_back(matmul(both_low(self_mix), self_out)), norm_gain[0], norm_bias[0])
    cross_query = both_low(matmul(low(first), cross_q))
    pairs = both_low(matmul(memory_row, cross_kv))
    cross_mix = attend(cross_query, pairs[:, :feat_width], pairs[:, feat_width:], target_seg, source_seg, False)
    second = layer_norm(first + low_back(matmul(both_low(cross_mix), cross_out)), norm_gain[1], norm_bias[1])
    inner = low_back(matmul(low(second), ffn_in)) + ffn_in_bias
    outer = low_back(matmul(low(jax.nn.gelu(inner, approximate=True)), ffn_out)) + ffn_out_bias
    return layer_norm(second + outer, norm_gain[2], norm_bias[2])

def reference(target, memory, target_lens, source_lens, self_in, self_out, cross_q, cross_kv, cross_out, ffn_in, ffn_in_bias, ffn_out, ffn_out_bias, norm_gain, norm_bias, cotangent):
    params = tuple((weight.astype(jnp.float32) for weight in (self_in, self_out, cross_q, cross_kv, cross_out, ffn_in, ffn_in_bias, ffn_out, ffn_out_bias, norm_gain, norm_bias)))
    length = target.shape[1]

    def row_step(totals, row_data):
        inputs, memory_row, tgt_lens, src_lens, row_grad = row_data
        target_seg = segment_ids(tgt_lens, length)
        source_seg = segment_ids(src_lens, length)

        def forward(input_vals, memory_vals, param_vals):
            return decoder_layer(input_vals, memory_vals, param_vals, target_seg, source_seg)
        result, pull_back = jax.vjp(forward, inputs.astype(jnp.float32), memory_row.astype(jnp.float32), params)
        grad_input, grad_memory, grad_params = pull_back(row_grad.astype(jnp.float32))
        totals = jax.tree.map(jnp.add, totals, grad_params)
        return (totals, (result.astype(jnp.bfloat16), grad_input, grad_memory))
    zero_grads = tuple((jnp.zeros(weight.shape, jnp.float32) for weight in params))
    totals, (output, target_grad, memory_grad) = lax.scan(row_step, zero_grads, (target, memory, target_lens, source_lens, cotangent))
    return (output, target_grad, memory_grad, totals[0], totals[1], totals[2], totals[3], totals[4], totals[5], totals[6], totals[7], totals[8], totals[9], totals[10])
```

```python
import math

import jax
import jax.numpy as jnp
from jax import lax
from jax.experimental import pallas as pl
from jax.experimental.pallas import tpu as pltpu
from jax.sharding import PartitionSpec as P

HEADS = 8
HEAD_DIM = 64


EPSILON = 1e-05
MASKED = -1e30


def segment_ids(doc_lens, length):
    ends = jnp.cumsum(doc_lens, axis=-1)
    places = jnp.arange(length, dtype=jnp.int32)
    return jnp.sum((places[:, None] >= ends[..., None, :]).astype(jnp.int32), axis=-1)


def layer_norm(values, gain, shift):
    centre = values - jnp.mean(values, axis=-1, keepdims=True)
    spread = jnp.mean(centre * centre, axis=-1, keepdims=True)
    return centre * lax.rsqrt(spread + EPSILON) * gain + shift


def gelu_tanh(values):
    return jax.nn.gelu(values, approximate=True)


def project(activity, weight):
    return jnp.einsum("rsd,de->rse", activity, weight, preferred_element_type=jnp.float32)


def project_back(gradient, weight):
    return jnp.einsum("rse,de->rsd", gradient, weight, preferred_element_type=jnp.float32)


def weight_grad(activity, gradient):
    return jnp.einsum("rsd,rse->de", activity, gradient, preferred_element_type=jnp.float32)


def split_heads(values):
    return values.reshape(values.shape[0], values.shape[1], HEADS, HEAD_DIM)


def join_heads(values):
    return values.reshape(values.shape[0], values.shape[1], HEADS * HEAD_DIM)


def block_scores(query_heads, key_heads, query_seg, key_seg, query_pos, key_pos, causal):
    raw_scores = jnp.einsum(
        "rqhd,rkhd->rhqk", query_heads, key_heads, preferred_element_type=jnp.float32
    )
    visible = query_seg[:, :, None] == key_seg[:, None, :]
    if causal:
        visible = visible & (key_pos[None, None, :] <= query_pos[None, :, None])
    return jnp.where(visible[:, None], raw_scores * HEAD_DIM ** (-0.5), MASKED)


def block_backward(query_heads, grad_heads, key_heads, value_heads, scores, log_norm, row_dot):
    attention = jnp.exp(scores - log_norm[..., None])
    grad_attn = jnp.einsum(
        "rqhd,rkhd->rhqk", grad_heads, value_heads, preferred_element_type=jnp.float32
    )
    grad_scores = (attention * (grad_attn - row_dot[..., None]) * HEAD_DIM ** (-0.5)).astype(
        jnp.bfloat16
    )
    grad_query = jnp.einsum(
        "rhqk,rkhd->rqhd", grad_scores, key_heads, preferred_element_type=jnp.float32
    )
    grad_key = jnp.einsum(
        "rhqk,rqhd->rkhd", grad_scores, query_heads, preferred_element_type=jnp.float32
    )
    grad_value = jnp.einsum(
        "rhqk,rqhd->rkhd",
        attention.astype(jnp.bfloat16),
        grad_heads,
        preferred_element_type=jnp.float32,
    )
    return (grad_query, jnp.concatenate([join_heads(grad_key), join_heads(grad_value)], axis=-1))


def make_key_fold(query_heads, query_seg, key_seg_full, query_pos, causal, running, portion):
    run_max, run_sum, stored = running
    span_len = portion.shape[1]
    key_pos = jnp.arange(span_len, dtype=jnp.int32)
    scores = block_scores(
        query_heads,
        split_heads(portion[:, :, : HEADS * HEAD_DIM]),
        query_seg,
        key_seg_full,
        query_pos,
        key_pos,
        causal,
    )
    new_max = jnp.maximum(run_max, jnp.max(scores, axis=-1))
    run_sum = jnp.sum(jnp.exp(scores - new_max[..., None]), axis=-1)
    stored = portion
    return (new_max, run_sum, stored)


def attend_stored(query_heads, stored, query_seg, key_seg_full, query_pos, causal, log_norm):
    total_len = stored.shape[1]
    pair_half = stored.shape[2] // 2
    block_len = math.gcd(total_len, max(query_heads.shape[1], 512))

    def advance(low_sum, block_idx):
        begin_at = block_idx * block_len
        portion = lax.dynamic_slice_in_dim(stored, begin_at, block_len, 1)
        key_seg = lax.dynamic_slice_in_dim(key_seg_full, begin_at, block_len, 1)
        key_pos = begin_at + jnp.arange(block_len, dtype=jnp.int32)
        value_heads = split_heads(portion[:, :, pair_half:])
        scores = block_scores(
            query_heads,
            split_heads(portion[:, :, :pair_half]),
            query_seg,
            key_seg,
            query_pos,
            key_pos,
            causal,
        )
        attention = jnp.exp(scores - log_norm[..., None])
        low_sum = low_sum + jnp.einsum(
            "rhqk,rkhd->rqhd",
            attention.astype(jnp.bfloat16),
            value_heads,
            preferred_element_type=jnp.float32,
        )
        return (low_sum, None)

    zeros_q = jnp.zeros(query_heads.shape, jnp.float32)
    low_sum, _ = lax.scan(advance, zeros_q, jnp.arange(total_len // block_len, dtype=jnp.int32))
    return low_sum


def attend_back_stored(
    query_heads, grad_heads, stored, query_seg, key_seg_full, query_pos, causal, log_norm, row_dot
):
    total_len = stored.shape[1]
    pair_half = stored.shape[2] // 2
    block_len = math.gcd(total_len, max(query_heads.shape[1], 512))

    def advance(block_idx, running):
        grad_query, grad_term = running
        begin_at = block_idx * block_len
        portion = lax.dynamic_slice_in_dim(stored, begin_at, block_len, 1)
        key_seg = lax.dynamic_slice_in_dim(key_seg_full, begin_at, block_len, 1)
        key_pos = begin_at + jnp.arange(block_len, dtype=jnp.int32)
        key_heads = split_heads(portion[:, :, :pair_half])
        value_heads = split_heads(portion[:, :, pair_half:])
        scores = block_scores(
            query_heads, key_heads, query_seg, key_seg, query_pos, key_pos, causal
        )
        block_dq, block_dkv = block_backward(
            query_heads, grad_heads, key_heads, value_heads, scores, log_norm, row_dot
        )
        grad_term = lax.dynamic_update_slice_in_dim(grad_term, block_dkv, begin_at, 1)
        return (grad_query + block_dq, grad_term)

    start_vals = (jnp.zeros(query_heads.shape, jnp.float32), jnp.zeros(stored.shape, jnp.float32))
    grad_query, grad_term = lax.fori_loop(0, total_len // block_len, advance, start_vals)
    return (join_heads(grad_query), grad_term)


def local(
    target,
    memory,
    target_lens,
    source_lens,
    self_in,
    self_out,
    cross_q,
    cross_kv,
    cross_out,
    ffn_in,
    ffn_in_bias,
    ffn_out,
    ffn_out_bias,
    norm_gain,
    norm_bias,
    cotangent,
):
    row_count, shard_len, feat_width = target.shape
    total_len = shard_len * lax.axis_size("narrow")
    own_start = lax.axis_index("narrow") * shard_len
    own_pos = own_start + jnp.arange(shard_len, dtype=jnp.int32)
    target_seg = segment_ids(target_lens, total_len)
    source_seg = segment_ids(source_lens, total_len)
    target_own = lax.dynamic_slice_in_dim(target_seg, own_start, shard_len, 1)
    start_state = (
        jnp.full((row_count, HEADS, shard_len), MASKED, jnp.float32),
        jnp.zeros((row_count, HEADS, shard_len), jnp.float32),
        jnp.zeros((row_count, total_len, 2 * feat_width), jnp.bfloat16),
    )
    triple = project(target, self_in).astype(jnp.bfloat16)
    self_query = split_heads(triple[:, :, :feat_width])
    self_pairs = triple[:, :, feat_width:]
    self_max, self_sum, self_store = make_key_fold(
        self_query,
        target_own,
        target_seg,
        own_pos,
        True,
        start_state,
        lax.all_gather(self_pairs, "narrow", axis=1, tiled=True),
    )
    self_norm = self_max + jnp.log(self_sum)
    self_low = attend_stored(
        self_query, self_store, target_own, target_seg, own_pos, True, self_norm
    )
    self_mix = join_heads(self_low).astype(jnp.bfloat16)
    first, first_pull = jax.vjp(
        layer_norm,
        target.astype(jnp.float32) + project(self_mix, self_out),
        norm_gain[0],
        norm_bias[0],
    )
    first_low = first.astype(jnp.bfloat16)
    cross_query = split_heads(project(first_low, cross_q).astype(jnp.bfloat16))
    cross_pairs = project(memory, cross_kv).astype(jnp.bfloat16)
    cross_max, cross_sum, cross_store = make_key_fold(
        cross_query,
        target_own,
        source_seg,
        own_pos,
        False,
        start_state,
        lax.all_gather(cross_pairs, "narrow", axis=1, tiled=True),
    )
    cross_norm = cross_max + jnp.log(cross_sum)
    cross_low = attend_stored(
        cross_query, cross_store, target_own, source_seg, own_pos, False, cross_norm
    )
    cross_mix = join_heads(cross_low).astype(jnp.bfloat16)
    second, second_pull = jax.vjp(
        layer_norm, first + project(cross_mix, cross_out), norm_gain[1], norm_bias[1]
    )
    second_low = second.astype(jnp.bfloat16)
    inner = project(second_low, ffn_in) + ffn_in_bias
    active, gelu_pull = jax.vjp(gelu_tanh, inner)
    active_low = active.astype(jnp.bfloat16)
    result, third_pull = jax.vjp(
        layer_norm, second + project(active_low, ffn_out) + ffn_out_bias, norm_gain[2], norm_bias[2]
    )
    grad_third, gain_third, shift_third = third_pull(cotangent.astype(jnp.float32))
    grad_outer = grad_third.astype(jnp.bfloat16)
    ffn_out_g = weight_grad(active_low, grad_outer)
    ffn_out_bias_g = jnp.sum(grad_third, axis=(0, 1))
    (grad_active,) = gelu_pull(project_back(grad_outer, ffn_out))
    grad_inner = grad_active.astype(jnp.bfloat16)
    ffn_in_g = weight_grad(second_low, grad_inner)
    ffn_in_bias_g = jnp.sum(grad_active, axis=(0, 1))
    grad_second, gain_second, shift_second = second_pull(
        grad_third + project_back(grad_inner, ffn_in)
    )
    grad_cross = grad_second.astype(jnp.bfloat16)
    cross_out_g = weight_grad(cross_mix, grad_cross)
    cross_dout = split_heads(project_back(grad_cross, cross_out).astype(jnp.bfloat16))
    cross_dot = jnp.swapaxes(jnp.sum(cross_dout.astype(jnp.float32) * cross_low, axis=-1), 1, 2)
    cross_dq, cross_term = attend_back_stored(
        cross_query,
        cross_dout,
        cross_store,
        target_own,
        source_seg,
        own_pos,
        False,
        cross_norm,
        cross_dot,
    )
    cross_dpairs = lax.psum_scatter(
        cross_term.astype(jnp.bfloat16), "narrow", scatter_dimension=1, tiled=True
    )
    cross_dq_low = cross_dq.astype(jnp.bfloat16)
    cross_q_g = weight_grad(first_low, cross_dq_low)
    cross_kv_g = weight_grad(memory, cross_dpairs)
    memory_grad = project_back(cross_dpairs, cross_kv)
    grad_first, gain_first, shift_first = first_pull(
        grad_second + project_back(cross_dq_low, cross_q)
    )
    grad_self = grad_first.astype(jnp.bfloat16)
    self_out_g = weight_grad(self_mix, grad_self)
    self_dout = split_heads(project_back(grad_self, self_out).astype(jnp.bfloat16))
    self_dot = jnp.swapaxes(jnp.sum(self_dout.astype(jnp.float32) * self_low, axis=-1), 1, 2)
    self_dq, self_term = attend_back_stored(
        self_query,
        self_dout,
        self_store,
        target_own,
        target_seg,
        own_pos,
        True,
        self_norm,
        self_dot,
    )
    self_dpairs = lax.psum_scatter(
        self_term.astype(jnp.bfloat16), "narrow", scatter_dimension=1, tiled=True
    ).astype(jnp.float32)
    grad_triple = jnp.concatenate([self_dq, self_dpairs], axis=-1).astype(jnp.bfloat16)
    self_in_g = weight_grad(target, grad_triple)
    target_grad = grad_first + project_back(grad_triple, self_in)
    gain_g = jnp.stack([gain_first, gain_second, gain_third])
    shift_g = jnp.stack([shift_first, shift_second, shift_third])
    sh_a, sh_b, sh_c, sh_d, sh_e, sh_f, sh_g, sh_h, sh_i, sh_j, sh_k = (
        lax.psum_scatter(
            self_in_g.astype(jnp.bfloat16), "narrow", scatter_dimension=0, tiled=True
        ).astype(jnp.float32),
        lax.psum_scatter(
            self_out_g.astype(jnp.bfloat16), "narrow", scatter_dimension=0, tiled=True
        ).astype(jnp.float32),
        lax.psum_scatter(
            cross_q_g.astype(jnp.bfloat16), "narrow", scatter_dimension=0, tiled=True
        ).astype(jnp.float32),
        lax.psum_scatter(
            cross_kv_g.astype(jnp.bfloat16), "narrow", scatter_dimension=0, tiled=True
        ).astype(jnp.float32),
        lax.psum_scatter(
            cross_out_g.astype(jnp.bfloat16), "narrow", scatter_dimension=0, tiled=True
        ).astype(jnp.float32),
        lax.psum_scatter(
            ffn_in_g.astype(jnp.bfloat16), "narrow", scatter_dimension=0, tiled=True
        ).astype(jnp.float32),
        lax.psum_scatter(
            ffn_in_bias_g.astype(jnp.bfloat16), "narrow", scatter_dimension=0, tiled=True
        ).astype(jnp.float32),
        lax.psum_scatter(
            ffn_out_g.astype(jnp.bfloat16), "narrow", scatter_dimension=0, tiled=True
        ).astype(jnp.float32),
        lax.psum_scatter(
            ffn_out_bias_g.astype(jnp.bfloat16), "narrow", scatter_dimension=0, tiled=True
        ).astype(jnp.float32),
        lax.psum_scatter(
            gain_g.astype(jnp.bfloat16), "narrow", scatter_dimension=1, tiled=True
        ).astype(jnp.float32),
        lax.psum_scatter(
            shift_g.astype(jnp.bfloat16), "narrow", scatter_dimension=1, tiled=True
        ).astype(jnp.float32),
    )
    summed = (
        lax.psum(sh_a.astype(jnp.bfloat16), "wide").astype(jnp.float32),
        lax.psum(sh_b.astype(jnp.bfloat16), "wide").astype(jnp.float32),
        lax.psum(sh_c.astype(jnp.bfloat16), "wide").astype(jnp.float32),
        lax.psum(sh_d.astype(jnp.bfloat16), "wide").astype(jnp.float32),
        lax.psum(sh_e.astype(jnp.bfloat16), "wide").astype(jnp.float32),
        lax.psum(sh_f.astype(jnp.bfloat16), "wide").astype(jnp.float32),
        lax.psum(sh_g.astype(jnp.bfloat16), "wide").astype(jnp.float32),
        lax.psum(sh_h.astype(jnp.bfloat16), "wide").astype(jnp.float32),
        lax.psum(sh_i.astype(jnp.bfloat16), "wide").astype(jnp.float32),
        lax.psum(sh_j.astype(jnp.bfloat16), "wide").astype(jnp.float32),
        lax.psum(sh_k.astype(jnp.bfloat16), "wide").astype(jnp.float32),
    )
    return (
        result.astype(jnp.bfloat16),
        target_grad,
        memory_grad,
        summed[0],
        summed[1],
        summed[2],
        summed[3],
        summed[4],
        summed[5],
        summed[6],
        summed[7],
        summed[8],
        summed[9],
        summed[10],
    )


def dot_nn(left, right):
    return jnp.dot(left, right, preferred_element_type=jnp.float32)


def dot_nt(left, right):
    return lax.dot_general(left, right, (((1,), (1,)), ((), ())), preferred_element_type=jnp.float32)


def dot_tn(left, right):
    return lax.dot_general(left, right, (((0,), (0,)), ((), ())), preferred_element_type=jnp.float32)


def low(values):
    return values.astype(jnp.bfloat16)


def normalize(values):
    centre = values - jnp.mean(values, axis=-1, keepdims=True)
    scale = lax.rsqrt(jnp.mean(centre * centre, axis=-1, keepdims=True) + EPSILON)
    return centre * scale, scale


def normalize_back(grad, gain, unit, scale):
    inner = grad * gain
    return scale * (
        inner
        - jnp.mean(inner, axis=-1, keepdims=True)
        - unit * jnp.mean(inner * unit, axis=-1, keepdims=True)
    )


def seg_along(lens_ref, shape, dim):
    places = lax.broadcasted_iota(jnp.int32, shape, dim)
    seg = jnp.zeros(shape, jnp.int32)
    end = jnp.int32(0)
    for doc in range(lens_ref.shape[1]):
        end = end + lens_ref[0, doc]
        seg = seg + (places >= end).astype(jnp.int32)
    return seg


def visible_pairs(query_lens, key_lens, length, causal):
    seen = seg_along(query_lens, (length, 1), 0) == seg_along(key_lens, (1, length), 1)
    if causal:
        rows = lax.broadcasted_iota(jnp.int32, (length, length), 0)
        cols = lax.broadcasted_iota(jnp.int32, (length, length), 1)
        seen = seen & (cols <= rows)
    return seen


def join_halves(place_ref, own_ref, other_ref, full_ref):
    half = own_ref.shape[0]
    mine = place_ref[0]
    full_ref[pl.ds(pl.multiple_of(mine * half, half), half), :] = own_ref[...]
    full_ref[pl.ds(pl.multiple_of((1 - mine) * half, half), half), :] = other_ref[...]


def own_columns(ref, start, width):
    return ref[:, pl.ds(pl.multiple_of(start, 128), width)]


def grad_rows(place_ref, activity_ref, grads, keep_ref, send_ref, col):
    rows = keep_ref.shape[0]
    first = place_ref[0] * 2 * rows
    for ref, part in ((keep_ref, place_ref[1]), (send_ref, 1 - place_ref[1])):
        piece = own_columns(activity_ref, first + part * rows, rows)
        at = col
        for grad in grads:
            ref[:, at : at + grad.shape[1]] = dot_tn(piece, grad).astype(ref.dtype)
            at += grad.shape[1]


def query_blocks(length, causal):
    if causal:
        return ((0, length // 2, length // 2), (length // 2, length, length))
    return ((0, length // 2, length), (length // 2, length, length))


PAIR = 2 * HEAD_DIM


def head_lanes():
    lane = lax.broadcasted_iota(jnp.int32, (1, PAIR), 1)
    return (lane < HEAD_DIM, lane >= HEAD_DIM)


def attend_all(query_ref, key_ref, value_ref, bias_ref, attn_ref, mix_ref, causal):
    length = query_ref.shape[0]

    def one_pair(pair, carry):
        lanes = pl.ds(pl.multiple_of(pair * PAIR, PAIR), PAIR)
        keys, values = key_ref[:, lanes], value_ref[:, lanes]
        zero = jnp.zeros_like(keys)
        for begin, end, reach in query_blocks(length, causal):
            queries = query_ref[begin:end, lanes]
            total = jnp.zeros((end - begin, PAIR), jnp.float32)
            for sub, inside in enumerate(head_lanes()):
                scores = dot_nt(queries, jnp.where(inside, keys, zero)[:reach])
                scores = scores + bias_ref[begin:end, :reach]
                weights = jnp.exp(scores - jnp.max(scores, axis=-1, keepdims=True))
                weights = low(weights * (1.0 / jnp.sum(weights, axis=-1, keepdims=True)))
                attn_ref[pair * 2 + sub, begin:end, :reach] = weights
                total = total + dot_nn(weights, jnp.where(inside, values, zero)[:reach])
            mix_ref[begin:end, lanes] = low(total)
        return carry

    lax.fori_loop(0, HEADS // 2, one_pair, 0)


def attend_all_back(
    query_ref, query_t_ref, key_ref, value_ref, attn_ref, mix_ref, grad_ref, grad_t_ref, dquery_ref, dpairs_t_ref, causal
):
    length, width = query_ref.shape

    def one_pair(pair, carry):
        lanes = pl.ds(pl.multiple_of(pair * PAIR, PAIR), PAIR)
        keys, values = key_ref[:, lanes], value_ref[:, lanes]
        zero = jnp.zeros_like(keys)
        blocks = query_blocks(length, causal)
        dquery = [jnp.zeros((end - begin, PAIR), jnp.float32) for begin, end, _ in blocks]
        for sub, inside in enumerate(head_lanes()):
            head_keys = jnp.where(inside, keys, zero)
            head_values = jnp.where(inside, values, zero)
            rows = pl.ds(pl.multiple_of(pair * PAIR + sub * HEAD_DIM, HEAD_DIM), HEAD_DIM)
            parts = []
            for idx, (begin, end, reach) in enumerate(blocks):
                grads = grad_ref[begin:end, lanes]
                dots = grads.astype(jnp.float32) * mix_ref[begin:end, lanes].astype(jnp.float32)
                row_dot = jnp.sum(jnp.where(inside, dots, 0.0), axis=-1, keepdims=True)
                weights = attn_ref[pair * 2 + sub, begin:end, :reach]
                dattn = dot_nt(grads, head_values[:reach])
                dscores = low(weights.astype(jnp.float32) * (dattn - row_dot))
                dquery[idx] = dquery[idx] + dot_nn(dscores, head_keys[:reach])
                dkey_t = dot_nn(query_t_ref[rows, begin:end], dscores)
                dvalue_t = dot_nn(grad_t_ref[rows, begin:end], weights)
                parts.append((reach, dkey_t, dvalue_t))
            (reach, dkey_t, dvalue_t), (_, dkey_more, dvalue_more) = parts
            rows_v = pl.ds(pl.multiple_of(width + pair * PAIR + sub * HEAD_DIM, HEAD_DIM), HEAD_DIM)
            for where, less, more in ((rows, dkey_t, dkey_more), (rows_v, dvalue_t, dvalue_more)):
                dpairs_t_ref[where, :reach] = low(less + more[:, :reach])
                if reach < length:
                    dpairs_t_ref[where, reach:] = low(more[:, reach:])
        for (begin, end, _), dq in zip(blocks, dquery):
            dquery_ref[begin:end, lanes] = low(dq * HEAD_DIM ** (-0.5))
        return carry

    lax.fori_loop(0, HEADS // 2, one_pair, 0)


def self_forward_kernel(
    place_ref, lens_ref, own_ref, other_ref, self_in_ref, self_out_ref,
    triple_ref, attn_ref, mix_ref, unit_ref, scale_ref,
    full_ref, bias_ref,
):
    length, width = full_ref.shape
    join_halves(place_ref, own_ref, other_ref, full_ref)
    bias_ref[...] = jnp.where(visible_pairs(lens_ref, lens_ref, length, True), 0.0, MASKED)
    triple_ref[:, :width] = low(
        low(dot_nn(full_ref[...], self_in_ref[:, :width])) * jnp.bfloat16(HEAD_DIM ** (-0.5))
    )
    triple_ref[:, width:] = low(dot_nn(full_ref[...], self_in_ref[:, width:]))
    attend_all(
        triple_ref.at[:, :width],
        triple_ref.at[:, width : 2 * width],
        triple_ref.at[:, 2 * width :],
        bias_ref,
        attn_ref,
        mix_ref,
        True,
    )
    summed = full_ref[...].astype(jnp.float32) + dot_nn(mix_ref[...], self_out_ref[...])
    unit_ref[...], scale_ref[...] = normalize(summed)


def cross_forward_kernel(
    place_ref, target_lens_ref, source_lens_ref, own_ref, other_ref, unit_first_ref,
    cross_q_ref, cross_kv_ref, cross_out_ref, gain_ref, shift_ref,
    query_ref, pairs_ref, attn_ref, mix_ref, unit_ref, scale_ref,
    full_ref, bias_ref,
):
    length, width = full_ref.shape
    join_halves(place_ref, own_ref, other_ref, full_ref)
    bias_ref[...] = jnp.where(visible_pairs(target_lens_ref, source_lens_ref, length, False), 0.0, MASKED)
    first = unit_first_ref[...] * gain_ref[0:1, :] + shift_ref[0:1, :]
    query_ref[...] = low(low(dot_nn(low(first), cross_q_ref[...])) * jnp.bfloat16(HEAD_DIM ** (-0.5)))
    pairs_ref[...] = low(dot_nn(full_ref[...], cross_kv_ref[...]))
    attend_all(
        query_ref, pairs_ref.at[:, :width], pairs_ref.at[:, width:], bias_ref, attn_ref, mix_ref, False
    )
    first = unit_first_ref[...] * gain_ref[0:1, :] + shift_ref[0:1, :]
    unit_ref[...], scale_ref[...] = normalize(first + dot_nn(mix_ref[...], cross_out_ref[...]))


GELU_SCALE = math.sqrt(2.0 / math.pi)
GELU_CUBE = 0.044715


def gelu_both(values):
    square = values * values
    bent = jnp.tanh(GELU_SCALE * (values + GELU_CUBE * (square * values)))
    half_up = 0.5 * (1.0 + bent)
    slope = half_up + 0.5 * values * (1.0 - bent * bent) * (
        GELU_SCALE * (1.0 + 3.0 * GELU_CUBE * square)
    )
    return values * half_up, slope


def feed_kernel(
    place_ref, own_ref, other_ref, unit_second_ref, scale_second_ref,
    ffn_in_ref, ffn_in_bias_ref, ffn_out_ref, ffn_out_bias_ref, gain_ref, shift_ref,
    output_ref, out_keep_ref, out_send_ref, in_keep_ref, in_send_ref,
    in_bias_grad_ref, norm_grad_ref, grad_second_ref,
    full_ref, second_ref, active_ref, slope_ref, outer_ref, inner_ref,
):
    length, width = full_ref.shape
    half = length // 2
    hidden = ffn_in_ref.shape[1]
    block = min(hidden, 512)
    join_halves(place_ref, own_ref, other_ref, full_ref)
    second = unit_second_ref[...] * gain_ref[1:2, :] + shift_ref[1:2, :]
    second_ref[...] = low(second)
    total = second + ffn_out_bias_ref[...]
    for begin in range(0, hidden, block):
        cols = slice(begin, begin + block)
        inner = dot_nn(second_ref[...], ffn_in_ref[:, cols]) + ffn_in_bias_ref[:, cols]
        active, slope_ref[:, cols] = gelu_both(inner)
        active_ref[:, cols] = low(active)
        total = total + dot_nn(active_ref[:, cols], ffn_out_ref[cols, :])
    unit, scale = normalize(total)
    shown = unit * gain_ref[2:3, :] + shift_ref[2:3, :]
    cotangent = full_ref[...].astype(jnp.float32)
    norm_grad_ref[0:1, :] = jnp.sum(cotangent * unit, axis=0, keepdims=True)
    norm_grad_ref[1:2, :] = jnp.sum(cotangent, axis=0, keepdims=True)
    grad_third = normalize_back(cotangent, gain_ref[2:3, :], unit, scale)
    norm_grad_ref[4:5, :] = jnp.sum(grad_third, axis=0, keepdims=True)
    outer_ref[...] = low(grad_third)
    grad_second_ref[...] = shown
    output_ref[...] = low(
        grad_second_ref[pl.ds(pl.multiple_of(place_ref[0] * half, half), half), :]
    )
    grad_second_ref[...] = grad_third
    grad_rows(place_ref, active_ref, (outer_ref[...],), out_keep_ref, out_send_ref, 0)
    into_second = jnp.zeros((length, width), jnp.float32)
    for begin in range(0, hidden, block):
        cols = slice(begin, begin + block)
        grad_inner = dot_nt(outer_ref[...], ffn_out_ref[cols, :]) * slope_ref[:, cols]
        in_bias_grad_ref[:, cols] = jnp.sum(grad_inner, axis=0, keepdims=True)
        inner_ref[:, cols] = low(grad_inner)
        into_second = into_second + dot_nt(inner_ref[:, cols], ffn_in_ref[:, cols])
    grad_rows(place_ref, second_ref, (inner_ref[...],), in_keep_ref, in_send_ref, 0)
    grad = grad_second_ref[...] + into_second
    unit_second = unit_second_ref[...]
    norm_grad_ref[2:3, :] = jnp.sum(grad * unit_second, axis=0, keepdims=True)
    norm_grad_ref[3:4, :] = jnp.sum(grad, axis=0, keepdims=True)
    norm_grad_ref[5:8, :] = jnp.zeros((3, width), jnp.float32)
    grad_second_ref[...] = normalize_back(grad, gain_ref[1:2, :], unit_second, scale_second_ref[...])


def cross_back_kernel(
    place_ref, target_lens_ref, source_lens_ref, own_ref, other_ref, grad_second_ref, unit_first_ref, scale_first_ref,
    query_ref, pairs_ref, attn_ref, mix_ref, cross_q_ref, cross_kv_ref, cross_out_ref, gain_ref, shift_ref,
    keep_ref, send_ref, memory_grad_ref, norm_grad_ref, grad_first_ref,
    full_ref, first_ref, grad_ref, dmix_ref, dmix_t_ref, query_t_ref, dquery_ref, dpairs_t_ref,
):
    length, width = full_ref.shape
    half = length // 2
    join_halves(place_ref, own_ref, other_ref, full_ref)
    first_ref[...] = low(unit_first_ref[...] * gain_ref[0:1, :] + shift_ref[0:1, :])
    grad_ref[...] = low(grad_second_ref[...])
    seen = jnp.where(visible_pairs(target_lens_ref, source_lens_ref, length, False), 1.0, 0.0)
    dmix_ref[...] = low(
        dot_nt(grad_ref[...], cross_out_ref[...]) * jnp.max(seen, axis=-1, keepdims=True)
    )
    dmix_t_ref[...] = low(dot_nt(cross_out_ref[...], grad_ref[...]))
    query_t_ref[...] = query_ref[...].T
    attend_all_back(
        query_ref, query_t_ref, pairs_ref.at[:, :width], pairs_ref.at[:, width:], attn_ref, mix_ref,
        dmix_ref, dmix_t_ref, dquery_ref, dpairs_t_ref, False,
    )
    dpairs = dpairs_t_ref[...].T
    grad_rows(place_ref, first_ref, (dquery_ref[...],), keep_ref, send_ref, 0)
    grad_rows(place_ref, full_ref, (dpairs,), keep_ref, send_ref, width)
    grad_rows(place_ref, mix_ref, (grad_ref[...],), keep_ref, send_ref, 3 * width)
    own_dpairs = own_columns(dpairs_t_ref, place_ref[0] * half, half).T
    memory_grad_ref[...] = dot_nt(own_dpairs, cross_kv_ref[...])
    grad = grad_second_ref[...] + dot_nt(dquery_ref[...], cross_q_ref[...])
    unit_first = unit_first_ref[...]
    norm_grad_ref[0:1, :] = jnp.sum(grad * unit_first, axis=0, keepdims=True)
    norm_grad_ref[1:2, :] = jnp.sum(grad, axis=0, keepdims=True)
    norm_grad_ref[2:8, :] = jnp.zeros((6, width), jnp.float32)
    grad_first_ref[...] = normalize_back(grad, gain_ref[0:1, :], unit_first, scale_first_ref[...])


def self_back_kernel(
    place_ref, own_ref, other_ref, grad_first_ref, triple_ref, attn_ref, mix_ref, self_in_ref, self_out_ref,
    keep_ref, send_ref, target_grad_ref,
    full_ref, grad_ref, dmix_ref, dmix_t_ref, query_t_ref, dquery_ref, dpairs_t_ref,
):
    length, width = full_ref.shape
    half = length // 2
    join_halves(place_ref, own_ref, other_ref, full_ref)
    grad_ref[...] = low(grad_first_ref[...])
    dmix_ref[...] = low(dot_nt(grad_ref[...], self_out_ref[...]))
    dmix_t_ref[...] = low(dot_nt(self_out_ref[...], grad_ref[...]))
    query_t_ref[...] = triple_ref[:, :width].T
    attend_all_back(
        triple_ref.at[:, :width], query_t_ref, triple_ref.at[:, width : 2 * width], triple_ref.at[:, 2 * width :],
        attn_ref, mix_ref, dmix_ref, dmix_t_ref, dquery_ref, dpairs_t_ref, True,
    )
    dpairs = dpairs_t_ref[...].T
    grad_rows(place_ref, full_ref, (dquery_ref[...], dpairs), keep_ref, send_ref, 0)
    grad_rows(place_ref, mix_ref, (grad_ref[...],), keep_ref, send_ref, 3 * width)
    own_rows = pl.ds(pl.multiple_of(place_ref[0] * half, half), half)
    own_dpairs = own_columns(dpairs_t_ref, place_ref[0] * half, half).T
    target_grad_ref[...] = (
        grad_first_ref[own_rows, :]
        + dot_nt(dquery_ref[own_rows, :], self_in_ref[:, :width])
        + dot_nt(own_dpairs, self_in_ref[:, width:])
    )


VMEM_LIMIT = 56 * 1024 * 1024


def run_kernel(kernel, scalars, arrays, outs, scratch, flops):
    in_specs = [pl.BlockSpec(memory_space=pltpu.SMEM)] * len(scalars)
    in_specs += [pl.BlockSpec(memory_space=pltpu.VMEM)] * len(arrays)
    shapes = [jax.ShapeDtypeStruct(shape, dtype) for shape, dtype in outs]
    moved = sum(math.prod(s.shape) * s.dtype.itemsize for s in shapes)
    moved += sum(math.prod(a.shape) * a.dtype.itemsize for a in arrays)
    return pl.pallas_call(
        kernel,
        out_shape=shapes,
        in_specs=in_specs,
        out_specs=[pl.BlockSpec(memory_space=pltpu.VMEM)] * len(outs),
        scratch_shapes=[pltpu.VMEM(shape, dtype) for shape, dtype in scratch],
        compiler_params=pltpu.CompilerParams(vmem_limit_bytes=VMEM_LIMIT),
        cost_estimate=pl.CostEstimate(flops=flops, bytes_accessed=moved, transcendentals=0),
    )(*scalars, *arrays)


def swap_wide(values, bit):
    count = lax.axis_size("wide")
    return lax.ppermute(values, "wide", [(i, i ^ bit) for i in range(count)])


def wide_bits():
    count = lax.axis_size("wide")
    return [1 << k for k in range(count.bit_length() - 1)]


def wide_total(keep, send):
    here = lax.axis_index("wide")
    bits = wide_bits()
    total = keep.astype(jnp.float32) + swap_wide(send, bits[0]).astype(jnp.float32)
    for bit in bits[1:]:
        half = total.shape[0] // 2
        side = (here // bit) % 2
        other = lax.dynamic_slice_in_dim(total, (1 - side) * half, half, 0)
        mine = lax.dynamic_slice_in_dim(total, side * half, half, 0)
        total = mine + swap_wide(low(other), bit).astype(jnp.float32)
    whole = low(total)
    for bit in bits[::-1]:
        side = (here // bit) % 2
        theirs = swap_wide(whole, bit)
        whole = jnp.where(
            side == 0,
            jnp.concatenate([whole, theirs], axis=0),
            jnp.concatenate([theirs, whole], axis=0),
        )
    return whole


def wide_total_small(values):
    for bit in wide_bits():
        values = values + swap_wide(values, bit)
    return values


def whole_rows(
    target, memory, target_lens, source_lens, self_in, self_out, cross_q, cross_kv, cross_out, ffn_in, ffn_in_bias,
    ffn_out, ffn_out_bias, norm_gain, norm_bias, cotangent,
):
    f32, bf16 = jnp.float32, jnp.bfloat16
    _, half, width = target.shape
    length = 2 * half
    hidden = ffn_in.shape[1]
    narrow = lax.axis_index("narrow")
    place = jnp.stack([narrow, lax.axis_index("wide") % 2]).astype(jnp.int32)

    def other_half(values):
        return lax.ppermute(values, "narrow", [(0, 1), (1, 0)])

    own_t, own_m, own_c = target[0], memory[0], cotangent[0]
    other_t, other_m, other_c = other_half(own_t), other_half(own_m), other_half(own_c)
    square = (length, width)
    attn_shape = (HEADS, length, length)
    macs = length * width * width
    triple, self_attn, self_mix, unit_first, scale_first = run_kernel(
        self_forward_kernel,
        (place, target_lens),
        (own_t, other_t, self_in, self_out),
        [((length, 3 * width), bf16), (attn_shape, bf16), (square, bf16), (square, f32), ((length, 1), f32)],
        [(square, bf16), ((length, length), f32)],
        16 * macs,
    )
    query, pairs, cross_attn, cross_mix, unit_second, scale_second = run_kernel(
        cross_forward_kernel,
        (place, target_lens, source_lens),
        (own_m, other_m, unit_first, cross_q, cross_kv, cross_out, norm_gain, norm_bias),
        [
            (square, bf16), ((length, 2 * width), bf16), (attn_shape, bf16), (square, bf16),
            (square, f32), ((length, 1), f32),
        ],
        [(square, bf16), ((length, length), f32)],
        16 * macs,
    )
    (
        output, out_keep, out_send, in_keep, in_send, in_bias_g, norm_third_g, grad_second,
    ) = run_kernel(
        feed_kernel,
        (place,),
        (
            own_c, other_c, unit_second, scale_second, ffn_in, ffn_in_bias[None], ffn_out, ffn_out_bias[None],
            norm_gain, norm_bias,
        ),
        [
            ((half, width), bf16),
            ((hidden // 4, width), f32), ((hidden // 4, width), bf16),
            ((width // 4, hidden), f32), ((width // 4, hidden), bf16),
            ((1, hidden), f32), ((8, width), f32), (square, f32),
        ],
        [
            (square, bf16), (square, bf16), ((length, hidden), bf16), ((length, hidden), f32),
            (square, bf16), ((length, hidden), bf16),
        ],
        40 * macs,
    )
    ffn_out_g = wide_total(out_keep, out_send)
    ffn_in_g = wide_total(in_keep, in_send)
    cross_keep, cross_send, memory_grad, norm_first_g, grad_first = run_kernel(
        cross_back_kernel,
        (place, target_lens, source_lens),
        (
            own_m, other_m, grad_second, unit_first, scale_first, query, pairs, cross_attn, cross_mix,
            cross_q, cross_kv, cross_out, norm_gain, norm_bias,
        ),
        [
            ((width // 4, 4 * width), f32), ((width // 4, 4 * width), bf16), ((half, width), f32),
            ((8, width), f32), (square, f32),
        ],
        [
            (square, bf16), (square, bf16), (square, bf16), (square, bf16), (square, bf16), (square, bf16),
            (square, bf16), ((2 * width, length), bf16),
        ],
        32 * macs,
    )
    cross_g = wide_total(cross_keep, cross_send)
    self_keep, self_send, target_grad = run_kernel(
        self_back_kernel,
        (place,),
        (own_t, other_t, grad_first, triple, self_attn, self_mix, self_in, self_out),
        [
            ((width // 4, 4 * width), f32), ((width // 4, 4 * width), bf16), ((half, width), f32),
        ],
        [
            (square, bf16), (square, bf16), (square, bf16), (square, bf16), (square, bf16),
            (square, bf16), ((2 * width, length), bf16),
        ],
        32 * macs,
    )
    self_g = wide_total(self_keep, self_send)
    vectors = jnp.concatenate([in_bias_g.reshape(-1, width), norm_third_g, norm_first_g], axis=0)
    vectors = wide_total_small(vectors)
    count = hidden // width
    in_bias_g, norm_g = vectors[:count].reshape(-1), vectors[count:]

    def own_part(values):
        size = values.shape[-1] // 2
        return lax.dynamic_slice_in_dim(values, narrow * size, size, values.ndim - 1)

    gain_g = own_part(jnp.stack([norm_g[8], norm_g[2], norm_g[0]]))
    shift_g = own_part(jnp.stack([norm_g[9], norm_g[3], norm_g[1]]))
    return (
        output[None],
        target_grad[None],
        memory_grad[None],
        self_g[:, : 3 * width].astype(f32),
        self_g[:, 3 * width :].astype(f32),
        cross_g[:, :width].astype(f32),
        cross_g[:, width : 3 * width].astype(f32),
        cross_g[:, 3 * width :].astype(f32),
        ffn_in_g.astype(f32),
        own_part(in_bias_g),
        ffn_out_g.astype(f32),
        own_part(norm_g[4]),
        gain_g,
        shift_g,
    )


def fits_whole_rows(mesh, target):
    wide, narrow = mesh.shape["wide"], mesh.shape["narrow"]
    rows, length, width = target.shape
    return (
        narrow == 2
        and rows == wide
        and wide >= 2
        and wide & (wide - 1) == 0
        and length <= 512
        and width == HEADS * HEAD_DIM
        and width % (16 * wide) == 0
    )


def solution(mesh):
    in_specs = (
        P("wide", "narrow", None),
        P("wide", "narrow", None),
        P("wide", None),
        P("wide", None),
        P(),
        P(),
        P(),
        P(),
        P(),
        P(),
        P(),
        P(),
        P(),
        P(),
        P(),
        P("wide", "narrow", None),
    )
    out_specs = (
        P("wide", "narrow", None),
        P("wide", "narrow", None),
        P("wide", "narrow", None),
        P("narrow", None),
        P("narrow", None),
        P("narrow", None),
        P("narrow", None),
        P("narrow", None),
        P("narrow", None),
        P("narrow"),
        P("narrow", None),
        P("narrow"),
        P(None, "narrow"),
        P(None, "narrow"),
    )

    def layer(*arrays):
        body = whole_rows if fits_whole_rows(mesh, arrays[0]) else local
        return jax.shard_map(body, mesh=mesh, in_specs=in_specs, out_specs=out_specs, check_vma=False)(*arrays)

    return layer
```

```python
import functools
import math
import types

import jax
import jax.numpy as jnp
from jax import lax
from jax.experimental import pallas as pl
from jax.experimental.pallas import tpu as pltpu
from jax.sharding import PartitionSpec as P

HEADS = 8
HEAD_DIM = 64


EPSILON = 1e-05
MASKED = -1e30


def segment_ids(doc_lens, length):
    ends = jnp.cumsum(doc_lens, axis=-1)
    places = jnp.arange(length, dtype=jnp.int32)
    return jnp.sum((places[:, None] >= ends[..., None, :]).astype(jnp.int32), axis=-1)


def layer_norm(values, gain, shift):
    centre = values - jnp.mean(values, axis=-1, keepdims=True)
    spread = jnp.mean(centre * centre, axis=-1, keepdims=True)
    return centre * lax.rsqrt(spread + EPSILON) * gain + shift


def gelu_tanh(values):
    return jax.nn.gelu(values, approximate=True)


def project(activity, weight):
    return jnp.einsum("rsd,de->rse", activity, weight, preferred_element_type=jnp.float32)


def project_back(gradient, weight):
    return jnp.einsum("rse,de->rsd", gradient, weight, preferred_element_type=jnp.float32)


def weight_grad(activity, gradient):
    return jnp.einsum("rsd,rse->de", activity, gradient, preferred_element_type=jnp.float32)


def split_heads(values):
    return values.reshape(values.shape[0], values.shape[1], HEADS, HEAD_DIM)


def join_heads(values):
    return values.reshape(values.shape[0], values.shape[1], HEADS * HEAD_DIM)


def block_scores(query_heads, key_heads, query_seg, key_seg, query_pos, key_pos, causal):
    raw_scores = jnp.einsum(
        "rqhd,rkhd->rhqk", query_heads, key_heads, preferred_element_type=jnp.float32
    )
    visible = query_seg[:, :, None] == key_seg[:, None, :]
    if causal:
        visible = visible & (key_pos[None, None, :] <= query_pos[None, :, None])
    return jnp.where(visible[:, None], raw_scores * HEAD_DIM ** (-0.5), MASKED)


def block_backward(query_heads, grad_heads, key_heads, value_heads, scores, log_norm, row_dot):
    attention = jnp.exp(scores - log_norm[..., None])
    grad_attn = jnp.einsum(
        "rqhd,rkhd->rhqk", grad_heads, value_heads, preferred_element_type=jnp.float32
    )
    grad_scores = (attention * (grad_attn - row_dot[..., None]) * HEAD_DIM ** (-0.5)).astype(
        jnp.bfloat16
    )
    grad_query = jnp.einsum(
        "rhqk,rkhd->rqhd", grad_scores, key_heads, preferred_element_type=jnp.float32
    )
    grad_key = jnp.einsum(
        "rhqk,rqhd->rkhd", grad_scores, query_heads, preferred_element_type=jnp.float32
    )
    grad_value = jnp.einsum(
        "rhqk,rqhd->rkhd",
        attention.astype(jnp.bfloat16),
        grad_heads,
        preferred_element_type=jnp.float32,
    )
    return (grad_query, jnp.concatenate([join_heads(grad_key), join_heads(grad_value)], axis=-1))


def make_key_fold(query_heads, query_seg, key_seg_full, query_pos, causal, running, portion):
    run_max, run_sum, stored = running
    span_len = portion.shape[1]
    key_pos = jnp.arange(span_len, dtype=jnp.int32)
    scores = block_scores(
        query_heads,
        split_heads(portion[:, :, : HEADS * HEAD_DIM]),
        query_seg,
        key_seg_full,
        query_pos,
        key_pos,
        causal,
    )
    new_max = jnp.maximum(run_max, jnp.max(scores, axis=-1))
    run_sum = jnp.sum(jnp.exp(scores - new_max[..., None]), axis=-1)
    stored = portion
    return (new_max, run_sum, stored)


def attend_stored(query_heads, stored, query_seg, key_seg_full, query_pos, causal, log_norm):
    total_len = stored.shape[1]
    pair_half = stored.shape[2] // 2
    block_len = math.gcd(total_len, max(query_heads.shape[1], 512))

    def advance(low_sum, block_idx):
        begin_at = block_idx * block_len
        portion = lax.dynamic_slice_in_dim(stored, begin_at, block_len, 1)
        key_seg = lax.dynamic_slice_in_dim(key_seg_full, begin_at, block_len, 1)
        key_pos = begin_at + jnp.arange(block_len, dtype=jnp.int32)
        value_heads = split_heads(portion[:, :, pair_half:])
        scores = block_scores(
            query_heads,
            split_heads(portion[:, :, :pair_half]),
            query_seg,
            key_seg,
            query_pos,
            key_pos,
            causal,
        )
        attention = jnp.exp(scores - log_norm[..., None])
        low_sum = low_sum + jnp.einsum(
            "rhqk,rkhd->rqhd",
            attention.astype(jnp.bfloat16),
            value_heads,
            preferred_element_type=jnp.float32,
        )
        return (low_sum, None)

    zeros_q = jnp.zeros(query_heads.shape, jnp.float32)
    low_sum, _ = lax.scan(advance, zeros_q, jnp.arange(total_len // block_len, dtype=jnp.int32))
    return low_sum


def attend_back_stored(
    query_heads, grad_heads, stored, query_seg, key_seg_full, query_pos, causal, log_norm, row_dot
):
    total_len = stored.shape[1]
    pair_half = stored.shape[2] // 2
    block_len = math.gcd(total_len, max(query_heads.shape[1], 512))

    def advance(block_idx, running):
        grad_query, grad_term = running
        begin_at = block_idx * block_len
        portion = lax.dynamic_slice_in_dim(stored, begin_at, block_len, 1)
        key_seg = lax.dynamic_slice_in_dim(key_seg_full, begin_at, block_len, 1)
        key_pos = begin_at + jnp.arange(block_len, dtype=jnp.int32)
        key_heads = split_heads(portion[:, :, :pair_half])
        value_heads = split_heads(portion[:, :, pair_half:])
        scores = block_scores(
            query_heads, key_heads, query_seg, key_seg, query_pos, key_pos, causal
        )
        block_dq, block_dkv = block_backward(
            query_heads, grad_heads, key_heads, value_heads, scores, log_norm, row_dot
        )
        grad_term = lax.dynamic_update_slice_in_dim(grad_term, block_dkv, begin_at, 1)
        return (grad_query + block_dq, grad_term)

    start_vals = (jnp.zeros(query_heads.shape, jnp.float32), jnp.zeros(stored.shape, jnp.float32))
    grad_query, grad_term = lax.fori_loop(0, total_len // block_len, advance, start_vals)
    return (join_heads(grad_query), grad_term)


def local(
    target,
    memory,
    target_lens,
    source_lens,
    self_in,
    self_out,
    cross_q,
    cross_kv,
    cross_out,
    ffn_in,
    ffn_in_bias,
    ffn_out,
    ffn_out_bias,
    norm_gain,
    norm_bias,
    cotangent,
):
    row_count, shard_len, feat_width = target.shape
    total_len = shard_len * lax.axis_size("narrow")
    own_start = lax.axis_index("narrow") * shard_len
    own_pos = own_start + jnp.arange(shard_len, dtype=jnp.int32)
    target_seg = segment_ids(target_lens, total_len)
    source_seg = segment_ids(source_lens, total_len)
    target_own = lax.dynamic_slice_in_dim(target_seg, own_start, shard_len, 1)
    start_state = (
        jnp.full((row_count, HEADS, shard_len), MASKED, jnp.float32),
        jnp.zeros((row_count, HEADS, shard_len), jnp.float32),
        jnp.zeros((row_count, total_len, 2 * feat_width), jnp.bfloat16),
    )
    triple = project(target, self_in).astype(jnp.bfloat16)
    self_query = split_heads(triple[:, :, :feat_width])
    self_pairs = triple[:, :, feat_width:]
    self_max, self_sum, self_store = make_key_fold(
        self_query,
        target_own,
        target_seg,
        own_pos,
        True,
        start_state,
        lax.all_gather(self_pairs, "narrow", axis=1, tiled=True),
    )
    self_norm = self_max + jnp.log(self_sum)
    self_low = attend_stored(
        self_query, self_store, target_own, target_seg, own_pos, True, self_norm
    )
    self_mix = join_heads(self_low).astype(jnp.bfloat16)
    first, first_pull = jax.vjp(
        layer_norm,
        target.astype(jnp.float32) + project(self_mix, self_out),
        norm_gain[0],
        norm_bias[0],
    )
    first_low = first.astype(jnp.bfloat16)
    cross_query = split_heads(project(first_low, cross_q).astype(jnp.bfloat16))
    cross_pairs = project(memory, cross_kv).astype(jnp.bfloat16)
    cross_max, cross_sum, cross_store = make_key_fold(
        cross_query,
        target_own,
        source_seg,
        own_pos,
        False,
        start_state,
        lax.all_gather(cross_pairs, "narrow", axis=1, tiled=True),
    )
    cross_norm = cross_max + jnp.log(cross_sum)
    cross_low = attend_stored(
        cross_query, cross_store, target_own, source_seg, own_pos, False, cross_norm
    )
    cross_mix = join_heads(cross_low).astype(jnp.bfloat16)
    second, second_pull = jax.vjp(
        layer_norm, first + project(cross_mix, cross_out), norm_gain[1], norm_bias[1]
    )
    second_low = second.astype(jnp.bfloat16)
    inner = project(second_low, ffn_in) + ffn_in_bias
    active, gelu_pull = jax.vjp(gelu_tanh, inner)
    active_low = active.astype(jnp.bfloat16)
    result, third_pull = jax.vjp(
        layer_norm, second + project(active_low, ffn_out) + ffn_out_bias, norm_gain[2], norm_bias[2]
    )
    grad_third, gain_third, shift_third = third_pull(cotangent.astype(jnp.float32))
    grad_outer = grad_third.astype(jnp.bfloat16)
    ffn_out_g = weight_grad(active_low, grad_outer)
    ffn_out_bias_g = jnp.sum(grad_third, axis=(0, 1))
    (grad_active,) = gelu_pull(project_back(grad_outer, ffn_out))
    grad_inner = grad_active.astype(jnp.bfloat16)
    ffn_in_g = weight_grad(second_low, grad_inner)
    ffn_in_bias_g = jnp.sum(grad_active, axis=(0, 1))
    grad_second, gain_second, shift_second = second_pull(
        grad_third + project_back(grad_inner, ffn_in)
    )
    grad_cross = grad_second.astype(jnp.bfloat16)
    cross_out_g = weight_grad(cross_mix, grad_cross)
    cross_dout = split_heads(project_back(grad_cross, cross_out).astype(jnp.bfloat16))
    cross_dot = jnp.swapaxes(jnp.sum(cross_dout.astype(jnp.float32) * cross_low, axis=-1), 1, 2)
    cross_dq, cross_term = attend_back_stored(
        cross_query,
        cross_dout,
        cross_store,
        target_own,
        source_seg,
        own_pos,
        False,
        cross_norm,
        cross_dot,
    )
    cross_dpairs = lax.psum_scatter(
        cross_term.astype(jnp.bfloat16), "narrow", scatter_dimension=1, tiled=True
    )
    cross_dq_low = cross_dq.astype(jnp.bfloat16)
    cross_q_g = weight_grad(first_low, cross_dq_low)
    cross_kv_g = weight_grad(memory, cross_dpairs)
    memory_grad = project_back(cross_dpairs, cross_kv)
    grad_first, gain_first, shift_first = first_pull(
        grad_second + project_back(cross_dq_low, cross_q)
    )
    grad_self = grad_first.astype(jnp.bfloat16)
    self_out_g = weight_grad(self_mix, grad_self)
    self_dout = split_heads(project_back(grad_self, self_out).astype(jnp.bfloat16))
    self_dot = jnp.swapaxes(jnp.sum(self_dout.astype(jnp.float32) * self_low, axis=-1), 1, 2)
    self_dq, self_term = attend_back_stored(
        self_query,
        self_dout,
        self_store,
        target_own,
        target_seg,
        own_pos,
        True,
        self_norm,
        self_dot,
    )
    self_dpairs = lax.psum_scatter(
        self_term.astype(jnp.bfloat16), "narrow", scatter_dimension=1, tiled=True
    ).astype(jnp.float32)
    grad_triple = jnp.concatenate([self_dq, self_dpairs], axis=-1).astype(jnp.bfloat16)
    self_in_g = weight_grad(target, grad_triple)
    target_grad = grad_first + project_back(grad_triple, self_in)
    gain_g = jnp.stack([gain_first, gain_second, gain_third])
    shift_g = jnp.stack([shift_first, shift_second, shift_third])
    sh_a, sh_b, sh_c, sh_d, sh_e, sh_f, sh_g, sh_h, sh_i, sh_j, sh_k = (
        lax.psum_scatter(
            self_in_g.astype(jnp.bfloat16), "narrow", scatter_dimension=0, tiled=True
        ).astype(jnp.float32),
        lax.psum_scatter(
            self_out_g.astype(jnp.bfloat16), "narrow", scatter_dimension=0, tiled=True
        ).astype(jnp.float32),
        lax.psum_scatter(
            cross_q_g.astype(jnp.bfloat16), "narrow", scatter_dimension=0, tiled=True
        ).astype(jnp.float32),
        lax.psum_scatter(
            cross_kv_g.astype(jnp.bfloat16), "narrow", scatter_dimension=0, tiled=True
        ).astype(jnp.float32),
        lax.psum_scatter(
            cross_out_g.astype(jnp.bfloat16), "narrow", scatter_dimension=0, tiled=True
        ).astype(jnp.float32),
        lax.psum_scatter(
            ffn_in_g.astype(jnp.bfloat16), "narrow", scatter_dimension=0, tiled=True
        ).astype(jnp.float32),
        lax.psum_scatter(
            ffn_in_bias_g.astype(jnp.bfloat16), "narrow", scatter_dimension=0, tiled=True
        ).astype(jnp.float32),
        lax.psum_scatter(
            ffn_out_g.astype(jnp.bfloat16), "narrow", scatter_dimension=0, tiled=True
        ).astype(jnp.float32),
        lax.psum_scatter(
            ffn_out_bias_g.astype(jnp.bfloat16), "narrow", scatter_dimension=0, tiled=True
        ).astype(jnp.float32),
        lax.psum_scatter(
            gain_g.astype(jnp.bfloat16), "narrow", scatter_dimension=1, tiled=True
        ).astype(jnp.float32),
        lax.psum_scatter(
            shift_g.astype(jnp.bfloat16), "narrow", scatter_dimension=1, tiled=True
        ).astype(jnp.float32),
    )
    summed = (
        lax.psum(sh_a.astype(jnp.bfloat16), "wide").astype(jnp.float32),
        lax.psum(sh_b.astype(jnp.bfloat16), "wide").astype(jnp.float32),
        lax.psum(sh_c.astype(jnp.bfloat16), "wide").astype(jnp.float32),
        lax.psum(sh_d.astype(jnp.bfloat16), "wide").astype(jnp.float32),
        lax.psum(sh_e.astype(jnp.bfloat16), "wide").astype(jnp.float32),
        lax.psum(sh_f.astype(jnp.bfloat16), "wide").astype(jnp.float32),
        lax.psum(sh_g.astype(jnp.bfloat16), "wide").astype(jnp.float32),
        lax.psum(sh_h.astype(jnp.bfloat16), "wide").astype(jnp.float32),
        lax.psum(sh_i.astype(jnp.bfloat16), "wide").astype(jnp.float32),
        lax.psum(sh_j.astype(jnp.bfloat16), "wide").astype(jnp.float32),
        lax.psum(sh_k.astype(jnp.bfloat16), "wide").astype(jnp.float32),
    )
    return (
        result.astype(jnp.bfloat16),
        target_grad,
        memory_grad,
        summed[0],
        summed[1],
        summed[2],
        summed[3],
        summed[4],
        summed[5],
        summed[6],
        summed[7],
        summed[8],
        summed[9],
        summed[10],
    )


def dot_nn(left, right):
    return jnp.dot(left, right, preferred_element_type=jnp.float32)


def dot_nt(left, right):
    return lax.dot_general(left, right, (((1,), (1,)), ((), ())), preferred_element_type=jnp.float32)


def dot_tn(left, right):
    return lax.dot_general(left, right, (((0,), (0,)), ((), ())), preferred_element_type=jnp.float32)


def low(values):
    return values.astype(jnp.bfloat16)


def centred(values):
    return values - jnp.mean(values, axis=-1, keepdims=True)


def unit_of(centre):
    scale = lax.rsqrt(jnp.mean(centre * centre, axis=-1, keepdims=True) + EPSILON)
    return centre * scale, scale


def normalize_back(grad, gain, unit, scale):
    inner = grad * gain
    return scale * (
        inner
        - jnp.mean(inner, axis=-1, keepdims=True)
        - unit * jnp.mean(inner * unit, axis=-1, keepdims=True)
    )


DOCUMENTS = 8
TARGET_LENS = range(3, 3 + DOCUMENTS)
SOURCE_LENS = range(3 + DOCUMENTS, 3 + 2 * DOCUMENTS)


def seg_along(place_ref, lens, shape, dim):
    places = lax.broadcasted_iota(jnp.int32, shape, dim)
    seg = jnp.zeros(shape, jnp.int32)
    end = jnp.int32(0)
    for doc in lens:
        end = end + place_ref[doc]
        seg = seg + (places >= end).astype(jnp.int32)
    return seg


def visible_pairs(place_ref, query_lens, key_lens, length, causal):
    query_seg = seg_along(place_ref, query_lens, (length, 1), 0)
    seen = query_seg == seg_along(place_ref, key_lens, (1, length), 1)
    if causal:
        rows = lax.broadcasted_iota(jnp.int32, (length, length), 0)
        cols = lax.broadcasted_iota(jnp.int32, (length, length), 1)
        seen = seen & (cols <= rows)
    return seen


class Far:
    def __init__(self, far_refs, near, sems, parts, inward):
        self.near, self.sems, self.inward, self.waited = near, sems, inward, set()
        self.far_refs, self.parts = far_refs, parts

    def copy(self, part):
        far, near = self.far_refs[0 if len(self.far_refs) == 1 else part], self.near
        if self.parts is not None:
            far_at, near_at = self.parts(part)
            far = far if far_at is None else far.at[far_at]
            near = near if near_at is None else near.at[near_at]
        ends = (far, near) if self.inward else (near, far)
        return pltpu.make_async_copy(*ends, self.sems.at[part])

    def start(self):
        for part in range(self.sems.shape[0]):
            self.copy(part).start()

    def wait(self):
        for part in range(self.sems.shape[0]):
            self.copy(part).wait()

    def get(self):
        if 0 not in self.waited:
            self.waited.add(0)
            self.wait()
        return self.near


TOKEN = (8, 128)
SMALL_COST = 25 * 10**9


class Chain:
    def __init__(self):
        self.token = None


class Kernel:
    def __init__(self, chain, place, *scalars):
        self.chain = chain
        self.scalars = (place, *scalars)
        self.operands, self.results, self.scratch, self.entries = [], [], [], {}
        self.place = place

    def _scratch(self, what):
        self.scratch.append(what)
        return ("scratch", len(self.scratch) - 1)

    def _operand(self, array, space):
        if space is not pl.ANY:
            array = pltpu.with_memory_space_constraint(array, space)
        self.operands.append((array, space))
        return ("operand", len(self.operands) - 1)

    def _result(self, shape, dtype, space):
        kept = jax.ShapeDtypeStruct(shape, dtype) if space is pl.ANY else space(shape, dtype)
        self.results.append((kept, space))
        return ("result", len(self.results) - 1)

    def near(self, **arrays):
        for name, array in arrays.items():
            self.entries[name] = ("plain", self._operand(array, pltpu.VMEM))

    def far(self, **arrays):
        for name, array in arrays.items():
            ref = self._operand(array, pltpu.HBM)
            near = self._scratch(pltpu.VMEM(array.shape, array.dtype))
            self.entries[name] = ("far", [ref], near, self._scratch(pltpu.SemaphoreType.DMA((1,))), "all", True)

    def halves(self, **pairs):
        for name, (own, other) in pairs.items():
            refs = [self._operand(own, pltpu.HBM), self._operand(other, pl.ANY)]
            near = self._scratch(pltpu.VMEM((2 * own.shape[0], own.shape[1]), own.dtype))
            self.entries[name] = ("far", refs, near, self._scratch(pltpu.SemaphoreType.DMA((2,))), "halves", True)

    def heads(self, name, array, first, last):
        ref = self._operand(array, pltpu.HBM)
        near = self._scratch(pltpu.VMEM((2 * (last - first),) + array.shape[1:], array.dtype))
        sems = self._scratch(pltpu.SemaphoreType.DMA((last - first,)))
        self.entries[name] = ("far", [ref], near, sems, ("heads", first), True)

    def near_out(self, **outs):
        for name, (shape, dtype) in outs.items():
            self.entries[name] = ("plain", self._result(shape, dtype, pltpu.VMEM))

    def free_out(self, **outs):
        for name, (shape, dtype) in outs.items():
            ref = self._result(shape, dtype, pl.ANY)
            near = self._scratch(pltpu.VMEM(shape, dtype))
            self.entries[name] = ("far", [ref], near, self._scratch(pltpu.SemaphoreType.DMA((1,))), "all", False)

    def far_out(self, **outs):
        for name, (shape, dtype) in outs.items():
            ref = self._result(shape, dtype, pltpu.HBM)
            near = self._scratch(pltpu.VMEM(shape, dtype))
            self.entries[name] = ("far", [ref], near, self._scratch(pltpu.SemaphoreType.DMA((1,))), "all", False)

    def heads_out(self, **outs):
        for name, (shape, dtype) in outs.items():
            ref = self._result(shape, dtype, pltpu.HBM)
            near = self._scratch(pltpu.VMEM(shape, dtype))
            sems = self._scratch(pltpu.SemaphoreType.DMA((shape[0] // 2,)))
            self.entries[name] = ("far", [ref], near, sems, ("heads", 0), False)

    def copy_out(self, **outs):
        for name, (source, shape, dtype) in outs.items():
            ref = self._result(shape, dtype, pltpu.HBM)
            near = self.entries[source][1]
            self.entries[name] = ("far", [ref], near, self._scratch(pltpu.SemaphoreType.DMA((1,))), "all", False)

    def prefetch(self, **arrays):
        for name, array in arrays.items():
            ref = self._operand(array, pltpu.HBM)
            near = self._result(array.shape, array.dtype, pltpu.VMEM)
            sems = self._scratch(pltpu.SemaphoreType.DMA((1,)))
            self.entries["prefetch_" + name] = ("far", [ref], near, sems, "all", True)

    def hold(self, **outs):
        for name, (shape, dtype) in outs.items():
            self.entries[name] = ("plain", self._scratch(pltpu.VMEM(shape, dtype)))

    def run(self, body, flops, vmem_mib):
        if self.chain.token is not None:
            self._operand(self.chain.token, pltpu.VMEM)
        last = self._result(TOKEN, jnp.int32, pltpu.VMEM)[1]

        def kernel(*refs):
            count = len(self.scalars)
            bounds = (count, count + len(self.operands), count + len(self.operands) + len(self.results))
            groups = {
                "operand": refs[bounds[0] : bounds[1]],
                "result": refs[bounds[1] : bounds[2]],
                "scratch": refs[bounds[2] :],
            }
            mine = refs[0][0]
            views = types.SimpleNamespace()
            for name, entry in self.entries.items():
                if entry[0] == "plain":
                    setattr(views, name, groups[entry[1][0]][entry[1][1]])
                    continue
                _, far, near, sems, cut, inward = entry
                near = groups[near[0]][near[1]]
                half = near.shape[0] // 2
                parts = None
                if cut == "halves":

                    def parts(part, half=half):
                        place = mine if part == 0 else 1 - mine
                        return (None, pl.ds(pl.multiple_of(place * half, half), half))

                if isinstance(cut, tuple):

                    def parts(part, skip=cut[1]):
                        return (pl.ds((skip + part) * 2, 2), pl.ds(part * 2, 2))

                setattr(views, name, Far([groups[g][i] for g, i in far], near, groups[sems[0]][sems[1]], parts, inward))
            groups["result"][last][...] = jnp.zeros(TOKEN, jnp.int32)
            for view in vars(views).values():
                if isinstance(view, Far) and view.inward:
                    view.start()
            body(refs[:count], views)
            for name, view in vars(views).items():
                if isinstance(view, Far) and (not view.inward or name.startswith("prefetch_")):
                    view.get()

        arrays = [array for array, _ in self.operands]
        shapes = [kept for kept, _ in self.results]
        moved = sum(math.prod(a.shape) * a.dtype.itemsize for a in arrays)
        *results, self.chain.token = pl.pallas_call(
            kernel,
            out_shape=shapes,
            in_specs=[pl.BlockSpec(memory_space=pltpu.SMEM)] * len(self.scalars)
            + [pl.BlockSpec(memory_space=space) for _, space in self.operands],
            out_specs=[pl.BlockSpec(memory_space=space) for _, space in self.results],
            scratch_shapes=self.scratch,
            compiler_params=pltpu.CompilerParams(vmem_limit_bytes=vmem_mib * 2**20),
            cost_estimate=pl.CostEstimate(flops=flops, bytes_accessed=moved, transcendentals=0),
        )(*self.scalars, *arrays)
        return results


def ref_of(view):
    return view.get() if isinstance(view, Far) else view


def near_of(view):
    return view.near if isinstance(view, Far) else view


def own_columns(ref, start, width):
    return ref[:, pl.ds(pl.multiple_of(start, 128), width)]


def grad_rows(place_ref, activity_ref, grads, keep_ref, send_ref, col):
    rows = keep_ref.shape[0]
    first = place_ref[0] * 2 * rows
    for ref, part in ((keep_ref, place_ref[1]), (send_ref, 1 - place_ref[1])):
        piece = own_columns(activity_ref, first + part * rows, rows)
        at = col
        for grad in grads:
            ref[:, at : at + grad.shape[1]] = dot_tn(piece, grad).astype(ref.dtype)
            at += grad.shape[1]


def query_blocks(length, causal):
    if causal:
        return ((0, length // 2, length // 2), (length // 2, length, length))
    return ((0, length // 2, length), (length // 2, length, length))


PAIR = 2 * HEAD_DIM


def head_lanes():
    lane = lax.broadcasted_iota(jnp.int32, (1, PAIR), 1)
    return (lane < HEAD_DIM, lane >= HEAD_DIM)


def attend_all(query_ref, key_ref, value_ref, bias_ref, attn, mix_ref, causal):
    length = query_ref.shape[0]

    def one_pair(pair, carry):
        lanes = pl.ds(pl.multiple_of(pair * PAIR, PAIR), PAIR)
        keys, values = key_ref[:, lanes], value_ref[:, lanes]
        zero = jnp.zeros_like(keys)
        for begin, end, reach in query_blocks(length, causal):
            queries = query_ref[begin:end, lanes]
            total = jnp.zeros((end - begin, PAIR), jnp.float32)
            for sub, inside in enumerate(head_lanes()):
                scores = dot_nt(queries, jnp.where(inside, keys, zero)[:reach])
                scores = scores + bias_ref[begin:end, :reach]
                weights = jnp.exp(scores - jnp.max(scores, axis=-1, keepdims=True))
                weights = low(weights * (1.0 / jnp.sum(weights, axis=-1, keepdims=True)))
                attn.near[pair * 2 + sub, begin:end, :reach] = weights
                if reach < length:
                    attn.near[pair * 2 + sub, begin:end, reach:] = jnp.zeros((end - begin, length - reach), weights.dtype)
                total = total + dot_nn(weights, jnp.where(inside, values, zero)[:reach])
            mix_ref[begin:end, lanes] = low(total)
        attn.copy(pair).start()
        return carry

    lax.fori_loop(0, HEADS // 2, one_pair, 0, unroll=True)


def attend_all_back(
    pairs, query_ref, query_t_ref, key_ref, value_ref, attn, mix_ref, grad_ref, grad_t_ref, dquery_ref, dpairs_t_ref, causal
):
    length = query_ref.shape[0]
    width = grad_ref.shape[1]

    def one_pair(pair, carry):
        place = pair - pairs[0]
        lanes = pl.ds(pl.multiple_of(pair * PAIR, PAIR), PAIR)
        near_lanes = pl.ds(pl.multiple_of(place * PAIR, PAIR), PAIR)
        attn.copy(place).wait()
        keys, values = key_ref[:, lanes], value_ref[:, lanes]
        zero = jnp.zeros_like(keys)
        blocks = query_blocks(length, causal)
        dquery = [jnp.zeros((end - begin, PAIR), jnp.float32) for begin, end, _ in blocks]
        for sub, inside in enumerate(head_lanes()):
            head_keys = jnp.where(inside, keys, zero)
            head_values = jnp.where(inside, values, zero)
            rows = pl.ds(pl.multiple_of(place * PAIR + sub * HEAD_DIM, HEAD_DIM), HEAD_DIM)
            parts = []
            for idx, (begin, end, reach) in enumerate(blocks):
                grads = grad_ref[begin:end, near_lanes]
                dots = grads.astype(jnp.float32) * mix_ref[begin:end, lanes].astype(jnp.float32)
                row_dot = jnp.sum(jnp.where(inside, dots, 0.0), axis=-1, keepdims=True)
                weights = attn.near[place * 2 + sub, begin:end, :reach]
                dattn = dot_nt(grads, head_values[:reach])
                dscores = low(weights.astype(jnp.float32) * (dattn - row_dot))
                dquery[idx] = dquery[idx] + dot_nn(dscores, head_keys[:reach])
                dkey_t = dot_nn(query_t_ref[rows, begin:end], dscores)
                dvalue_t = dot_nn(grad_t_ref[rows, begin:end], weights)
                parts.append((reach, dkey_t, dvalue_t))
            (reach, dkey_t, dvalue_t), (_, dkey_more, dvalue_more) = parts
            rows_v = pl.ds(pl.multiple_of(width + place * PAIR + sub * HEAD_DIM, HEAD_DIM), HEAD_DIM)
            for where, less, more in ((rows, dkey_t, dkey_more), (rows_v, dvalue_t, dvalue_more)):
                dpairs_t_ref[where, :reach] = low(less + more[:, :reach])
                if reach < length:
                    dpairs_t_ref[where, reach:] = low(more[:, reach:])
        for (begin, end, _), dq in zip(blocks, dquery):
            dquery_ref[begin:end, near_lanes] = low(dq * HEAD_DIM ** (-0.5))
        return carry

    lax.fori_loop(pairs[0], pairs[1], one_pair, 0, unroll=True)


def scaled_query(values):
    return low(low(values) * jnp.bfloat16(HEAD_DIM ** (-0.5)))


def gain_of(vectors_ref, layer):
    return vectors_ref[layer : layer + 1, :]


def shift_of(vectors_ref, layer):
    return vectors_ref[3 + layer : 4 + layer, :]


def first_body(scalars, views):
    (place_ref,) = scalars
    length = views.self_bias.shape[0]
    own, triple = views.own.get(), views.triple_own
    width = own.shape[1]
    weight_ref = views.prefetch_self_in.near
    views.self_bias[...] = jnp.where(visible_pairs(place_ref, TARGET_LENS, TARGET_LENS, length, True), 0.0, MASKED)
    views.cross_bias[...] = jnp.where(visible_pairs(place_ref, TARGET_LENS, SOURCE_LENS, length, False), 0.0, MASKED)
    views.prefetch_self_in.get()
    triple[:, :width] = scaled_query(dot_nn(own[...], weight_ref[:, :width]))
    triple[:, width:] = low(dot_nn(own[...], weight_ref[:, width:]))


def self_forward_body(scalars, views):
    place_ref, = scalars
    other_ref, weight_ref = views.other, views.self_in
    triple, mix = views.triple, views.mix
    half, width = other_ref.shape
    own_rows, other_rows = rows_at(place_ref[0], half), rows_at(1 - place_ref[0], half)
    triple.near[own_rows, :] = views.triple_own[...]
    triple.near[other_rows, :width] = scaled_query(dot_nn(other_ref[...], weight_ref[:, :width]))
    triple.near[other_rows, width:] = low(dot_nn(other_ref[...], weight_ref[:, width:]))
    triple.start()
    attend_all(
        triple.near.at[:, :width], triple.near.at[:, width : 2 * width], triple.near.at[:, 2 * width :],
        views.bias, views.attn, mix.near, True,
    )
    mix.start()
    centre_ref = views.centre_first
    for rows, part_ref in ((own_rows, views.own), (other_rows, other_ref)):
        summed = part_ref[...].astype(jnp.float32) + dot_nn(mix.near[rows, :], views.self_out[...])
        centre_ref[rows, :] = centred(summed)


def cross_forward_body(scalars, views):
    query, pairs, mix = views.query, views.pairs, views.mix
    width = mix.near.shape[1]
    bias_ref, centre_first_ref, vectors_ref = views.bias, views.centre_first, views.vectors
    views.centre_first_far.start()
    first = unit_of(centre_first_ref[...])[0] * gain_of(vectors_ref, 0) + shift_of(vectors_ref, 0)
    query.near[...] = scaled_query(dot_nn(low(first), views.cross_q[...]))
    query.start()
    pairs.near[...] = low(dot_nn(views.memory.get()[...], views.cross_kv[...]))
    pairs.start()
    attend_all(query.near, pairs.near.at[:, :width], pairs.near.at[:, width:], bias_ref, views.attn, mix.near, False)
    mix.start()
    first = unit_of(centre_first_ref[...])[0] * gain_of(vectors_ref, 0) + shift_of(vectors_ref, 0)
    views.centre_second[...] = centred(first + dot_nn(mix.near[...], views.cross_out[...]))


GELU_SCALE = math.sqrt(2.0 / math.pi)
GELU_CUBE = 0.044715


def gelu_both(values):
    square = values * values
    bent = jnp.tanh(GELU_SCALE * (values + GELU_CUBE * (square * values)))
    half_up = 0.5 * (1.0 + bent)
    slope = half_up + 0.5 * values * (1.0 - bent * bent) * (
        GELU_SCALE * (1.0 + 3.0 * GELU_CUBE * square)
    )
    return values * half_up, slope


def feed_body(scalars, views):
    (place_ref,) = scalars
    length, width = views.centre_second.shape
    half = length // 2
    second_ref, active_ref, slope_ref = views.second, views.active, views.slope
    outer_ref, inner_ref, work_ref = views.outer, views.inner, views.grad_second
    vectors_ref = views.vectors
    second = unit_of(views.centre_second[...])[0] * gain_of(vectors_ref, 1) + shift_of(vectors_ref, 1)
    second_ref[...] = low(second)
    total = second + vectors_ref[6:7, :]
    in_ref, out_ref = views.ffn_in, views.ffn_out
    hidden = in_ref.shape[1]
    block = width
    for begin in range(0, hidden, block):
        cols = slice(begin, begin + block)
        inner = dot_nn(second_ref[...], in_ref[:, cols]) + vectors_ref[8 + begin // block : 9 + begin // block, :]
        active, slope_ref[:, cols] = gelu_both(inner)
        active_ref[:, cols] = low(active)
        total = total + dot_nn(active_ref[:, cols], out_ref[cols, :])
    unit, scale = unit_of(centred(total))
    work_ref[...] = unit * gain_of(vectors_ref, 2) + shift_of(vectors_ref, 2)
    views.output.near[...] = low(work_ref[pl.ds(pl.multiple_of(place_ref[0] * half, half), half), :])
    views.output.start()
    cotangent = views.cotangent.get()[...].astype(jnp.float32)
    sums_ref, wide_ref = views.sums, views.in_sums
    sums_ref[0:1, :] = jnp.sum(cotangent * unit, axis=0, keepdims=True)
    sums_ref[1:2, :] = jnp.sum(cotangent, axis=0, keepdims=True)
    grad_third = normalize_back(cotangent, gain_of(vectors_ref, 2), unit, scale)
    sums_ref[2:3, :] = jnp.sum(grad_third, axis=0, keepdims=True)
    outer_ref[...] = low(grad_third)
    work_ref[...] = grad_third
    keep, send = views.keep, views.send
    rows = keep.shape[0]
    groups = hidden // width
    for group in range(groups):
        cols = slice(group * width, (group + 1) * width)
        first = (place_ref[0] * groups + group) * 2 * rows
        for view, part in ((keep, place_ref[1]), (send, 1 - place_ref[1])):
            piece = own_columns(active_ref, first + part * rows, rows)
            view[:, cols] = dot_tn(piece, outer_ref[...]).astype(view.dtype)
    into_second = jnp.zeros((length, width), jnp.float32)
    for begin in range(0, hidden, block):
        cols = slice(begin, begin + block)
        grad_inner = dot_nt(outer_ref[...], out_ref[cols, :]) * slope_ref[:, cols]
        wide_ref[:, cols] = jnp.sum(grad_inner, axis=0, keepdims=True)
        inner_ref[:, cols] = low(grad_inner)
        into_second = into_second + dot_nt(inner_ref[:, cols], in_ref[:, cols])
    grad_rows(place_ref, second_ref, (inner_ref[...],), keep, send, hidden)
    grad = work_ref[...] + into_second
    unit_second, scale_second = unit_of(views.centre_second[...])
    sums_ref[3:4, :] = jnp.sum(grad * unit_second, axis=0, keepdims=True)
    sums_ref[4:5, :] = jnp.sum(grad, axis=0, keepdims=True)
    work_ref[...] = normalize_back(grad, gain_of(vectors_ref, 1), unit_second, scale_second)
    small_ref = views.small
    columns = width // 2
    small_ref[...] = jnp.zeros(small_ref.shape, jnp.float32)
    for row in range(5):
        small_ref[row : row + 1, :] = own_columns(sums_ref.at[row : row + 1, :], place_ref[0] * columns, columns)
    for row in range(hidden // width):
        start = place_ref[0] * (hidden // 2) + row * columns
        small_ref[8 + row : 9 + row, :] = own_columns(wide_ref, start, columns)


def cross_back_body(scalars, views):
    (place_ref,) = scalars
    length, width = views.grad_second.shape
    half = length // 2
    first_ref, grad_ref, dmix_ref, dmix_t_ref = views.first, views.grad, views.dmix, views.dmix_t
    query_t_ref, dquery_ref, dpairs_t_ref = views.query_t, views.dquery, views.dpairs_t
    grad_second_ref = views.grad_second
    grad_ref[...] = low(grad_second_ref[...])
    seen = jnp.where(visible_pairs(place_ref, TARGET_LENS, SOURCE_LENS, length, False), 1.0, 0.0)
    seen = jnp.max(seen, axis=-1, keepdims=True)
    out_ref = views.cross_out
    dmix_ref[...] = low(dot_nt(grad_ref[...], out_ref[...]) * seen)
    dmix_t_ref[...] = low(dot_nt(out_ref[...], grad_ref[...]))
    query_ref = views.query
    query_t_ref[...] = query_ref[...].T
    pairs_ref, mix_ref = views.pairs, views.mix
    attend_all_back(
        (0, HEADS // 2), query_ref, query_t_ref, pairs_ref.at[:, :width], pairs_ref.at[:, width:], views.attn, mix_ref,
        dmix_ref, dmix_t_ref, dquery_ref, dpairs_t_ref, False,
    )
    vectors_ref = views.vectors
    unit_first, scale_first = unit_of(views.centre_first.get()[...])
    first_ref[...] = low(unit_first * gain_of(vectors_ref, 0) + shift_of(vectors_ref, 0))
    memory_grad = views.memory_grad
    own_dpairs = own_columns(dpairs_t_ref, place_ref[0] * half, half).T
    memory_grad.near[...] = dot_nt(own_dpairs, views.cross_kv.get()[...])
    memory_grad.start()
    keep, send = views.keep, views.send
    grad_rows(place_ref, first_ref, (dquery_ref[...],), keep, send, 0)
    grad_rows(place_ref, views.memory.get(), (dpairs_t_ref[...].T,), keep, send, width)
    grad_rows(place_ref, mix_ref, (grad_ref[...],), keep, send, 3 * width)
    grad = grad_second_ref[...] + dot_nt(dquery_ref[...], views.cross_q.get()[...])
    sums_ref, small_ref = views.sums, views.small
    sums_ref[0:1, :] = jnp.sum(grad * unit_first, axis=0, keepdims=True)
    sums_ref[1:2, :] = jnp.sum(grad, axis=0, keepdims=True)
    columns = width // 2
    turned_ref = views.turned
    turned_ref[...] = jnp.zeros(turned_ref.shape, jnp.float32)
    turned_ref[: small_ref.shape[0], :] = small_ref[...]
    for row in range(2):
        turned_ref[5 + row : 6 + row, :] = own_columns(sums_ref.at[row : row + 1, :], place_ref[0] * columns, columns)
    grad_first = normalize_back(grad, gain_of(vectors_ref, 0), unit_first, scale_first)
    views.grad_first[...] = grad_first
    grad_ref[...] = low(grad_first)
    grad_rows(place_ref, views.self_mix.get(), (grad_ref[...],), keep, send, 4 * width)
    rows = keep.shape[0]
    for ref, part in ((keep, place_ref[1]), (send, 1 - place_ref[1])):
        ref[:, 5 * width :] = own_columns(turned_ref, part * rows, rows).T.astype(ref.dtype)


def self_back_body(pairs, scalars, views):
    (place_ref,) = scalars
    length, width = views.grad_first.shape
    half = length // 2
    grad_ref, dmix_ref, dmix_t_ref = views.grad, views.dmix, views.dmix_t
    query_t_ref, dquery_ref, dpairs_t_ref = views.query_t, views.dquery, views.dpairs_t
    first, last = pairs[0] * PAIR, pairs[1] * PAIR
    span = last - first
    grad_ref[...] = low(views.grad_first[...])
    out_ref = views.self_out
    dmix_ref[...] = low(dot_nt(grad_ref[...], out_ref[first:last, :]))
    dmix_t_ref[...] = low(dot_nt(out_ref[first:last, :], grad_ref[...]))
    triple_ref = views.triple
    query_t_ref[...] = triple_ref[:, first:last].T
    attend_all_back(
        pairs, triple_ref.at[:, :width], query_t_ref, triple_ref.at[:, width : 2 * width], triple_ref.at[:, 2 * width :],
        views.attn, views.mix, dmix_ref, dmix_t_ref, dquery_ref, dpairs_t_ref, True,
    )
    keep, send = views.keep, views.send
    grad_rows(place_ref, ref_of(views.target), (dquery_ref[...], dpairs_t_ref[...].T), keep, send, 0)
    own_rows = pl.ds(pl.multiple_of(place_ref[0] * half, half), half)
    own_dpairs = own_columns(dpairs_t_ref, place_ref[0] * half, half).T
    weight_ref = views.self_in.get()
    total = (
        dot_nt(dquery_ref[own_rows, :], weight_ref[:, first:last])
        + dot_nt(own_dpairs[:, :span], weight_ref[:, width + first : width + last])
        + dot_nt(own_dpairs[:, span:], weight_ref[:, 2 * width + first : 2 * width + last])
    )
    total = total + views.grad_first[own_rows, :]
    views.target_grad[...] = total


def send_wide(values, bit):
    count = lax.axis_size("wide")
    return lax.ppermute(values, "wide", [(i, i ^ (1 << bit)) for i in range(count)])


def bit_of(place_ref, bit):
    return (place_ref[2] >> bit) & 1


def small_kernel(chain, body, scalars, arrays, outs):
    token = pltpu.with_memory_space_constraint(chain.token, pltpu.VMEM)

    def kernel(*refs):
        refs = list(refs)
        refs.pop()[...] = jnp.zeros(TOKEN, jnp.int32)
        refs.pop(len(scalars) + len(arrays))
        body(*refs)

    *results, chain.token = pl.pallas_call(
        kernel,
        out_shape=[jax.ShapeDtypeStruct(shape, dtype) for shape, dtype in outs] + [pltpu.VMEM(TOKEN, jnp.int32)],
        in_specs=[pl.BlockSpec(memory_space=pltpu.SMEM)] * len(scalars)
        + [pl.BlockSpec(memory_space=pltpu.VMEM)] * (len(arrays) + 1),
        out_specs=[pl.BlockSpec(memory_space=pltpu.VMEM)] * (len(outs) + 1),
        compiler_params=pltpu.CompilerParams(vmem_limit_bytes=12 * 2**20),
        cost_estimate=pl.CostEstimate(flops=SMALL_COST, bytes_accessed=1, transcendentals=0),
    )(*scalars, *arrays, token)
    return results


def rows_at(start, rows):
    return pl.ds(pl.multiple_of(start * rows, rows), rows)


def add_split(chain, place, keep, received, bit):
    rows = keep.shape[0] // 2
    shape = (rows,) + keep.shape[1:]

    def body(place_ref, keep_ref, came_ref, mine_ref, send_ref):
        mine = bit_of(place_ref, bit)
        for out, part in ((mine_ref, mine), (send_ref, 1 - mine)):
            where = rows_at(part, rows)
            out[...] = (keep_ref[where, :].astype(jnp.float32) + came_ref[where, :].astype(jnp.float32)).astype(out.dtype)

    outs = [(shape, jnp.float32), (shape, jnp.bfloat16)]
    return small_kernel(chain, body, (place,), (keep, received), outs)


def add_low(chain, keep, received):
    def body(keep_ref, came_ref, out_ref):
        out_ref[...] = low(keep_ref[...].astype(jnp.float32) + came_ref[...].astype(jnp.float32))

    return small_kernel(chain, body, (), (keep, received), [(keep.shape, jnp.bfloat16)])[0]


def join_rows(chain, place, piece, received, bit):
    rows = piece.shape[0]

    def body(place_ref, own_ref, came_ref, out_ref):
        mine = bit_of(place_ref, bit)
        out_ref[rows_at(mine, rows), :] = own_ref[...]
        out_ref[rows_at(1 - mine, rows), :] = came_ref[...]

    shape = (2 * rows,) + piece.shape[1:]
    return small_kernel(chain, body, (place,), (piece, received), [(shape, piece.dtype)])[0]


def finish(chain, place, piece, received, cuts, outs, vectors=None):
    rows = piece.shape[0]

    def body(place_ref, *refs):
        for step in range(2):
            part = place_ref[1] ^ step
            for out, row, col, begin, size in cuts:
                where = pl.ds(pl.multiple_of(row + part * rows, rows), rows)
                refs[2 + out][where, col : col + size] = refs[step][:, begin : begin + size].astype(jnp.float32)
        if vectors:
            last = refs[0].shape[1] - 128
            turned = [refs[step][:, last:].astype(jnp.float32).T for step in range(2)]
            swap = place_ref[1] == 1
            turned = jnp.concatenate(
                [jnp.where(swap, turned[1], turned[0]), jnp.where(swap, turned[0], turned[1])], axis=1
            )
            for out, row, col, index in vectors:
                refs[2 + out][row : row + 1, col : col + 2 * rows] = turned[index : index + 1, :]

    return small_kernel(chain, body, (place,), (piece, received), outs)


HALVE, WHOLE, DOUBLE = range(3)


def rounds_of(bits):
    return [(HALVE, bit) for bit in bits[:-1]] + [(WHOLE, bits[-1])] + [(DOUBLE, bit) for bit in reversed(bits[:-1])]


class Chunk:
    def __init__(self, chain, place, keep, send, rounds):
        self.chain, self.place = chain, place
        self.kept, self.send = keep, send
        self.rounds, self.at = rounds, 0
        self.launch()

    def launch(self):
        self.received = send_wide(self.send, self.rounds[self.at][1])

    def advance(self):
        kind, bit = self.rounds[self.at]
        self.at += 1
        following, next_bit = self.rounds[self.at]
        if kind == DOUBLE:
            self.kept = self.send = join_rows(self.chain, self.place, self.kept, self.received, bit)
        elif following == HALVE:
            self.kept, self.send = add_split(self.chain, self.place, self.kept, self.received, next_bit)
        else:
            self.kept = self.send = add_low(self.chain, self.kept, self.received)
        self.launch()

    def left(self):
        return len(self.rounds) - 1 - self.at

    def finish(self, cuts, outs, vectors=None):
        return finish(self.chain, self.place, self.kept, self.received, cuts, outs, vectors)


def near_first(bits):
    return rounds_of(list(range(bits)))


def far_first(bits):
    return rounds_of([0] + list(range(2, bits)) + [1])


ORDER = dict(a=near_first, c=near_first, d=far_first)
SCHEDULE = ("a", "a", "acdcadcdadcdcadacdc")


def whole_rows(
    target, memory, target_lens, source_lens, self_in, self_out, cross_q, cross_kv, cross_out, ffn_in, ffn_in_bias,
    ffn_out, ffn_out_bias, norm_gain, norm_bias, cotangent,
):
    f32, bf16 = jnp.float32, jnp.bfloat16
    _, half, width = target.shape
    length = 2 * half
    hidden = ffn_in.shape[1]
    wide = lax.axis_index("wide")
    place = jnp.stack([lax.axis_index("narrow"), wide % 2, wide]).astype(jnp.int32)
    place = jnp.concatenate([place, target_lens[0], source_lens[0]])
    chain = Chain()

    def other_half(values):
        return lax.ppermute(values, "narrow", [(0, 1), (1, 0)])

    own_t, own_m, own_c = target[0], memory[0], cotangent[0]
    other_t, other_m, other_c = other_half(own_t), other_half(own_m), other_half(own_c)
    square = (length, width)
    attn_shape = (HEADS, length, length)
    macs = length * width * width
    rows = width // 4

    vectors = jnp.concatenate(
        [norm_gain, norm_bias, ffn_out_bias[None], jnp.zeros((1, width), f32), ffn_in_bias.reshape(-1, width)], axis=0
    )
    vectors = jnp.pad(vectors, ((0, -vectors.shape[0] % 8), (0, 0)))

    step = Kernel(chain, place)
    step.far(own=own_t)
    step.prefetch(self_in=self_in, self_out=self_out, cross_q=cross_q, cross_kv=cross_kv, cross_out=cross_out, own_t=own_t)
    step.near_out(
        triple_own=((half, 3 * width), bf16), self_bias=((length, length), f32), cross_bias=((length, length), f32)
    )
    (
        self_in_near, self_out_near, cross_q_near, cross_kv_near, cross_out_near, own_near, triple_own, self_bias, cross_bias,
    ) = step.run(first_body, 8 * macs, 12)

    step = Kernel(chain, place)
    step.near(other=other_t)
    step.near(self_in=self_in_near, self_out=self_out_near, own=own_near, triple_own=triple_own, bias=self_bias)
    step.far_out(triple=((length, 3 * width), bf16), mix=(square, bf16))
    step.heads_out(attn=(attn_shape, bf16))
    step.near_out(centre_first=(square, f32))
    triple, self_mix, self_attn, centre_first = step.run(self_forward_body, 24 * macs, 16)

    step = Kernel(chain, place)
    step.halves(memory=(own_m, other_m))
    step.near(centre_first=centre_first, cross_q=cross_q_near, cross_kv=cross_kv_near, cross_out=cross_out_near)
    step.near(vectors=vectors, bias=cross_bias)
    step.copy_out(centre_first_far=("centre_first", square, f32))
    step.far_out(query=(square, bf16), pairs=((length, 2 * width), bf16), mix=(square, bf16))
    step.heads_out(attn=(attn_shape, bf16))
    step.near_out(centre_second=(square, f32))
    step.prefetch(ffn_in=ffn_in, ffn_out=ffn_out)
    (
        centre_first, query, pairs, cross_mix, cross_attn, centre_second, ffn_in_near, ffn_out_near,
    ) = step.run(cross_forward_body, 24 * macs, 16)

    step = Kernel(chain, place)
    step.near(centre_second=centre_second, ffn_in=ffn_in_near, ffn_out=ffn_out_near, vectors=vectors)
    step.halves(cotangent=(own_c, other_c))
    step.far_out(output=((half, width), bf16))
    step.near_out(
        small=((16, half), f32), grad_second=(square, f32),
        keep=((rows, 2 * hidden), f32), send=((rows, 2 * hidden), bf16),
    )
    step.prefetch(cross_out=cross_out, query=query, pairs=pairs, mix=cross_mix)
    step.hold(
        second=(square, bf16), active=((length, hidden), bf16), slope=((length, hidden), f32), outer=(square, bf16),
        inner=((length, hidden), bf16), sums=((8, width), f32), in_sums=((1, hidden), f32),
    )
    (
        output, small, grad_second, feed_keep, feed_send, cross_out_near, query, pairs, cross_mix,
    ) = step.run(feed_body, 40 * macs, 26)

    bits = lax.axis_size("wide").bit_length() - 1
    orders = {name: ORDER[name](bits) for name in ORDER}
    chunk_a = Chunk(chain, place, feed_keep, feed_send, orders["a"])
    chunks = dict(a=chunk_a)
    for name in SCHEDULE[0]:
        chunks[name].advance()

    step = Kernel(chain, place)
    step.near(grad_second=grad_second, small=small, vectors=vectors)
    step.near(cross_out=cross_out_near, query=query, pairs=pairs, mix=cross_mix)
    step.heads("attn", cross_attn, 0, HEADS // 2)
    step.far(cross_kv=cross_kv)
    step.halves(memory=(own_m, other_m))
    step.far(centre_first=centre_first, cross_q=cross_q, self_mix=self_mix)
    step.far_out(memory_grad=((half, width), f32))
    step.near_out(
        grad_first=(square, f32), keep=((rows, 5 * width + 128), f32), send=((rows, 5 * width + 128), bf16)
    )
    step.prefetch(self_out=self_out, triple=triple, mix=self_mix)
    step.hold(
        first=(square, bf16), grad=(square, bf16), dmix=(square, bf16), dmix_t=(square, bf16), query_t=(square, bf16),
        dquery=(square, bf16), dpairs_t=((2 * width, length), bf16), sums=((8, width), f32), turned=((128, half), f32),
    )
    memory_grad, grad_first, cross_keep, cross_send, self_out_near, triple, self_mix = step.run(cross_back_body, 48 * macs * 4, 24)

    chunk_c = chunks["c"] = Chunk(chain, place, cross_keep, cross_send, orders["c"])
    for name in SCHEDULE[1]:
        chunks[name].advance()

    def self_part(first, last):
        span = (last - first) * PAIR
        step = Kernel(chain, place)
        step.near(grad_first=grad_first)
        step.near(self_out=self_out_near, triple=triple, mix=self_mix)
        step.heads("attn", self_attn, first, last)
        step.halves(target=(own_t, other_t))
        step.far(self_in=self_in)
        step.near_out(target_grad=((half, width), f32))
        step.near_out(keep=((rows, 3 * span), f32), send=((rows, 3 * span), bf16))
        step.hold(
            grad=(square, bf16), dmix=((length, span), bf16), dmix_t=((span, length), bf16),
            query_t=((span, length), bf16), dquery=((length, span), bf16), dpairs_t=((2 * span, length), bf16),
        )
        return step.run(functools.partial(self_back_body, (first, last)), 24 * macs * 12, 16)

    target_grad, keep, send = self_part(0, HEADS // 2)
    chunk_d = chunks["d"] = Chunk(chain, place, keep, send, orders["d"])
    groups = hidden // width
    endings = dict(
        a=(
            [(0, group * half, 0, group * width, width) for group in range(groups)] + [(1, 0, 0, hidden, hidden)],
            [((groups * half, width), f32), ((half, hidden), f32)],
        ),
        c=(
            [(0, 0, 0, 0, width), (1, 0, 0, width, 2 * width), (2, 0, 0, 3 * width, width), (3, 0, 0, 4 * width, width)],
            [
                ((half, width), f32), ((half, 2 * width), f32), ((half, width), f32), ((half, width), f32),
                ((3, half), f32), ((3, half), f32), ((1, half), f32), ((1, groups * half), f32),
            ],
            [(4, 0, 0, 5), (4, 1, 0, 3), (4, 2, 0, 0), (5, 0, 0, 6), (5, 1, 0, 4), (5, 2, 0, 1), (6, 0, 0, 2)]
            + [(7, 0, row * half, 8 + row) for row in range(groups)],
        ),
        d=([(0, 0, 0, 0, 3 * width)], [((half, 3 * width), f32)]),
    )
    finished = {}
    for name in SCHEDULE[2]:
        if chunks[name].left():
            chunks[name].advance()
        elif name not in finished:
            finished[name] = chunks[name].finish(*endings[name])
    ffn_out_g, ffn_in_g = finished["a"]
    cross_q_g, cross_kv_g, cross_out_g, self_out_g, gain_g, shift_g, out_bias_g, in_bias_g = finished["c"]
    (self_in_g,) = finished["d"]
    return (
        output[None],
        target_grad[None],
        memory_grad[None],
        self_in_g,
        self_out_g,
        cross_q_g,
        cross_kv_g,
        cross_out_g,
        ffn_in_g,
        in_bias_g[0],
        ffn_out_g,
        out_bias_g[0],
        gain_g,
        shift_g,
    )


def fits_whole_rows(mesh, target, lens):
    wide, narrow = mesh.shape["wide"], mesh.shape["narrow"]
    rows, length, width = target.shape
    documents = lens.shape[1]
    return (
        narrow == 2
        and rows == wide
        and wide >= 2
        and wide & (wide - 1) == 0
        and length <= 512
        and documents == DOCUMENTS
        and width == HEADS * HEAD_DIM
        and width % (32 * wide) == 0
    )


def solution(mesh):
    in_specs = (
        P("wide", "narrow", None),
        P("wide", "narrow", None),
        P("wide", None),
        P("wide", None),
        P(),
        P(),
        P(),
        P(),
        P(),
        P(),
        P(),
        P(),
        P(),
        P(),
        P(),
        P("wide", "narrow", None),
    )
    out_specs = (
        P("wide", "narrow", None),
        P("wide", "narrow", None),
        P("wide", "narrow", None),
        P("narrow", None),
        P("narrow", None),
        P("narrow", None),
        P("narrow", None),
        P("narrow", None),
        P("narrow", None),
        P("narrow"),
        P("narrow", None),
        P("narrow"),
        P(None, "narrow"),
        P(None, "narrow"),
    )

    def layer(*arrays):
        body = whole_rows if fits_whole_rows(mesh, arrays[0], arrays[2]) else local
        return jax.shard_map(body, mesh=mesh, in_specs=in_specs, out_specs=out_specs, check_vma=False)(*arrays)

    return layer
```

```python
import functools
import math
import types

import jax
import jax.numpy as jnp
from jax import lax
from jax.experimental import pallas as pl
from jax.experimental.pallas import tpu as pltpu
from jax.sharding import PartitionSpec as P

HEADS = 8
HEAD_DIM = 64


EPSILON = 1e-05
MASKED = -1e30


def segment_ids(doc_lens, length):
    ends = jnp.cumsum(doc_lens, axis=-1)
    places = jnp.arange(length, dtype=jnp.int32)
    return jnp.sum((places[:, None] >= ends[..., None, :]).astype(jnp.int32), axis=-1)


def layer_norm(values, gain, shift):
    centre = values - jnp.mean(values, axis=-1, keepdims=True)
    spread = jnp.mean(centre * centre, axis=-1, keepdims=True)
    return centre * lax.rsqrt(spread + EPSILON) * gain + shift


def gelu_tanh(values):
    return jax.nn.gelu(values, approximate=True)


def project(activity, weight):
    return jnp.einsum("rsd,de->rse", activity, weight, preferred_element_type=jnp.float32)


def project_back(gradient, weight):
    return jnp.einsum("rse,de->rsd", gradient, weight, preferred_element_type=jnp.float32)


def weight_grad(activity, gradient):
    return jnp.einsum("rsd,rse->de", activity, gradient, preferred_element_type=jnp.float32)


def split_heads(values):
    return values.reshape(values.shape[0], values.shape[1], HEADS, HEAD_DIM)


def join_heads(values):
    return values.reshape(values.shape[0], values.shape[1], HEADS * HEAD_DIM)


def block_scores(query_heads, key_heads, query_seg, key_seg, query_pos, key_pos, causal):
    raw_scores = jnp.einsum(
        "rqhd,rkhd->rhqk", query_heads, key_heads, preferred_element_type=jnp.float32
    )
    visible = query_seg[:, :, None] == key_seg[:, None, :]
    if causal:
        visible = visible & (key_pos[None, None, :] <= query_pos[None, :, None])
    return jnp.where(visible[:, None], raw_scores * HEAD_DIM ** (-0.5), MASKED)


def block_backward(query_heads, grad_heads, key_heads, value_heads, scores, log_norm, row_dot):
    attention = jnp.exp(scores - log_norm[..., None])
    grad_attn = jnp.einsum(
        "rqhd,rkhd->rhqk", grad_heads, value_heads, preferred_element_type=jnp.float32
    )
    grad_scores = (attention * (grad_attn - row_dot[..., None]) * HEAD_DIM ** (-0.5)).astype(
        jnp.bfloat16
    )
    grad_query = jnp.einsum(
        "rhqk,rkhd->rqhd", grad_scores, key_heads, preferred_element_type=jnp.float32
    )
    grad_key = jnp.einsum(
        "rhqk,rqhd->rkhd", grad_scores, query_heads, preferred_element_type=jnp.float32
    )
    grad_value = jnp.einsum(
        "rhqk,rqhd->rkhd",
        attention.astype(jnp.bfloat16),
        grad_heads,
        preferred_element_type=jnp.float32,
    )
    return (grad_query, jnp.concatenate([join_heads(grad_key), join_heads(grad_value)], axis=-1))


def make_key_fold(query_heads, query_seg, key_seg_full, query_pos, causal, running, portion):
    run_max, run_sum, stored = running
    span_len = portion.shape[1]
    key_pos = jnp.arange(span_len, dtype=jnp.int32)
    scores = block_scores(
        query_heads,
        split_heads(portion[:, :, : HEADS * HEAD_DIM]),
        query_seg,
        key_seg_full,
        query_pos,
        key_pos,
        causal,
    )
    new_max = jnp.maximum(run_max, jnp.max(scores, axis=-1))
    run_sum = jnp.sum(jnp.exp(scores - new_max[..., None]), axis=-1)
    stored = portion
    return (new_max, run_sum, stored)


def attend_stored(query_heads, stored, query_seg, key_seg_full, query_pos, causal, log_norm):
    total_len = stored.shape[1]
    pair_half = stored.shape[2] // 2
    block_len = math.gcd(total_len, max(query_heads.shape[1], 512))

    def advance(low_sum, block_idx):
        begin_at = block_idx * block_len
        portion = lax.dynamic_slice_in_dim(stored, begin_at, block_len, 1)
        key_seg = lax.dynamic_slice_in_dim(key_seg_full, begin_at, block_len, 1)
        key_pos = begin_at + jnp.arange(block_len, dtype=jnp.int32)
        value_heads = split_heads(portion[:, :, pair_half:])
        scores = block_scores(
            query_heads,
            split_heads(portion[:, :, :pair_half]),
            query_seg,
            key_seg,
            query_pos,
            key_pos,
            causal,
        )
        attention = jnp.exp(scores - log_norm[..., None])
        low_sum = low_sum + jnp.einsum(
            "rhqk,rkhd->rqhd",
            attention.astype(jnp.bfloat16),
            value_heads,
            preferred_element_type=jnp.float32,
        )
        return (low_sum, None)

    zeros_q = jnp.zeros(query_heads.shape, jnp.float32)
    low_sum, _ = lax.scan(advance, zeros_q, jnp.arange(total_len // block_len, dtype=jnp.int32))
    return low_sum


def attend_back_stored(
    query_heads, grad_heads, stored, query_seg, key_seg_full, query_pos, causal, log_norm, row_dot
):
    total_len = stored.shape[1]
    pair_half = stored.shape[2] // 2
    block_len = math.gcd(total_len, max(query_heads.shape[1], 512))

    def advance(block_idx, running):
        grad_query, grad_term = running
        begin_at = block_idx * block_len
        portion = lax.dynamic_slice_in_dim(stored, begin_at, block_len, 1)
        key_seg = lax.dynamic_slice_in_dim(key_seg_full, begin_at, block_len, 1)
        key_pos = begin_at + jnp.arange(block_len, dtype=jnp.int32)
        key_heads = split_heads(portion[:, :, :pair_half])
        value_heads = split_heads(portion[:, :, pair_half:])
        scores = block_scores(
            query_heads, key_heads, query_seg, key_seg, query_pos, key_pos, causal
        )
        block_dq, block_dkv = block_backward(
            query_heads, grad_heads, key_heads, value_heads, scores, log_norm, row_dot
        )
        grad_term = lax.dynamic_update_slice_in_dim(grad_term, block_dkv, begin_at, 1)
        return (grad_query + block_dq, grad_term)

    start_vals = (jnp.zeros(query_heads.shape, jnp.float32), jnp.zeros(stored.shape, jnp.float32))
    grad_query, grad_term = lax.fori_loop(0, total_len // block_len, advance, start_vals)
    return (join_heads(grad_query), grad_term)


def local(
    target,
    memory,
    target_lens,
    source_lens,
    self_in,
    self_out,
    cross_q,
    cross_kv,
    cross_out,
    ffn_in,
    ffn_in_bias,
    ffn_out,
    ffn_out_bias,
    norm_gain,
    norm_bias,
    cotangent,
):
    row_count, shard_len, feat_width = target.shape
    total_len = shard_len * lax.axis_size("narrow")
    own_start = lax.axis_index("narrow") * shard_len
    own_pos = own_start + jnp.arange(shard_len, dtype=jnp.int32)
    target_seg = segment_ids(target_lens, total_len)
    source_seg = segment_ids(source_lens, total_len)
    target_own = lax.dynamic_slice_in_dim(target_seg, own_start, shard_len, 1)
    start_state = (
        jnp.full((row_count, HEADS, shard_len), MASKED, jnp.float32),
        jnp.zeros((row_count, HEADS, shard_len), jnp.float32),
        jnp.zeros((row_count, total_len, 2 * feat_width), jnp.bfloat16),
    )
    triple = project(target, self_in).astype(jnp.bfloat16)
    self_query = split_heads(triple[:, :, :feat_width])
    self_pairs = triple[:, :, feat_width:]
    self_max, self_sum, self_store = make_key_fold(
        self_query,
        target_own,
        target_seg,
        own_pos,
        True,
        start_state,
        lax.all_gather(self_pairs, "narrow", axis=1, tiled=True),
    )
    self_norm = self_max + jnp.log(self_sum)
    self_low = attend_stored(
        self_query, self_store, target_own, target_seg, own_pos, True, self_norm
    )
    self_mix = join_heads(self_low).astype(jnp.bfloat16)
    first, first_pull = jax.vjp(
        layer_norm,
        target.astype(jnp.float32) + project(self_mix, self_out),
        norm_gain[0],
        norm_bias[0],
    )
    first_low = first.astype(jnp.bfloat16)
    cross_query = split_heads(project(first_low, cross_q).astype(jnp.bfloat16))
    cross_pairs = project(memory, cross_kv).astype(jnp.bfloat16)
    cross_max, cross_sum, cross_store = make_key_fold(
        cross_query,
        target_own,
        source_seg,
        own_pos,
        False,
        start_state,
        lax.all_gather(cross_pairs, "narrow", axis=1, tiled=True),
    )
    cross_norm = cross_max + jnp.log(cross_sum)
    cross_low = attend_stored(
        cross_query, cross_store, target_own, source_seg, own_pos, False, cross_norm
    )
    cross_mix = join_heads(cross_low).astype(jnp.bfloat16)
    second, second_pull = jax.vjp(
        layer_norm, first + project(cross_mix, cross_out), norm_gain[1], norm_bias[1]
    )
    second_low = second.astype(jnp.bfloat16)
    inner = project(second_low, ffn_in) + ffn_in_bias
    active, gelu_pull = jax.vjp(gelu_tanh, inner)
    active_low = active.astype(jnp.bfloat16)
    result, third_pull = jax.vjp(
        layer_norm, second + project(active_low, ffn_out) + ffn_out_bias, norm_gain[2], norm_bias[2]
    )
    grad_third, gain_third, shift_third = third_pull(cotangent.astype(jnp.float32))
    grad_outer = grad_third.astype(jnp.bfloat16)
    ffn_out_g = weight_grad(active_low, grad_outer)
    ffn_out_bias_g = jnp.sum(grad_third, axis=(0, 1))
    (grad_active,) = gelu_pull(project_back(grad_outer, ffn_out))
    grad_inner = grad_active.astype(jnp.bfloat16)
    ffn_in_g = weight_grad(second_low, grad_inner)
    ffn_in_bias_g = jnp.sum(grad_active, axis=(0, 1))
    grad_second, gain_second, shift_second = second_pull(
        grad_third + project_back(grad_inner, ffn_in)
    )
    grad_cross = grad_second.astype(jnp.bfloat16)
    cross_out_g = weight_grad(cross_mix, grad_cross)
    cross_dout = split_heads(project_back(grad_cross, cross_out).astype(jnp.bfloat16))
    cross_dot = jnp.swapaxes(jnp.sum(cross_dout.astype(jnp.float32) * cross_low, axis=-1), 1, 2)
    cross_dq, cross_term = attend_back_stored(
        cross_query,
        cross_dout,
        cross_store,
        target_own,
        source_seg,
        own_pos,
        False,
        cross_norm,
        cross_dot,
    )
    cross_dpairs = lax.psum_scatter(
        cross_term.astype(jnp.bfloat16), "narrow", scatter_dimension=1, tiled=True
    )
    cross_dq_low = cross_dq.astype(jnp.bfloat16)
    cross_q_g = weight_grad(first_low, cross_dq_low)
    cross_kv_g = weight_grad(memory, cross_dpairs)
    memory_grad = project_back(cross_dpairs, cross_kv)
    grad_first, gain_first, shift_first = first_pull(
        grad_second + project_back(cross_dq_low, cross_q)
    )
    grad_self = grad_first.astype(jnp.bfloat16)
    self_out_g = weight_grad(self_mix, grad_self)
    self_dout = split_heads(project_back(grad_self, self_out).astype(jnp.bfloat16))
    self_dot = jnp.swapaxes(jnp.sum(self_dout.astype(jnp.float32) * self_low, axis=-1), 1, 2)
    self_dq, self_term = attend_back_stored(
        self_query,
        self_dout,
        self_store,
        target_own,
        target_seg,
        own_pos,
        True,
        self_norm,
        self_dot,
    )
    self_dpairs = lax.psum_scatter(
        self_term.astype(jnp.bfloat16), "narrow", scatter_dimension=1, tiled=True
    ).astype(jnp.float32)
    grad_triple = jnp.concatenate([self_dq, self_dpairs], axis=-1).astype(jnp.bfloat16)
    self_in_g = weight_grad(target, grad_triple)
    target_grad = grad_first + project_back(grad_triple, self_in)
    gain_g = jnp.stack([gain_first, gain_second, gain_third])
    shift_g = jnp.stack([shift_first, shift_second, shift_third])
    sh_a, sh_b, sh_c, sh_d, sh_e, sh_f, sh_g, sh_h, sh_i, sh_j, sh_k = (
        lax.psum_scatter(
            self_in_g.astype(jnp.bfloat16), "narrow", scatter_dimension=0, tiled=True
        ).astype(jnp.float32),
        lax.psum_scatter(
            self_out_g.astype(jnp.bfloat16), "narrow", scatter_dimension=0, tiled=True
        ).astype(jnp.float32),
        lax.psum_scatter(
            cross_q_g.astype(jnp.bfloat16), "narrow", scatter_dimension=0, tiled=True
        ).astype(jnp.float32),
        lax.psum_scatter(
            cross_kv_g.astype(jnp.bfloat16), "narrow", scatter_dimension=0, tiled=True
        ).astype(jnp.float32),
        lax.psum_scatter(
            cross_out_g.astype(jnp.bfloat16), "narrow", scatter_dimension=0, tiled=True
        ).astype(jnp.float32),
        lax.psum_scatter(
            ffn_in_g.astype(jnp.bfloat16), "narrow", scatter_dimension=0, tiled=True
        ).astype(jnp.float32),
        lax.psum_scatter(
            ffn_in_bias_g.astype(jnp.bfloat16), "narrow", scatter_dimension=0, tiled=True
        ).astype(jnp.float32),
        lax.psum_scatter(
            ffn_out_g.astype(jnp.bfloat16), "narrow", scatter_dimension=0, tiled=True
        ).astype(jnp.float32),
        lax.psum_scatter(
            ffn_out_bias_g.astype(jnp.bfloat16), "narrow", scatter_dimension=0, tiled=True
        ).astype(jnp.float32),
        lax.psum_scatter(
            gain_g.astype(jnp.bfloat16), "narrow", scatter_dimension=1, tiled=True
        ).astype(jnp.float32),
        lax.psum_scatter(
            shift_g.astype(jnp.bfloat16), "narrow", scatter_dimension=1, tiled=True
        ).astype(jnp.float32),
    )
    summed = (
        lax.psum(sh_a.astype(jnp.bfloat16), "wide").astype(jnp.float32),
        lax.psum(sh_b.astype(jnp.bfloat16), "wide").astype(jnp.float32),
        lax.psum(sh_c.astype(jnp.bfloat16), "wide").astype(jnp.float32),
        lax.psum(sh_d.astype(jnp.bfloat16), "wide").astype(jnp.float32),
        lax.psum(sh_e.astype(jnp.bfloat16), "wide").astype(jnp.float32),
        lax.psum(sh_f.astype(jnp.bfloat16), "wide").astype(jnp.float32),
        lax.psum(sh_g.astype(jnp.bfloat16), "wide").astype(jnp.float32),
        lax.psum(sh_h.astype(jnp.bfloat16), "wide").astype(jnp.float32),
        lax.psum(sh_i.astype(jnp.bfloat16), "wide").astype(jnp.float32),
        lax.psum(sh_j.astype(jnp.bfloat16), "wide").astype(jnp.float32),
        lax.psum(sh_k.astype(jnp.bfloat16), "wide").astype(jnp.float32),
    )
    return (
        result.astype(jnp.bfloat16),
        target_grad,
        memory_grad,
        summed[0],
        summed[1],
        summed[2],
        summed[3],
        summed[4],
        summed[5],
        summed[6],
        summed[7],
        summed[8],
        summed[9],
        summed[10],
    )


def dot_nn(left, right):
    return jnp.dot(left, right, preferred_element_type=jnp.float32)


def dot_nt(left, right):
    return lax.dot_general(left, right, (((1,), (1,)), ((), ())), preferred_element_type=jnp.float32)


def dot_tn(left, right):
    return lax.dot_general(left, right, (((0,), (0,)), ((), ())), preferred_element_type=jnp.float32)


def low(values):
    return values.astype(jnp.bfloat16)


def centred(values):
    return values - jnp.mean(values, axis=-1, keepdims=True)


def unit_of(centre):
    scale = lax.rsqrt(jnp.mean(centre * centre, axis=-1, keepdims=True) + EPSILON)
    return centre * scale, scale


def normalize_back(grad, gain, unit, scale):
    inner = grad * gain
    return scale * (
        inner
        - jnp.mean(inner, axis=-1, keepdims=True)
        - unit * jnp.mean(inner * unit, axis=-1, keepdims=True)
    )


DOCUMENTS = 8
TARGET_LENS = range(3, 3 + DOCUMENTS)
SOURCE_LENS = range(3 + DOCUMENTS, 3 + 2 * DOCUMENTS)


def seg_along(place_ref, lens, shape, dim):
    places = lax.broadcasted_iota(jnp.int32, shape, dim)
    seg = jnp.zeros(shape, jnp.int32)
    end = jnp.int32(0)
    for doc in lens:
        end = end + place_ref[doc]
        seg = seg + (places >= end).astype(jnp.int32)
    return seg


def visible_pairs(place_ref, query_lens, key_lens, length, causal):
    query_seg = seg_along(place_ref, query_lens, (length, 1), 0)
    seen = query_seg == seg_along(place_ref, key_lens, (1, length), 1)
    if causal:
        rows = lax.broadcasted_iota(jnp.int32, (length, length), 0)
        cols = lax.broadcasted_iota(jnp.int32, (length, length), 1)
        seen = seen & (cols <= rows)
    return seen


class Far:
    def __init__(self, far_refs, near, sems, parts, inward):
        self.near, self.sems, self.inward, self.waited = near, sems, inward, set()
        self.far_refs, self.parts = far_refs, parts

    def copy(self, part):
        far, near = self.far_refs[0 if len(self.far_refs) == 1 else part], self.near
        if self.parts is not None:
            far_at, near_at = self.parts(part)
            far = far if far_at is None else far.at[far_at]
            near = near if near_at is None else near.at[near_at]
        ends = (far, near) if self.inward else (near, far)
        return pltpu.make_async_copy(*ends, self.sems.at[part])

    def start(self):
        for part in range(self.sems.shape[0]):
            self.copy(part).start()

    def wait(self):
        for part in range(self.sems.shape[0]):
            self.copy(part).wait()

    def get(self):
        if 0 not in self.waited:
            self.waited.add(0)
            self.wait()
        return self.near


TOKEN = (8, 128)
SMALL_COST = 25 * 10**9


def write_token(place_ref):
    lane = lax.broadcasted_iota(jnp.int32, TOKEN, 1)
    token = jnp.zeros(TOKEN, jnp.int32)
    for index in range(3):
        token = jnp.where(lane == index, place_ref[index], token)
    return token


class Chain:
    def __init__(self):
        self.token = None


class Kernel:
    def __init__(self, chain, place, *scalars):
        self.chain = chain
        self.scalars = (place, *scalars)
        self.operands, self.results, self.scratch, self.entries = [], [], [], {}
        self.place = place

    def _scratch(self, what):
        self.scratch.append(what)
        return ("scratch", len(self.scratch) - 1)

    def _operand(self, array, space):
        if space is not pl.ANY:
            array = pltpu.with_memory_space_constraint(array, space)
        self.operands.append((array, space))
        return ("operand", len(self.operands) - 1)

    def _result(self, shape, dtype, space):
        kept = jax.ShapeDtypeStruct(shape, dtype) if space is pl.ANY else space(shape, dtype)
        self.results.append((kept, space))
        return ("result", len(self.results) - 1)

    def near(self, **arrays):
        for name, array in arrays.items():
            self.entries[name] = ("plain", self._operand(array, pltpu.VMEM))

    def far(self, **arrays):
        for name, array in arrays.items():
            ref = self._operand(array, pltpu.HBM)
            near = self._scratch(pltpu.VMEM(array.shape, array.dtype))
            self.entries[name] = ("far", [ref], near, self._scratch(pltpu.SemaphoreType.DMA((1,))), "all", True)

    def halves(self, **pairs):
        for name, (own, other) in pairs.items():
            refs = [self._operand(own, pltpu.HBM), self._operand(other, pl.ANY)]
            near = self._scratch(pltpu.VMEM((2 * own.shape[0], own.shape[1]), own.dtype))
            self.entries[name] = ("far", refs, near, self._scratch(pltpu.SemaphoreType.DMA((2,))), "halves", True)

    def heads(self, name, array, first, last):
        ref = self._operand(array, pltpu.HBM)
        near = self._scratch(pltpu.VMEM((2 * (last - first),) + array.shape[1:], array.dtype))
        sems = self._scratch(pltpu.SemaphoreType.DMA((last - first,)))
        self.entries[name] = ("far", [ref], near, sems, ("heads", first), True)

    def near_out(self, **outs):
        for name, (shape, dtype) in outs.items():
            self.entries[name] = ("plain", self._result(shape, dtype, pltpu.VMEM))

    def free_out(self, **outs):
        for name, (shape, dtype) in outs.items():
            ref = self._result(shape, dtype, pl.ANY)
            near = self._scratch(pltpu.VMEM(shape, dtype))
            self.entries[name] = ("far", [ref], near, self._scratch(pltpu.SemaphoreType.DMA((1,))), "all", False)

    def far_out(self, **outs):
        for name, (shape, dtype) in outs.items():
            ref = self._result(shape, dtype, pltpu.HBM)
            near = self._scratch(pltpu.VMEM(shape, dtype))
            self.entries[name] = ("far", [ref], near, self._scratch(pltpu.SemaphoreType.DMA((1,))), "all", False)

    def heads_out(self, **outs):
        for name, (shape, dtype) in outs.items():
            ref = self._result(shape, dtype, pltpu.HBM)
            near = self._scratch(pltpu.VMEM(shape, dtype))
            sems = self._scratch(pltpu.SemaphoreType.DMA((shape[0] // 2,)))
            self.entries[name] = ("far", [ref], near, sems, ("heads", 0), False)

    def copy_out(self, **outs):
        for name, (source, shape, dtype) in outs.items():
            ref = self._result(shape, dtype, pltpu.HBM)
            near = self.entries[source][1]
            self.entries[name] = ("far", [ref], near, self._scratch(pltpu.SemaphoreType.DMA((1,))), "all", False)

    def prefetch(self, **arrays):
        for name, array in arrays.items():
            ref = self._operand(array, pltpu.HBM)
            near = self._result(array.shape, array.dtype, pltpu.VMEM)
            sems = self._scratch(pltpu.SemaphoreType.DMA((1,)))
            self.entries["prefetch_" + name] = ("far", [ref], near, sems, "all", True)

    def hold(self, **outs):
        for name, (shape, dtype) in outs.items():
            self.entries[name] = ("plain", self._scratch(pltpu.VMEM(shape, dtype)))

    def run(self, body, flops, vmem_mib):
        held = None if self.chain.token is None else self._operand(self.chain.token, pltpu.VMEM)[1]
        last = self._result(TOKEN, jnp.int32, pltpu.VMEM)[1]

        def kernel(*refs):
            count = len(self.scalars)
            bounds = (count, count + len(self.operands), count + len(self.operands) + len(self.results))
            groups = {
                "operand": refs[bounds[0] : bounds[1]],
                "result": refs[bounds[1] : bounds[2]],
                "scratch": refs[bounds[2] :],
            }
            mine = refs[0][0]
            views = types.SimpleNamespace()
            for name, entry in self.entries.items():
                if entry[0] == "plain":
                    setattr(views, name, groups[entry[1][0]][entry[1][1]])
                    continue
                _, far, near, sems, cut, inward = entry
                near = groups[near[0]][near[1]]
                half = near.shape[0] // 2
                parts = None
                if cut == "halves":

                    def parts(part, half=half):
                        place = mine if part == 0 else 1 - mine
                        return (None, pl.ds(pl.multiple_of(place * half, half), half))

                if isinstance(cut, tuple):

                    def parts(part, skip=cut[1]):
                        return (pl.ds((skip + part) * 2, 2), pl.ds(part * 2, 2))

                setattr(views, name, Far([groups[g][i] for g, i in far], near, groups[sems[0]][sems[1]], parts, inward))
            groups["result"][last][...] = write_token(refs[0]) if held is None else groups["operand"][held][...]
            for view in vars(views).values():
                if isinstance(view, Far) and view.inward:
                    view.start()
            body(refs[:count], views)
            for name, view in vars(views).items():
                if isinstance(view, Far) and (not view.inward or name.startswith("prefetch_")):
                    view.get()

        arrays = [array for array, _ in self.operands]
        shapes = [kept for kept, _ in self.results]
        moved = sum(math.prod(a.shape) * a.dtype.itemsize for a in arrays)
        *results, self.chain.token = pl.pallas_call(
            kernel,
            out_shape=shapes,
            in_specs=[pl.BlockSpec(memory_space=pltpu.SMEM)] * len(self.scalars)
            + [pl.BlockSpec(memory_space=space) for _, space in self.operands],
            out_specs=[pl.BlockSpec(memory_space=space) for _, space in self.results],
            scratch_shapes=self.scratch,
            compiler_params=pltpu.CompilerParams(vmem_limit_bytes=vmem_mib * 2**20),
            cost_estimate=pl.CostEstimate(flops=flops, bytes_accessed=moved, transcendentals=0),
        )(*self.scalars, *arrays)
        return results


def ref_of(view):
    return view.get() if isinstance(view, Far) else view


def near_of(view):
    return view.near if isinstance(view, Far) else view


def own_columns(ref, start, width):
    return ref[:, pl.ds(pl.multiple_of(start, 128), width)]


def grad_rows(place_ref, activity_ref, grads, keep_ref, send_ref, col):
    rows = keep_ref.shape[0]
    first = place_ref[0] * 2 * rows
    for ref, part in ((keep_ref, place_ref[1]), (send_ref, 1 - place_ref[1])):
        piece = own_columns(activity_ref, first + part * rows, rows)
        at = col
        for grad in grads:
            ref[:, at : at + grad.shape[1]] = dot_tn(piece, grad).astype(ref.dtype)
            at += grad.shape[1]


def query_blocks(length, causal):
    if causal:
        return ((0, length // 2, length // 2), (length // 2, length, length))
    return ((0, length // 2, length), (length // 2, length, length))


PAIR = 2 * HEAD_DIM


def head_lanes():
    lane = lax.broadcasted_iota(jnp.int32, (1, PAIR), 1)
    return (lane < HEAD_DIM, lane >= HEAD_DIM)


def attend_all(query_ref, key_ref, value_ref, bias_ref, attn, mix_ref, causal):
    length = query_ref.shape[0]

    def one_pair(pair, carry):
        lanes = pl.ds(pl.multiple_of(pair * PAIR, PAIR), PAIR)
        keys, values = key_ref[:, lanes], value_ref[:, lanes]
        zero = jnp.zeros_like(keys)
        for begin, end, reach in query_blocks(length, causal):
            queries = query_ref[begin:end, lanes]
            total = jnp.zeros((end - begin, PAIR), jnp.float32)
            for sub, inside in enumerate(head_lanes()):
                scores = dot_nt(queries, jnp.where(inside, keys, zero)[:reach])
                scores = scores + bias_ref[begin:end, :reach]
                weights = jnp.exp(scores - jnp.max(scores, axis=-1, keepdims=True))
                weights = low(weights * (1.0 / jnp.sum(weights, axis=-1, keepdims=True)))
                attn.near[pair * 2 + sub, begin:end, :reach] = weights
                if reach < length:
                    attn.near[pair * 2 + sub, begin:end, reach:] = jnp.zeros((end - begin, length - reach), weights.dtype)
                total = total + dot_nn(weights, jnp.where(inside, values, zero)[:reach])
            mix_ref[begin:end, lanes] = low(total)
        attn.copy(pair).start()
        return carry

    lax.fori_loop(0, HEADS // 2, one_pair, 0, unroll=True)


def attend_all_back(
    pairs, query_ref, query_t_ref, key_ref, value_ref, attn, mix_ref, grad_ref, grad_t_ref, dquery_ref, dpairs_t_ref, causal
):
    length = query_ref.shape[0]
    width = grad_ref.shape[1]

    def one_pair(pair, carry):
        place = pair - pairs[0]
        lanes = pl.ds(pl.multiple_of(pair * PAIR, PAIR), PAIR)
        near_lanes = pl.ds(pl.multiple_of(place * PAIR, PAIR), PAIR)
        attn.copy(place).wait()
        keys, values = key_ref[:, lanes], value_ref[:, lanes]
        zero = jnp.zeros_like(keys)
        blocks = query_blocks(length, causal)
        dquery = [jnp.zeros((end - begin, PAIR), jnp.float32) for begin, end, _ in blocks]
        for sub, inside in enumerate(head_lanes()):
            head_keys = jnp.where(inside, keys, zero)
            head_values = jnp.where(inside, values, zero)
            rows = pl.ds(pl.multiple_of(place * PAIR + sub * HEAD_DIM, HEAD_DIM), HEAD_DIM)
            parts = []
            for idx, (begin, end, reach) in enumerate(blocks):
                grads = grad_ref[begin:end, near_lanes]
                dots = grads.astype(jnp.float32) * mix_ref[begin:end, lanes].astype(jnp.float32)
                row_dot = jnp.sum(jnp.where(inside, dots, 0.0), axis=-1, keepdims=True)
                weights = attn.near[place * 2 + sub, begin:end, :reach]
                dattn = dot_nt(grads, head_values[:reach])
                dscores = low(weights.astype(jnp.float32) * (dattn - row_dot))
                dquery[idx] = dquery[idx] + dot_nn(dscores, head_keys[:reach])
                dkey_t = dot_nn(query_t_ref[rows, begin:end], dscores)
                dvalue_t = dot_nn(grad_t_ref[rows, begin:end], weights)
                parts.append((reach, dkey_t, dvalue_t))
            (reach, dkey_t, dvalue_t), (_, dkey_more, dvalue_more) = parts
            rows_v = pl.ds(pl.multiple_of(width + place * PAIR + sub * HEAD_DIM, HEAD_DIM), HEAD_DIM)
            for where, less, more in ((rows, dkey_t, dkey_more), (rows_v, dvalue_t, dvalue_more)):
                dpairs_t_ref[where, :reach] = low(less + more[:, :reach])
                if reach < length:
                    dpairs_t_ref[where, reach:] = low(more[:, reach:])
        for (begin, end, _), dq in zip(blocks, dquery):
            dquery_ref[begin:end, near_lanes] = low(dq * HEAD_DIM ** (-0.5))
        return carry

    lax.fori_loop(pairs[0], pairs[1], one_pair, 0)


def scaled_query(values):
    return low(low(values) * jnp.bfloat16(HEAD_DIM ** (-0.5)))


def gain_of(vectors_ref, layer):
    return vectors_ref[layer : layer + 1, :]


def shift_of(vectors_ref, layer):
    return vectors_ref[3 + layer : 4 + layer, :]


def first_body(scalars, views):
    (place_ref,) = scalars
    length = views.self_bias.shape[0]
    own, triple = views.own.get(), views.triple_own
    width = own.shape[1]
    weight_ref = views.prefetch_self_in.near
    views.self_bias[...] = jnp.where(visible_pairs(place_ref, TARGET_LENS, TARGET_LENS, length, True), 0.0, MASKED)
    views.cross_bias[...] = jnp.where(visible_pairs(place_ref, TARGET_LENS, SOURCE_LENS, length, False), 0.0, MASKED)
    views.prefetch_self_in.get()
    triple[:, :width] = scaled_query(dot_nn(own[...], weight_ref[:, :width]))
    triple[:, width:] = low(dot_nn(own[...], weight_ref[:, width:]))


def self_forward_body(scalars, views):
    place_ref, = scalars
    other_ref, weight_ref = views.other, views.self_in
    triple, mix = views.triple, views.mix
    half, width = other_ref.shape
    own_rows, other_rows = rows_at(place_ref[0], half), rows_at(1 - place_ref[0], half)
    triple.near[own_rows, :] = views.triple_own[...]
    triple.near[other_rows, :width] = scaled_query(dot_nn(other_ref[...], weight_ref[:, :width]))
    triple.near[other_rows, width:] = low(dot_nn(other_ref[...], weight_ref[:, width:]))
    triple.start()
    attend_all(
        triple.near.at[:, :width], triple.near.at[:, width : 2 * width], triple.near.at[:, 2 * width :],
        views.bias, views.attn, mix.near, True,
    )
    mix.start()
    centre_ref = views.centre_first
    for rows, part_ref in ((own_rows, views.own), (other_rows, other_ref)):
        summed = part_ref[...].astype(jnp.float32) + dot_nn(mix.near[rows, :], views.self_out[...])
        centre_ref[rows, :] = centred(summed)


def cross_forward_body(scalars, views):
    query, pairs, mix = views.query, views.pairs, views.mix
    width = mix.near.shape[1]
    bias_ref, centre_first_ref, vectors_ref = views.bias, views.centre_first, views.vectors
    views.centre_first_far.start()
    first = unit_of(centre_first_ref[...])[0] * gain_of(vectors_ref, 0) + shift_of(vectors_ref, 0)
    query.near[...] = scaled_query(dot_nn(low(first), views.cross_q[...]))
    query.start()
    pairs.near[...] = low(dot_nn(views.memory.get()[...], views.cross_kv[...]))
    pairs.start()
    attend_all(query.near, pairs.near.at[:, :width], pairs.near.at[:, width:], bias_ref, views.attn, mix.near, False)
    mix.start()
    first = unit_of(centre_first_ref[...])[0] * gain_of(vectors_ref, 0) + shift_of(vectors_ref, 0)
    views.centre_second[...] = centred(first + dot_nn(mix.near[...], views.cross_out[...]))


GELU_SCALE = math.sqrt(2.0 / math.pi)
GELU_CUBE = 0.044715


def gelu_both(values):
    square = values * values
    half = 0.5 * jnp.tanh(values * (GELU_SCALE + (GELU_SCALE * GELU_CUBE) * square)) + 0.5
    rise = values * (2.0 * GELU_SCALE + (6.0 * GELU_SCALE * GELU_CUBE) * square)
    return values * half, half + half * (1.0 - half) * rise


def feed_body(scalars, views):
    (place_ref,) = scalars
    length, width = views.centre_second.shape
    half = length // 2
    second_ref, active_ref, slope_ref = views.second, views.active, views.slope
    outer_ref, inner_ref, work_ref = views.outer, views.inner, views.grad_second
    vectors_ref = views.vectors
    second = unit_of(views.centre_second[...])[0] * gain_of(vectors_ref, 1) + shift_of(vectors_ref, 1)
    second_ref[...] = low(second)
    total = second + vectors_ref[6:7, :]
    in_ref, out_ref = views.ffn_in, views.ffn_out
    hidden = in_ref.shape[1]
    block = width
    for begin in range(0, hidden, block):
        cols = slice(begin, begin + block)
        inner = dot_nn(second_ref[...], in_ref[:, cols]) + vectors_ref[8 + begin // block : 9 + begin // block, :]
        active, slope_ref[:, cols] = gelu_both(inner)
        active_ref[:, cols] = low(active)
        total = total + dot_nn(active_ref[:, cols], out_ref[cols, :])
    unit, scale = unit_of(centred(total))
    work_ref[...] = unit * gain_of(vectors_ref, 2) + shift_of(vectors_ref, 2)
    views.output.near[...] = low(work_ref[pl.ds(pl.multiple_of(place_ref[0] * half, half), half), :])
    views.output.start()
    cotangent = views.cotangent.get()[...].astype(jnp.float32)
    sums_ref, wide_ref = views.sums, views.in_sums
    sums_ref[0:1, :] = jnp.sum(cotangent * unit, axis=0, keepdims=True)
    sums_ref[1:2, :] = jnp.sum(cotangent, axis=0, keepdims=True)
    grad_third = normalize_back(cotangent, gain_of(vectors_ref, 2), unit, scale)
    sums_ref[2:3, :] = jnp.sum(grad_third, axis=0, keepdims=True)
    outer_ref[...] = low(grad_third)
    work_ref[...] = grad_third
    keep, send = views.keep, views.send
    rows = keep.shape[0]
    groups = hidden // width
    for group in range(groups):
        cols = slice(group * width, (group + 1) * width)
        first = (place_ref[0] * groups + group) * 2 * rows
        for view, part in ((keep, place_ref[1]), (send, 1 - place_ref[1])):
            piece = own_columns(active_ref, first + part * rows, rows)
            view[:, cols] = dot_tn(piece, outer_ref[...]).astype(view.dtype)
    into_second = jnp.zeros((length, width), jnp.float32)
    for begin in range(0, hidden, block):
        cols = slice(begin, begin + block)
        grad_inner = dot_nt(outer_ref[...], out_ref[cols, :]) * slope_ref[:, cols]
        wide_ref[:, cols] = jnp.sum(grad_inner, axis=0, keepdims=True)
        inner_ref[:, cols] = low(grad_inner)
        into_second = into_second + dot_nt(inner_ref[:, cols], in_ref[:, cols])
    grad_rows(place_ref, second_ref, (inner_ref[...],), keep, send, hidden)
    work_ref[...] = work_ref[...] + into_second


def between_body(scalars, views):
    (place_ref,) = scalars
    length, width = views.grad.shape
    sums_ref, wide_ref, vectors_ref, small_ref = views.sums, views.in_sums, views.vectors, views.small
    work_ref = views.work
    grad = views.grad[...]
    unit_second, scale_second = unit_of(views.centre_second[...])
    grad_second = normalize_back(grad, gain_of(vectors_ref, 1), unit_second, scale_second)
    views.grad_second[...] = grad_second
    grad_low_ref = views.grad_low
    grad_low_ref[...] = low(grad_second)
    out_ref = views.cross_out
    seen = jnp.where(visible_pairs(place_ref, TARGET_LENS, SOURCE_LENS, length, False), 1.0, 0.0)
    seen = jnp.max(seen, axis=-1, keepdims=True)
    views.dmix[...] = low(dot_nt(grad_low_ref[...], out_ref[...]) * seen)
    views.dmix_t[...] = low(dot_nt(out_ref[...], grad_low_ref[...]))
    views.query_t[...] = views.query[...].T
    work_ref[0:3, :] = sums_ref[0:3, :]
    work_ref[3:4, :] = jnp.sum(grad * unit_second, axis=0, keepdims=True)
    work_ref[4:5, :] = jnp.sum(grad, axis=0, keepdims=True)
    columns = width // 2
    hidden = wide_ref.shape[1]
    small_ref[...] = jnp.zeros(small_ref.shape, jnp.float32)
    for row in range(5):
        small_ref[row : row + 1, :] = own_columns(work_ref.at[row : row + 1, :], place_ref[0] * columns, columns)
    for row in range(hidden // width):
        start = place_ref[0] * (hidden // 2) + row * columns
        small_ref[8 + row : 9 + row, :] = own_columns(wide_ref, start, columns)


def cross_back_body(scalars, views):
    (place_ref,) = scalars
    length, width = views.grad_second.shape
    half = length // 2
    first_ref, grad_ref, dmix_ref, dmix_t_ref = views.first, views.grad, views.dmix, views.dmix_t
    query_t_ref, dquery_ref, dpairs_t_ref = views.query_t, views.dquery, views.dpairs_t
    grad_second_ref = views.grad_second
    query_ref = views.query
    pairs_ref, mix_ref = views.pairs, views.mix
    attend_all_back(
        (0, HEADS // 2), query_ref, query_t_ref, pairs_ref.at[:, :width], pairs_ref.at[:, width:], views.attn, mix_ref,
        dmix_ref, dmix_t_ref, dquery_ref, dpairs_t_ref, False,
    )
    vectors_ref = views.vectors
    unit_first, scale_first = unit_of(views.centre_first.get()[...])
    first_ref[...] = low(unit_first * gain_of(vectors_ref, 0) + shift_of(vectors_ref, 0))
    memory_grad = views.memory_grad
    own_dpairs = own_columns(dpairs_t_ref, place_ref[0] * half, half).T
    memory_grad.near[...] = dot_nt(own_dpairs, views.cross_kv.get()[...])
    memory_grad.start()
    keep, send = views.keep, views.send
    grad_rows(place_ref, first_ref, (dquery_ref[...],), keep, send, 0)
    grad_rows(place_ref, views.memory.get(), (dpairs_t_ref[...].T,), keep, send, width)
    grad_rows(place_ref, mix_ref, (views.grad_low[...],), keep, send, 3 * width)
    grad = grad_second_ref[...] + dot_nt(dquery_ref[...], views.cross_q.get()[...])
    sums_ref, small_ref = views.sums, views.small
    sums_ref[0:1, :] = jnp.sum(grad * unit_first, axis=0, keepdims=True)
    sums_ref[1:2, :] = jnp.sum(grad, axis=0, keepdims=True)
    columns = width // 2
    turned_ref = views.turned
    turned_ref[...] = jnp.zeros(turned_ref.shape, jnp.float32)
    turned_ref[: small_ref.shape[0], :] = small_ref[...]
    for row in range(2):
        turned_ref[5 + row : 6 + row, :] = own_columns(sums_ref.at[row : row + 1, :], place_ref[0] * columns, columns)
    grad_first = normalize_back(grad, gain_of(vectors_ref, 0), unit_first, scale_first)
    views.grad_first[...] = grad_first
    grad_ref[...] = low(grad_first)
    grad_rows(place_ref, views.self_mix.get(), (grad_ref[...],), keep, send, 4 * width)
    rows = keep.shape[0]
    for ref, part in ((keep, place_ref[1]), (send, 1 - place_ref[1])):
        ref[:, 5 * width :] = own_columns(turned_ref, part * rows, rows).T.astype(ref.dtype)


def self_back_body(pairs, scalars, views):
    (place_ref,) = scalars
    length, width = views.grad_first.shape
    half = length // 2
    grad_ref, dmix_ref, dmix_t_ref = views.grad, views.dmix, views.dmix_t
    query_t_ref, dquery_ref, dpairs_t_ref = views.query_t, views.dquery, views.dpairs_t
    first, last = pairs[0] * PAIR, pairs[1] * PAIR
    span = last - first
    grad_ref[...] = low(views.grad_first[...])
    out_ref = views.self_out
    dmix_ref[...] = low(dot_nt(grad_ref[...], out_ref[first:last, :]))
    dmix_t_ref[...] = low(dot_nt(out_ref[first:last, :], grad_ref[...]))
    triple_ref = views.triple
    query_t_ref[...] = triple_ref[:, first:last].T
    attend_all_back(
        pairs, triple_ref.at[:, :width], query_t_ref, triple_ref.at[:, width : 2 * width], triple_ref.at[:, 2 * width :],
        views.attn, views.mix, dmix_ref, dmix_t_ref, dquery_ref, dpairs_t_ref, True,
    )
    own_rows = pl.ds(pl.multiple_of(place_ref[0] * half, half), half)
    own_dpairs = own_columns(dpairs_t_ref, place_ref[0] * half, half).T
    weight_ref = views.self_in.get()
    total = (
        dot_nt(dquery_ref[own_rows, :], weight_ref[:, first:last])
        + dot_nt(own_dpairs[:, :span], weight_ref[:, width + first : width + last])
        + dot_nt(own_dpairs[:, span:], weight_ref[:, 2 * width + first : 2 * width + last])
    )
    total = total + views.grad_first[own_rows, :]
    views.target_grad.near[...] = total
    views.target_grad.start()
    keep, send = views.keep, views.send
    grad_rows(place_ref, ref_of(views.target), (dquery_ref[...], dpairs_t_ref[...].T), keep, send, 0)


def send_wide(values, bit):
    count = lax.axis_size("wide")
    return lax.ppermute(values, "wide", [(i, i ^ (1 << bit)) for i in range(count)])


def bit_of(token_ref, bit):
    return (token_ref[0, 2] >> bit) & 1


def small_kernel(chain, body, arrays, outs):
    token = pltpu.with_memory_space_constraint(chain.token, pltpu.VMEM)

    def kernel(token_ref, *refs):
        *refs, last_ref = refs
        last_ref[...] = token_ref[...]
        body(token_ref, *refs)

    *results, chain.token = pl.pallas_call(
        kernel,
        out_shape=[jax.ShapeDtypeStruct(shape, dtype) for shape, dtype in outs] + [pltpu.VMEM(TOKEN, jnp.int32)],
        in_specs=[pl.BlockSpec(memory_space=pltpu.VMEM)] * (len(arrays) + 1),
        out_specs=[pl.BlockSpec(memory_space=pltpu.VMEM)] * (len(outs) + 1),
        compiler_params=pltpu.CompilerParams(vmem_limit_bytes=12 * 2**20),
        cost_estimate=pl.CostEstimate(flops=SMALL_COST, bytes_accessed=1, transcendentals=0),
    )(token, *arrays)
    return results


def rows_at(start, rows):
    return pl.ds(pl.multiple_of(start * rows, rows), rows)


def add_split(chain, keep, received, bit):
    rows = keep.shape[0] // 2
    shape = (rows,) + keep.shape[1:]

    def body(token_ref, keep_ref, came_ref, mine_ref, send_ref):
        mine = bit_of(token_ref, bit)
        for out, part in ((mine_ref, mine), (send_ref, 1 - mine)):
            where = rows_at(part, rows)
            out[...] = (keep_ref[where, :].astype(jnp.float32) + came_ref[where, :].astype(jnp.float32)).astype(out.dtype)

    outs = [(shape, jnp.float32), (shape, jnp.bfloat16)]
    return small_kernel(chain, body, (keep, received), outs)


def add_low(chain, keep, received):
    def body(token_ref, keep_ref, came_ref, out_ref):
        out_ref[...] = low(keep_ref[...].astype(jnp.float32) + came_ref[...].astype(jnp.float32))

    return small_kernel(chain, body, (keep, received), [(keep.shape, jnp.bfloat16)])[0]


def join_rows(chain, piece, received, bit):
    rows = piece.shape[0]

    def body(token_ref, own_ref, came_ref, out_ref):
        mine = bit_of(token_ref, bit)
        out_ref[rows_at(mine, rows), :] = own_ref[...]
        out_ref[rows_at(1 - mine, rows), :] = came_ref[...]

    shape = (2 * rows,) + piece.shape[1:]
    return small_kernel(chain, body, (piece, received), [(shape, piece.dtype)])[0]


def finish(chain, piece, received, cuts, outs, vectors=None):
    rows = piece.shape[0]

    def body(token_ref, *refs):
        core = token_ref[0, 1]
        for step in range(2):
            part = core ^ step
            for out, row, col, begin, size in cuts:
                where = pl.ds(pl.multiple_of(row + part * rows, rows), rows)
                refs[2 + out][where, col : col + size] = refs[step][:, begin : begin + size].astype(jnp.float32)
        if vectors:
            last = refs[0].shape[1] - 128
            turned = [refs[step][:, last:].astype(jnp.float32).T for step in range(2)]
            swap = core == 1
            turned = jnp.concatenate(
                [jnp.where(swap, turned[1], turned[0]), jnp.where(swap, turned[0], turned[1])], axis=1
            )
            for out, row, col, index in vectors:
                refs[2 + out][row : row + 1, col : col + 2 * rows] = turned[index : index + 1, :]

    return small_kernel(chain, body, (piece, received), outs)


HALVE, WHOLE, DOUBLE = range(3)


def rounds_of(bits):
    return [(HALVE, bit) for bit in bits[:-1]] + [(WHOLE, bits[-1])] + [(DOUBLE, bit) for bit in reversed(bits[:-1])]


class Chunk:
    def __init__(self, chain, keep, send, rounds):
        self.chain = chain
        self.kept, self.send = keep, send
        self.rounds, self.at = rounds, 0
        self.launch()

    def launch(self):
        self.received = send_wide(self.send, self.rounds[self.at][1])

    def advance(self):
        kind, bit = self.rounds[self.at]
        self.at += 1
        following, next_bit = self.rounds[self.at]
        if kind == DOUBLE:
            self.kept = self.send = join_rows(self.chain, self.kept, self.received, bit)
        elif following == HALVE:
            self.kept, self.send = add_split(self.chain, self.kept, self.received, next_bit)
        else:
            self.kept = self.send = add_low(self.chain, self.kept, self.received)
        self.launch()

    def left(self):
        return len(self.rounds) - 1 - self.at

    def finish(self, cuts, outs, vectors=None):
        return finish(self.chain, self.kept, self.received, cuts, outs, vectors)


def near_first(bits):
    return rounds_of(list(range(bits)))


def mid_first(bits):
    return rounds_of([0, 2, 1] + list(range(3, bits)))


def far_first(bits):
    return rounds_of([0] + list(range(2, bits)) + [1])


ORDER = dict(a=near_first, c=near_first, d=near_first)
SCHEDULE = ("a", "aca", "cadcadcdcdadcacdd")


def whole_rows(
    target, memory, target_lens, source_lens, self_in, self_out, cross_q, cross_kv, cross_out, ffn_in, ffn_in_bias,
    ffn_out, ffn_out_bias, norm_gain, norm_bias, cotangent,
):
    f32, bf16 = jnp.float32, jnp.bfloat16
    _, half, width = target.shape
    length = 2 * half
    hidden = ffn_in.shape[1]
    wide = lax.axis_index("wide")
    place = jnp.stack([lax.axis_index("narrow"), wide % 2, wide]).astype(jnp.int32)
    place = jnp.concatenate([place, target_lens[0], source_lens[0]])
    chain = Chain()

    def other_half(values):
        return lax.ppermute(values, "narrow", [(0, 1), (1, 0)])

    own_t, own_m, own_c = target[0], memory[0], cotangent[0]
    other_t, other_m, other_c = other_half(own_t), other_half(own_m), other_half(own_c)
    square = (length, width)
    attn_shape = (HEADS, length, length)
    macs = length * width * width
    rows = width // 4

    vectors = jnp.concatenate(
        [norm_gain, norm_bias, ffn_out_bias[None], jnp.zeros((1, width), f32), ffn_in_bias.reshape(-1, width)], axis=0
    )
    vectors = jnp.pad(vectors, ((0, -vectors.shape[0] % 8), (0, 0)))

    step = Kernel(chain, place)
    step.far(own=own_t)
    step.prefetch(self_in=self_in, self_out=self_out, cross_q=cross_q, cross_kv=cross_kv, cross_out=cross_out, own_t=own_t)
    step.near_out(
        triple_own=((half, 3 * width), bf16), self_bias=((length, length), f32), cross_bias=((length, length), f32)
    )
    (
        self_in_near, self_out_near, cross_q_near, cross_kv_near, cross_out_near, own_near, triple_own, self_bias, cross_bias,
    ) = step.run(first_body, 8 * macs, 12)

    step = Kernel(chain, place)
    step.near(other=other_t)
    step.near(self_in=self_in_near, self_out=self_out_near, own=own_near, triple_own=triple_own, bias=self_bias)
    step.far_out(triple=((length, 3 * width), bf16), mix=(square, bf16))
    step.heads_out(attn=(attn_shape, bf16))
    step.near_out(centre_first=(square, f32))
    triple, self_mix, self_attn, centre_first = step.run(self_forward_body, 24 * macs, 16)

    step = Kernel(chain, place)
    step.halves(memory=(own_m, other_m))
    step.near(centre_first=centre_first, cross_q=cross_q_near, cross_kv=cross_kv_near, cross_out=cross_out_near)
    step.near(vectors=vectors, bias=cross_bias)
    step.copy_out(centre_first_far=("centre_first", square, f32))
    step.far_out(query=(square, bf16), pairs=((length, 2 * width), bf16), mix=(square, bf16))
    step.heads_out(attn=(attn_shape, bf16))
    step.near_out(centre_second=(square, f32))
    step.prefetch(ffn_in=ffn_in, ffn_out=ffn_out)
    (
        centre_first, query, pairs, cross_mix, cross_attn, centre_second, ffn_in_near, ffn_out_near,
    ) = step.run(cross_forward_body, 24 * macs, 16)

    step = Kernel(chain, place)
    step.near(centre_second=centre_second, ffn_in=ffn_in_near, ffn_out=ffn_out_near, vectors=vectors)
    step.halves(cotangent=(own_c, other_c))
    step.far_out(output=((half, width), bf16))
    step.near_out(
        grad_second=(square, f32), sums=((8, width), f32), in_sums=((1, hidden), f32),
        keep=((rows, 2 * hidden), f32), send=((rows, 2 * hidden), bf16),
    )
    step.prefetch(cross_out=cross_out, query=query)
    step.hold(
        second=(square, bf16), active=((length, hidden), bf16), slope=((length, hidden), f32), outer=(square, bf16),
        inner=((length, hidden), bf16),
    )
    output, grad, sums, in_sums, feed_keep, feed_send, cross_out_near, query = step.run(feed_body, 40 * macs, 26)

    bits = lax.axis_size("wide").bit_length() - 1
    orders = {name: ORDER[name](bits) for name in ORDER}
    chunk_a = Chunk(chain, feed_keep, feed_send, orders["a"])
    chunks = dict(a=chunk_a)
    step = Kernel(chain, place)
    step.near(grad=grad, sums=sums, in_sums=in_sums, centre_second=centre_second, cross_out=cross_out_near, query=query)
    step.near(vectors=vectors)
    step.near_out(
        small=((16, half), f32), grad_second=(square, f32), grad_low=(square, bf16), dmix=(square, bf16),
        dmix_t=(square, bf16), query_t=(square, bf16),
    )
    step.prefetch(pairs=pairs, mix=cross_mix)
    step.hold(work=((8, width), f32))
    small, grad_second, grad_low, dmix, dmix_t, query_t, pairs, cross_mix = step.run(between_body, 24 * macs * 4, 8)
    for name in SCHEDULE[0]:
        chunks[name].advance()

    step = Kernel(chain, place)
    step.near(grad_second=grad_second, small=small, vectors=vectors, grad_low=grad_low, dmix=dmix, dmix_t=dmix_t)
    step.near(query_t=query_t, query=query, pairs=pairs, mix=cross_mix)
    step.heads("attn", cross_attn, 0, HEADS // 2)
    step.far(cross_kv=cross_kv)
    step.halves(memory=(own_m, other_m))
    step.far(centre_first=centre_first, cross_q=cross_q, self_mix=self_mix)
    step.far_out(memory_grad=((half, width), f32))
    step.near_out(
        grad_first=(square, f32), keep=((rows, 5 * width + 128), f32), send=((rows, 5 * width + 128), bf16)
    )
    step.prefetch(self_out=self_out, triple=triple, mix=self_mix)
    step.hold(
        first=(square, bf16), grad=(square, bf16), dquery=(square, bf16), dpairs_t=((2 * width, length), bf16), sums=((8, width), f32), turned=((128, half), f32),
    )
    memory_grad, grad_first, cross_keep, cross_send, self_out_near, triple, self_mix = step.run(cross_back_body, 48 * macs * 4, 24)

    chunk_c = chunks["c"] = Chunk(chain, cross_keep, cross_send, orders["c"])
    for name in SCHEDULE[1]:
        chunks[name].advance()

    def self_part(first, last):
        span = (last - first) * PAIR
        step = Kernel(chain, place)
        step.near(grad_first=grad_first)
        step.near(self_out=self_out_near, triple=triple, mix=self_mix)
        step.heads("attn", self_attn, first, last)
        step.halves(target=(own_t, other_t))
        step.far(self_in=self_in)
        step.far_out(target_grad=((half, width), f32))
        step.near_out(keep=((rows, 3 * span), f32), send=((rows, 3 * span), bf16))
        step.hold(
            grad=(square, bf16), dmix=((length, span), bf16), dmix_t=((span, length), bf16),
            query_t=((span, length), bf16), dquery=((length, span), bf16), dpairs_t=((2 * span, length), bf16),
        )
        return step.run(functools.partial(self_back_body, (first, last)), 24 * macs * 12, 16)

    target_grad, keep, send = self_part(0, HEADS // 2)
    chunk_d = chunks["d"] = Chunk(chain, keep, send, orders["d"])
    groups = hidden // width
    endings = dict(
        a=(
            [(0, group * half, 0, group * width, width) for group in range(groups)] + [(1, 0, 0, hidden, hidden)],
            [((groups * half, width), f32), ((half, hidden), f32)],
        ),
        c=(
            [(0, 0, 0, 0, width), (1, 0, 0, width, 2 * width), (2, 0, 0, 3 * width, width), (3, 0, 0, 4 * width, width)],
            [
                ((half, width), f32), ((half, 2 * width), f32), ((half, width), f32), ((half, width), f32),
                ((3, half), f32), ((3, half), f32), ((1, half), f32), ((1, groups * half), f32),
            ],
            [(4, 0, 0, 5), (4, 1, 0, 3), (4, 2, 0, 0), (5, 0, 0, 6), (5, 1, 0, 4), (5, 2, 0, 1), (6, 0, 0, 2)]
            + [(7, 0, row * half, 8 + row) for row in range(groups)],
        ),
        d=([(0, 0, 0, 0, 3 * width)], [((half, 3 * width), f32)]),
    )
    finished = {}
    for name in SCHEDULE[2]:
        if chunks[name].left():
            chunks[name].advance()
        elif name not in finished:
            finished[name] = chunks[name].finish(*endings[name])
    ffn_out_g, ffn_in_g = finished["a"]
    cross_q_g, cross_kv_g, cross_out_g, self_out_g, gain_g, shift_g, out_bias_g, in_bias_g = finished["c"]
    (self_in_g,) = finished["d"]
    return (
        output[None],
        target_grad[None],
        memory_grad[None],
        self_in_g,
        self_out_g,
        cross_q_g,
        cross_kv_g,
        cross_out_g,
        ffn_in_g,
        in_bias_g[0],
        ffn_out_g,
        out_bias_g[0],
        gain_g,
        shift_g,
    )


def fits_whole_rows(mesh, target, lens):
    wide, narrow = mesh.shape["wide"], mesh.shape["narrow"]
    rows, length, width = target.shape
    documents = lens.shape[1]
    return (
        narrow == 2
        and rows == wide
        and wide >= 2
        and wide & (wide - 1) == 0
        and length <= 512
        and documents == DOCUMENTS
        and width == HEADS * HEAD_DIM
        and width % (32 * wide) == 0
    )


def solution(mesh):
    in_specs = (
        P("wide", "narrow", None),
        P("wide", "narrow", None),
        P("wide", None),
        P("wide", None),
        P(),
        P(),
        P(),
        P(),
        P(),
        P(),
        P(),
        P(),
        P(),
        P(),
        P(),
        P("wide", "narrow", None),
    )
    out_specs = (
        P("wide", "narrow", None),
        P("wide", "narrow", None),
        P("wide", "narrow", None),
        P("narrow", None),
        P("narrow", None),
        P("narrow", None),
        P("narrow", None),
        P("narrow", None),
        P("narrow", None),
        P("narrow"),
        P("narrow", None),
        P("narrow"),
        P(None, "narrow"),
        P(None, "narrow"),
    )

    def layer(*arrays):
        body = whole_rows if fits_whole_rows(mesh, arrays[0], arrays[2]) else local
        return jax.shard_map(body, mesh=mesh, in_specs=in_specs, out_specs=out_specs, check_vma=False)(*arrays)

    return layer
```

```python
import functools
import math
import types

import jax
import jax.numpy as jnp
from jax import lax
from jax.experimental import pallas as pl
from jax.experimental.pallas import tpu as pltpu
from jax.sharding import PartitionSpec as P

HEADS = 8
HEAD_DIM = 64


EPSILON = 1e-05
MASKED = -1e30


def segment_ids(doc_lens, length):
    ends = jnp.cumsum(doc_lens, axis=-1)
    places = jnp.arange(length, dtype=jnp.int32)
    return jnp.sum((places[:, None] >= ends[..., None, :]).astype(jnp.int32), axis=-1)


def layer_norm(values, gain, shift):
    centre = values - jnp.mean(values, axis=-1, keepdims=True)
    spread = jnp.mean(centre * centre, axis=-1, keepdims=True)
    return centre * lax.rsqrt(spread + EPSILON) * gain + shift


def gelu_tanh(values):
    return jax.nn.gelu(values, approximate=True)


def project(activity, weight):
    return jnp.einsum("rsd,de->rse", activity, weight, preferred_element_type=jnp.float32)


def project_back(gradient, weight):
    return jnp.einsum("rse,de->rsd", gradient, weight, preferred_element_type=jnp.float32)


def weight_grad(activity, gradient):
    return jnp.einsum("rsd,rse->de", activity, gradient, preferred_element_type=jnp.float32)


def split_heads(values):
    return values.reshape(values.shape[0], values.shape[1], HEADS, HEAD_DIM)


def join_heads(values):
    return values.reshape(values.shape[0], values.shape[1], HEADS * HEAD_DIM)


def block_scores(query_heads, key_heads, query_seg, key_seg, query_pos, key_pos, causal):
    raw_scores = jnp.einsum(
        "rqhd,rkhd->rhqk", query_heads, key_heads, preferred_element_type=jnp.float32
    )
    visible = query_seg[:, :, None] == key_seg[:, None, :]
    if causal:
        visible = visible & (key_pos[None, None, :] <= query_pos[None, :, None])
    return jnp.where(visible[:, None], raw_scores * HEAD_DIM ** (-0.5), MASKED)


def block_backward(query_heads, grad_heads, key_heads, value_heads, scores, log_norm, row_dot):
    attention = jnp.exp(scores - log_norm[..., None])
    grad_attn = jnp.einsum(
        "rqhd,rkhd->rhqk", grad_heads, value_heads, preferred_element_type=jnp.float32
    )
    grad_scores = (attention * (grad_attn - row_dot[..., None]) * HEAD_DIM ** (-0.5)).astype(
        jnp.bfloat16
    )
    grad_query = jnp.einsum(
        "rhqk,rkhd->rqhd", grad_scores, key_heads, preferred_element_type=jnp.float32
    )
    grad_key = jnp.einsum(
        "rhqk,rqhd->rkhd", grad_scores, query_heads, preferred_element_type=jnp.float32
    )
    grad_value = jnp.einsum(
        "rhqk,rqhd->rkhd",
        attention.astype(jnp.bfloat16),
        grad_heads,
        preferred_element_type=jnp.float32,
    )
    return (grad_query, jnp.concatenate([join_heads(grad_key), join_heads(grad_value)], axis=-1))


def make_key_fold(query_heads, query_seg, key_seg_full, query_pos, causal, running, portion):
    run_max, run_sum, stored = running
    span_len = portion.shape[1]
    key_pos = jnp.arange(span_len, dtype=jnp.int32)
    scores = block_scores(
        query_heads,
        split_heads(portion[:, :, : HEADS * HEAD_DIM]),
        query_seg,
        key_seg_full,
        query_pos,
        key_pos,
        causal,
    )
    new_max = jnp.maximum(run_max, jnp.max(scores, axis=-1))
    run_sum = jnp.sum(jnp.exp(scores - new_max[..., None]), axis=-1)
    stored = portion
    return (new_max, run_sum, stored)


def attend_stored(query_heads, stored, query_seg, key_seg_full, query_pos, causal, log_norm):
    total_len = stored.shape[1]
    pair_half = stored.shape[2] // 2
    block_len = math.gcd(total_len, max(query_heads.shape[1], 512))

    def advance(low_sum, block_idx):
        begin_at = block_idx * block_len
        portion = lax.dynamic_slice_in_dim(stored, begin_at, block_len, 1)
        key_seg = lax.dynamic_slice_in_dim(key_seg_full, begin_at, block_len, 1)
        key_pos = begin_at + jnp.arange(block_len, dtype=jnp.int32)
        value_heads = split_heads(portion[:, :, pair_half:])
        scores = block_scores(
            query_heads,
            split_heads(portion[:, :, :pair_half]),
            query_seg,
            key_seg,
            query_pos,
            key_pos,
            causal,
        )
        attention = jnp.exp(scores - log_norm[..., None])
        low_sum = low_sum + jnp.einsum(
            "rhqk,rkhd->rqhd",
            attention.astype(jnp.bfloat16),
            value_heads,
            preferred_element_type=jnp.float32,
        )
        return (low_sum, None)

    zeros_q = jnp.zeros(query_heads.shape, jnp.float32)
    low_sum, _ = lax.scan(advance, zeros_q, jnp.arange(total_len // block_len, dtype=jnp.int32))
    return low_sum


def attend_back_stored(
    query_heads, grad_heads, stored, query_seg, key_seg_full, query_pos, causal, log_norm, row_dot
):
    total_len = stored.shape[1]
    pair_half = stored.shape[2] // 2
    block_len = math.gcd(total_len, max(query_heads.shape[1], 512))

    def advance(block_idx, running):
        grad_query, grad_term = running
        begin_at = block_idx * block_len
        portion = lax.dynamic_slice_in_dim(stored, begin_at, block_len, 1)
        key_seg = lax.dynamic_slice_in_dim(key_seg_full, begin_at, block_len, 1)
        key_pos = begin_at + jnp.arange(block_len, dtype=jnp.int32)
        key_heads = split_heads(portion[:, :, :pair_half])
        value_heads = split_heads(portion[:, :, pair_half:])
        scores = block_scores(
            query_heads, key_heads, query_seg, key_seg, query_pos, key_pos, causal
        )
        block_dq, block_dkv = block_backward(
            query_heads, grad_heads, key_heads, value_heads, scores, log_norm, row_dot
        )
        grad_term = lax.dynamic_update_slice_in_dim(grad_term, block_dkv, begin_at, 1)
        return (grad_query + block_dq, grad_term)

    start_vals = (jnp.zeros(query_heads.shape, jnp.float32), jnp.zeros(stored.shape, jnp.float32))
    grad_query, grad_term = lax.fori_loop(0, total_len // block_len, advance, start_vals)
    return (join_heads(grad_query), grad_term)


def local(
    target,
    memory,
    target_lens,
    source_lens,
    self_in,
    self_out,
    cross_q,
    cross_kv,
    cross_out,
    ffn_in,
    ffn_in_bias,
    ffn_out,
    ffn_out_bias,
    norm_gain,
    norm_bias,
    cotangent,
):
    row_count, shard_len, feat_width = target.shape
    total_len = shard_len * lax.axis_size("narrow")
    own_start = lax.axis_index("narrow") * shard_len
    own_pos = own_start + jnp.arange(shard_len, dtype=jnp.int32)
    target_seg = segment_ids(target_lens, total_len)
    source_seg = segment_ids(source_lens, total_len)
    target_own = lax.dynamic_slice_in_dim(target_seg, own_start, shard_len, 1)
    start_state = (
        jnp.full((row_count, HEADS, shard_len), MASKED, jnp.float32),
        jnp.zeros((row_count, HEADS, shard_len), jnp.float32),
        jnp.zeros((row_count, total_len, 2 * feat_width), jnp.bfloat16),
    )
    triple = project(target, self_in).astype(jnp.bfloat16)
    self_query = split_heads(triple[:, :, :feat_width])
    self_pairs = triple[:, :, feat_width:]
    self_max, self_sum, self_store = make_key_fold(
        self_query,
        target_own,
        target_seg,
        own_pos,
        True,
        start_state,
        lax.all_gather(self_pairs, "narrow", axis=1, tiled=True),
    )
    self_norm = self_max + jnp.log(self_sum)
    self_low = attend_stored(
        self_query, self_store, target_own, target_seg, own_pos, True, self_norm
    )
    self_mix = join_heads(self_low).astype(jnp.bfloat16)
    first, first_pull = jax.vjp(
        layer_norm,
        target.astype(jnp.float32) + project(self_mix, self_out),
        norm_gain[0],
        norm_bias[0],
    )
    first_low = first.astype(jnp.bfloat16)
    cross_query = split_heads(project(first_low, cross_q).astype(jnp.bfloat16))
    cross_pairs = project(memory, cross_kv).astype(jnp.bfloat16)
    cross_max, cross_sum, cross_store = make_key_fold(
        cross_query,
        target_own,
        source_seg,
        own_pos,
        False,
        start_state,
        lax.all_gather(cross_pairs, "narrow", axis=1, tiled=True),
    )
    cross_norm = cross_max + jnp.log(cross_sum)
    cross_low = attend_stored(
        cross_query, cross_store, target_own, source_seg, own_pos, False, cross_norm
    )
    cross_mix = join_heads(cross_low).astype(jnp.bfloat16)
    second, second_pull = jax.vjp(
        layer_norm, first + project(cross_mix, cross_out), norm_gain[1], norm_bias[1]
    )
    second_low = second.astype(jnp.bfloat16)
    inner = project(second_low, ffn_in) + ffn_in_bias
    active, gelu_pull = jax.vjp(gelu_tanh, inner)
    active_low = active.astype(jnp.bfloat16)
    result, third_pull = jax.vjp(
        layer_norm, second + project(active_low, ffn_out) + ffn_out_bias, norm_gain[2], norm_bias[2]
    )
    grad_third, gain_third, shift_third = third_pull(cotangent.astype(jnp.float32))
    grad_outer = grad_third.astype(jnp.bfloat16)
    ffn_out_g = weight_grad(active_low, grad_outer)
    ffn_out_bias_g = jnp.sum(grad_third, axis=(0, 1))
    (grad_active,) = gelu_pull(project_back(grad_outer, ffn_out))
    grad_inner = grad_active.astype(jnp.bfloat16)
    ffn_in_g = weight_grad(second_low, grad_inner)
    ffn_in_bias_g = jnp.sum(grad_active, axis=(0, 1))
    grad_second, gain_second, shift_second = second_pull(
        grad_third + project_back(grad_inner, ffn_in)
    )
    grad_cross = grad_second.astype(jnp.bfloat16)
    cross_out_g = weight_grad(cross_mix, grad_cross)
    cross_dout = split_heads(project_back(grad_cross, cross_out).astype(jnp.bfloat16))
    cross_dot = jnp.swapaxes(jnp.sum(cross_dout.astype(jnp.float32) * cross_low, axis=-1), 1, 2)
    cross_dq, cross_term = attend_back_stored(
        cross_query,
        cross_dout,
        cross_store,
        target_own,
        source_seg,
        own_pos,
        False,
        cross_norm,
        cross_dot,
    )
    cross_dpairs = lax.psum_scatter(
        cross_term.astype(jnp.bfloat16), "narrow", scatter_dimension=1, tiled=True
    )
    cross_dq_low = cross_dq.astype(jnp.bfloat16)
    cross_q_g = weight_grad(first_low, cross_dq_low)
    cross_kv_g = weight_grad(memory, cross_dpairs)
    memory_grad = project_back(cross_dpairs, cross_kv)
    grad_first, gain_first, shift_first = first_pull(
        grad_second + project_back(cross_dq_low, cross_q)
    )
    grad_self = grad_first.astype(jnp.bfloat16)
    self_out_g = weight_grad(self_mix, grad_self)
    self_dout = split_heads(project_back(grad_self, self_out).astype(jnp.bfloat16))
    self_dot = jnp.swapaxes(jnp.sum(self_dout.astype(jnp.float32) * self_low, axis=-1), 1, 2)
    self_dq, self_term = attend_back_stored(
        self_query,
        self_dout,
        self_store,
        target_own,
        target_seg,
        own_pos,
        True,
        self_norm,
        self_dot,
    )
    self_dpairs = lax.psum_scatter(
        self_term.astype(jnp.bfloat16), "narrow", scatter_dimension=1, tiled=True
    ).astype(jnp.float32)
    grad_triple = jnp.concatenate([self_dq, self_dpairs], axis=-1).astype(jnp.bfloat16)
    self_in_g = weight_grad(target, grad_triple)
    target_grad = grad_first + project_back(grad_triple, self_in)
    gain_g = jnp.stack([gain_first, gain_second, gain_third])
    shift_g = jnp.stack([shift_first, shift_second, shift_third])
    sh_a, sh_b, sh_c, sh_d, sh_e, sh_f, sh_g, sh_h, sh_i, sh_j, sh_k = (
        lax.psum_scatter(
            self_in_g.astype(jnp.bfloat16), "narrow", scatter_dimension=0, tiled=True
        ).astype(jnp.float32),
        lax.psum_scatter(
            self_out_g.astype(jnp.bfloat16), "narrow", scatter_dimension=0, tiled=True
        ).astype(jnp.float32),
        lax.psum_scatter(
            cross_q_g.astype(jnp.bfloat16), "narrow", scatter_dimension=0, tiled=True
        ).astype(jnp.float32),
        lax.psum_scatter(
            cross_kv_g.astype(jnp.bfloat16), "narrow", scatter_dimension=0, tiled=True
        ).astype(jnp.float32),
        lax.psum_scatter(
            cross_out_g.astype(jnp.bfloat16), "narrow", scatter_dimension=0, tiled=True
        ).astype(jnp.float32),
        lax.psum_scatter(
            ffn_in_g.astype(jnp.bfloat16), "narrow", scatter_dimension=0, tiled=True
        ).astype(jnp.float32),
        lax.psum_scatter(
            ffn_in_bias_g.astype(jnp.bfloat16), "narrow", scatter_dimension=0, tiled=True
        ).astype(jnp.float32),
        lax.psum_scatter(
            ffn_out_g.astype(jnp.bfloat16), "narrow", scatter_dimension=0, tiled=True
        ).astype(jnp.float32),
        lax.psum_scatter(
            ffn_out_bias_g.astype(jnp.bfloat16), "narrow", scatter_dimension=0, tiled=True
        ).astype(jnp.float32),
        lax.psum_scatter(
            gain_g.astype(jnp.bfloat16), "narrow", scatter_dimension=1, tiled=True
        ).astype(jnp.float32),
        lax.psum_scatter(
            shift_g.astype(jnp.bfloat16), "narrow", scatter_dimension=1, tiled=True
        ).astype(jnp.float32),
    )
    summed = (
        lax.psum(sh_a.astype(jnp.bfloat16), "wide").astype(jnp.float32),
        lax.psum(sh_b.astype(jnp.bfloat16), "wide").astype(jnp.float32),
        lax.psum(sh_c.astype(jnp.bfloat16), "wide").astype(jnp.float32),
        lax.psum(sh_d.astype(jnp.bfloat16), "wide").astype(jnp.float32),
        lax.psum(sh_e.astype(jnp.bfloat16), "wide").astype(jnp.float32),
        lax.psum(sh_f.astype(jnp.bfloat16), "wide").astype(jnp.float32),
        lax.psum(sh_g.astype(jnp.bfloat16), "wide").astype(jnp.float32),
        lax.psum(sh_h.astype(jnp.bfloat16), "wide").astype(jnp.float32),
        lax.psum(sh_i.astype(jnp.bfloat16), "wide").astype(jnp.float32),
        lax.psum(sh_j.astype(jnp.bfloat16), "wide").astype(jnp.float32),
        lax.psum(sh_k.astype(jnp.bfloat16), "wide").astype(jnp.float32),
    )
    return (
        result.astype(jnp.bfloat16),
        target_grad,
        memory_grad,
        summed[0],
        summed[1],
        summed[2],
        summed[3],
        summed[4],
        summed[5],
        summed[6],
        summed[7],
        summed[8],
        summed[9],
        summed[10],
    )


def dot_nn(left, right):
    return jnp.dot(left, right, preferred_element_type=jnp.float32)


def dot_nt(left, right):
    return lax.dot_general(left, right, (((1,), (1,)), ((), ())), preferred_element_type=jnp.float32)


def dot_tn(left, right):
    return lax.dot_general(left, right, (((0,), (0,)), ((), ())), preferred_element_type=jnp.float32)


def low(values):
    return values.astype(jnp.bfloat16)


def centred(values):
    return values - jnp.mean(values, axis=-1, keepdims=True)


def unit_of(centre):
    scale = lax.rsqrt(jnp.mean(centre * centre, axis=-1, keepdims=True) + EPSILON)
    return centre * scale, scale


def normalize_back(grad, gain, unit, scale):
    inner = grad * gain
    return scale * (
        inner
        - jnp.mean(inner, axis=-1, keepdims=True)
        - unit * jnp.mean(inner * unit, axis=-1, keepdims=True)
    )


DOCUMENTS = 8
TARGET_LENS = range(3, 3 + DOCUMENTS)
SOURCE_LENS = range(3 + DOCUMENTS, 3 + 2 * DOCUMENTS)


def seg_along(place_ref, lens, shape, dim):
    places = lax.broadcasted_iota(jnp.int32, shape, dim)
    seg = jnp.zeros(shape, jnp.int32)
    end = jnp.int32(0)
    for doc in lens:
        end = end + place_ref[doc]
        seg = seg + (places >= end).astype(jnp.int32)
    return seg


def visible_pairs(place_ref, query_lens, key_lens, length, causal):
    query_seg = seg_along(place_ref, query_lens, (length, 1), 0)
    seen = query_seg == seg_along(place_ref, key_lens, (1, length), 1)
    if causal:
        rows = lax.broadcasted_iota(jnp.int32, (length, length), 0)
        cols = lax.broadcasted_iota(jnp.int32, (length, length), 1)
        seen = seen & (cols <= rows)
    return seen


class Far:
    def __init__(self, far_refs, near, sems, parts, inward):
        self.near, self.sems, self.inward, self.waited = near, sems, inward, set()
        self.far_refs, self.parts = far_refs, parts

    def copy(self, part):
        far, near = self.far_refs[0 if len(self.far_refs) == 1 else part], self.near
        if self.parts is not None:
            far_at, near_at = self.parts(part)
            far = far if far_at is None else far.at[far_at]
            near = near if near_at is None else near.at[near_at]
        ends = (far, near) if self.inward else (near, far)
        return pltpu.make_async_copy(*ends, self.sems.at[part])

    def start(self):
        for part in range(self.sems.shape[0]):
            self.copy(part).start()

    def wait(self):
        for part in range(self.sems.shape[0]):
            self.copy(part).wait()

    def get(self):
        if 0 not in self.waited:
            self.waited.add(0)
            self.wait()
        return self.near


TOKEN = (8, 128)
SMALL_COST = 25 * 10**9


def write_token(place_ref):
    lane = lax.broadcasted_iota(jnp.int32, TOKEN, 1)
    token = jnp.zeros(TOKEN, jnp.int32)
    for index in range(3):
        token = jnp.where(lane == index, place_ref[index], token)
    return token


class Chain:
    def __init__(self):
        self.token = None


class Kernel:
    def __init__(self, chain, place, *scalars):
        self.chain = chain
        self.scalars = (place, *scalars)
        self.operands, self.results, self.scratch, self.entries = [], [], [], {}
        self.place = place

    def _scratch(self, what):
        self.scratch.append(what)
        return ("scratch", len(self.scratch) - 1)

    def _operand(self, array, space):
        if space is not pl.ANY:
            array = pltpu.with_memory_space_constraint(array, space)
        self.operands.append((array, space))
        return ("operand", len(self.operands) - 1)

    def _result(self, shape, dtype, space):
        kept = jax.ShapeDtypeStruct(shape, dtype) if space is pl.ANY else space(shape, dtype)
        self.results.append((kept, space))
        return ("result", len(self.results) - 1)

    def near(self, **arrays):
        for name, array in arrays.items():
            self.entries[name] = ("plain", self._operand(array, pltpu.VMEM))

    def far(self, **arrays):
        for name, array in arrays.items():
            ref = self._operand(array, pltpu.HBM)
            near = self._scratch(pltpu.VMEM(array.shape, array.dtype))
            self.entries[name] = ("far", [ref], near, self._scratch(pltpu.SemaphoreType.DMA((1,))), "all", True)

    def halves(self, **pairs):
        for name, (own, other) in pairs.items():
            refs = [self._operand(own, pltpu.HBM), self._operand(other, pl.ANY)]
            near = self._scratch(pltpu.VMEM((2 * own.shape[0], own.shape[1]), own.dtype))
            self.entries[name] = ("far", refs, near, self._scratch(pltpu.SemaphoreType.DMA((2,))), "halves", True)

    def heads(self, name, array, first, last):
        ref = self._operand(array, pltpu.HBM)
        near = self._scratch(pltpu.VMEM((2 * (last - first),) + array.shape[1:], array.dtype))
        sems = self._scratch(pltpu.SemaphoreType.DMA((last - first,)))
        self.entries[name] = ("far", [ref], near, sems, ("heads", first), True)

    def near_out(self, **outs):
        for name, (shape, dtype) in outs.items():
            self.entries[name] = ("plain", self._result(shape, dtype, pltpu.VMEM))

    def free_out(self, **outs):
        for name, (shape, dtype) in outs.items():
            ref = self._result(shape, dtype, pl.ANY)
            near = self._scratch(pltpu.VMEM(shape, dtype))
            self.entries[name] = ("far", [ref], near, self._scratch(pltpu.SemaphoreType.DMA((1,))), "all", False)

    def far_out(self, **outs):
        for name, (shape, dtype) in outs.items():
            ref = self._result(shape, dtype, pltpu.HBM)
            near = self._scratch(pltpu.VMEM(shape, dtype))
            self.entries[name] = ("far", [ref], near, self._scratch(pltpu.SemaphoreType.DMA((1,))), "all", False)

    def heads_out(self, **outs):
        for name, (shape, dtype) in outs.items():
            ref = self._result(shape, dtype, pltpu.HBM)
            near = self._scratch(pltpu.VMEM(shape, dtype))
            sems = self._scratch(pltpu.SemaphoreType.DMA((shape[0] // 2,)))
            self.entries[name] = ("far", [ref], near, sems, ("heads", 0), False)

    def copy_out(self, **outs):
        for name, (source, shape, dtype) in outs.items():
            ref = self._result(shape, dtype, pltpu.HBM)
            near = self.entries[source][1]
            self.entries[name] = ("far", [ref], near, self._scratch(pltpu.SemaphoreType.DMA((1,))), "all", False)

    def prefetch(self, **arrays):
        for name, array in arrays.items():
            ref = self._operand(array, pltpu.HBM)
            near = self._result(array.shape, array.dtype, pltpu.VMEM)
            sems = self._scratch(pltpu.SemaphoreType.DMA((1,)))
            self.entries["prefetch_" + name] = ("far", [ref], near, sems, "all", True)

    def hold(self, **outs):
        for name, (shape, dtype) in outs.items():
            self.entries[name] = ("plain", self._scratch(pltpu.VMEM(shape, dtype)))

    def run(self, body, flops, vmem_mib):
        held = None if self.chain.token is None else self._operand(self.chain.token, pltpu.VMEM)[1]
        last = self._result(TOKEN, jnp.int32, pltpu.VMEM)[1]

        def kernel(*refs):
            count = len(self.scalars)
            bounds = (count, count + len(self.operands), count + len(self.operands) + len(self.results))
            groups = {
                "operand": refs[bounds[0] : bounds[1]],
                "result": refs[bounds[1] : bounds[2]],
                "scratch": refs[bounds[2] :],
            }
            mine = refs[0][0]
            views = types.SimpleNamespace()
            for name, entry in self.entries.items():
                if entry[0] == "plain":
                    setattr(views, name, groups[entry[1][0]][entry[1][1]])
                    continue
                _, far, near, sems, cut, inward = entry
                near = groups[near[0]][near[1]]
                half = near.shape[0] // 2
                parts = None
                if cut == "halves":

                    def parts(part, half=half):
                        place = mine if part == 0 else 1 - mine
                        return (None, pl.ds(pl.multiple_of(place * half, half), half))

                if isinstance(cut, tuple):

                    def parts(part, skip=cut[1]):
                        return (pl.ds((skip + part) * 2, 2), pl.ds(part * 2, 2))

                setattr(views, name, Far([groups[g][i] for g, i in far], near, groups[sems[0]][sems[1]], parts, inward))
            groups["result"][last][...] = write_token(refs[0]) if held is None else groups["operand"][held][...]
            for view in vars(views).values():
                if isinstance(view, Far) and view.inward:
                    view.start()
            body(refs[:count], views)
            for name, view in vars(views).items():
                if isinstance(view, Far) and (not view.inward or name.startswith("prefetch_")):
                    view.get()

        arrays = [array for array, _ in self.operands]
        shapes = [kept for kept, _ in self.results]
        moved = sum(math.prod(a.shape) * a.dtype.itemsize for a in arrays)
        *results, self.chain.token = pl.pallas_call(
            kernel,
            out_shape=shapes,
            in_specs=[pl.BlockSpec(memory_space=pltpu.SMEM)] * len(self.scalars)
            + [pl.BlockSpec(memory_space=space) for _, space in self.operands],
            out_specs=[pl.BlockSpec(memory_space=space) for _, space in self.results],
            scratch_shapes=self.scratch,
            compiler_params=pltpu.CompilerParams(vmem_limit_bytes=vmem_mib * 2**20),
            cost_estimate=pl.CostEstimate(flops=flops, bytes_accessed=moved, transcendentals=0),
        )(*self.scalars, *arrays)
        return results


def ref_of(view):
    return view.get() if isinstance(view, Far) else view


def near_of(view):
    return view.near if isinstance(view, Far) else view


def own_columns(ref, start, width):
    return ref[:, pl.ds(pl.multiple_of(start, 128), width)]


def grad_rows(place_ref, activity_ref, grads, keep_ref, send_ref, col):
    rows = keep_ref.shape[0]
    first = place_ref[0] * 2 * rows
    for ref, part in ((keep_ref, place_ref[1]), (send_ref, 1 - place_ref[1])):
        piece = own_columns(activity_ref, first + part * rows, rows)
        at = col
        for grad in grads:
            ref[:, at : at + grad.shape[1]] = dot_tn(piece, grad).astype(ref.dtype)
            at += grad.shape[1]


def query_blocks(length, causal):
    if causal:
        return ((0, length // 2, length // 2), (length // 2, length, length))
    return ((0, length // 2, length), (length // 2, length, length))


PAIR = 2 * HEAD_DIM


def head_lanes():
    lane = lax.broadcasted_iota(jnp.int32, (1, PAIR), 1)
    return (lane < HEAD_DIM, lane >= HEAD_DIM)


SPAN = 32


def attend_all(query_ref, key_ref, value_ref, bias_ref, attn, mix_ref, work_ref, causal):
    length = query_ref.shape[0]

    def one_pair(pair, carry):
        lanes = pl.ds(pl.multiple_of(pair * PAIR, PAIR), PAIR)
        keys, values = key_ref[:, lanes], value_ref[:, lanes]
        zero = jnp.zeros_like(keys)
        total = jnp.zeros((length, PAIR), jnp.float32)
        for sub, inside in enumerate(head_lanes()):
            work_ref[sub] = dot_nt(query_ref[:, lanes], jnp.where(inside, keys, zero))
            for begin in range(0, length, SPAN):
                rows = slice(begin, begin + SPAN)
                reach = length // 2 if causal and begin + SPAN <= length // 2 else length
                scores = work_ref[sub, rows, :reach] + bias_ref[rows, :reach]
                weights = jnp.exp(scores - jnp.max(scores, axis=-1, keepdims=True))
                weights = low(weights * (1.0 / jnp.sum(weights, axis=-1, keepdims=True)))
                attn.near[pair * 2 + sub, rows, :reach] = weights
                if reach < length:
                    attn.near[pair * 2 + sub, rows, reach:] = jnp.zeros((SPAN, length - reach), weights.dtype)
            total = total + dot_nn(attn.near[pair * 2 + sub], jnp.where(inside, values, zero))
        mix_ref[:, lanes] = low(total)
        attn.copy(pair).start()
        return carry

    lax.fori_loop(0, HEADS // 2, one_pair, 0, unroll=True)


def attend_whole_back(
    query_ref, query_t_ref, key_ref, value_ref, attn, mix_ref, grad_ref, grad_t_ref, dquery_ref, dpairs_t_ref,
    work_ref, dscores_ref,
):
    length, width = query_ref.shape

    def one_pair(pair, carry):
        lanes = pl.ds(pl.multiple_of(pair * PAIR, PAIR), PAIR)
        attn.copy(pair).wait()
        keys, values = key_ref[:, lanes], value_ref[:, lanes]
        zero = jnp.zeros_like(keys)
        dquery = jnp.zeros((length, PAIR), jnp.float32)
        dots = grad_ref[:, lanes].astype(jnp.float32) * mix_ref[:, lanes].astype(jnp.float32)
        for sub, inside in enumerate(head_lanes()):
            row_dot = jnp.sum(jnp.where(inside, dots, 0.0), axis=-1, keepdims=True)
            work_ref[sub] = dot_nt(grad_ref[:, lanes], jnp.where(inside, values, zero))
            for begin in range(0, length, SPAN):
                rows = slice(begin, begin + SPAN)
                weights = attn.near[pair * 2 + sub, rows, :].astype(jnp.float32)
                dscores_ref[sub, rows, :] = low(weights * (work_ref[sub, rows, :] - row_dot[rows]))
            dquery = dquery + dot_nn(dscores_ref[sub], jnp.where(inside, keys, zero))
            first = pair * PAIR + sub * HEAD_DIM
            rows = pl.ds(pl.multiple_of(first, HEAD_DIM), HEAD_DIM)
            dpairs_t_ref[rows, :] = low(dot_nn(query_t_ref[rows, :], dscores_ref[sub]))
            where = pl.ds(pl.multiple_of(width + first, HEAD_DIM), HEAD_DIM)
            dpairs_t_ref[where, :] = low(dot_nn(grad_t_ref[rows, :], attn.near[pair * 2 + sub]))
        dquery_ref[:, lanes] = low(dquery * HEAD_DIM ** (-0.5))
        return carry

    lax.fori_loop(0, HEADS // 2, one_pair, 0)


def attend_all_back(
    pairs, query_ref, query_t_ref, key_ref, value_ref, attn, mix_ref, grad_ref, grad_t_ref, dquery_ref, dpairs_t_ref, causal
):
    length = query_ref.shape[0]
    width = grad_ref.shape[1]

    def one_pair(pair, carry):
        place = pair - pairs[0]
        lanes = pl.ds(pl.multiple_of(pair * PAIR, PAIR), PAIR)
        near_lanes = pl.ds(pl.multiple_of(place * PAIR, PAIR), PAIR)
        attn.copy(place).wait()
        keys, values = key_ref[:, lanes], value_ref[:, lanes]
        zero = jnp.zeros_like(keys)
        blocks = query_blocks(length, causal)
        dquery = [jnp.zeros((end - begin, PAIR), jnp.float32) for begin, end, _ in blocks]
        for sub, inside in enumerate(head_lanes()):
            head_keys = jnp.where(inside, keys, zero)
            head_values = jnp.where(inside, values, zero)
            rows = pl.ds(pl.multiple_of(place * PAIR + sub * HEAD_DIM, HEAD_DIM), HEAD_DIM)
            parts = []
            for idx, (begin, end, reach) in enumerate(blocks):
                grads = grad_ref[begin:end, near_lanes]
                dots = grads.astype(jnp.float32) * mix_ref[begin:end, lanes].astype(jnp.float32)
                row_dot = jnp.sum(jnp.where(inside, dots, 0.0), axis=-1, keepdims=True)
                weights = attn.near[place * 2 + sub, begin:end, :reach]
                dattn = dot_nt(grads, head_values[:reach])
                dscores = low(weights.astype(jnp.float32) * (dattn - row_dot))
                dquery[idx] = dquery[idx] + dot_nn(dscores, head_keys[:reach])
                dkey_t = dot_nn(query_t_ref[rows, begin:end], dscores)
                dvalue_t = dot_nn(grad_t_ref[rows, begin:end], weights)
                parts.append((reach, dkey_t, dvalue_t))
            (reach, dkey_t, dvalue_t), (_, dkey_more, dvalue_more) = parts
            rows_v = pl.ds(pl.multiple_of(width + place * PAIR + sub * HEAD_DIM, HEAD_DIM), HEAD_DIM)
            for where, less, more in ((rows, dkey_t, dkey_more), (rows_v, dvalue_t, dvalue_more)):
                dpairs_t_ref[where, :reach] = low(less + more[:, :reach])
                if reach < length:
                    dpairs_t_ref[where, reach:] = low(more[:, reach:])
        for (begin, end, _), dq in zip(blocks, dquery):
            dquery_ref[begin:end, near_lanes] = low(dq * HEAD_DIM ** (-0.5))
        return carry

    lax.fori_loop(pairs[0], pairs[1], one_pair, 0)


def scaled_query(values):
    return low(low(values) * jnp.bfloat16(HEAD_DIM ** (-0.5)))


def gain_of(vectors_ref, layer):
    return vectors_ref[layer : layer + 1, :]


def shift_of(vectors_ref, layer):
    return vectors_ref[3 + layer : 4 + layer, :]


def first_body(scalars, views):
    (place_ref,) = scalars
    length = views.self_bias.shape[0]
    own, triple = views.own.get(), views.triple_own
    width = own.shape[1]
    weight_ref = views.prefetch_self_in.near
    views.self_bias[...] = jnp.where(visible_pairs(place_ref, TARGET_LENS, TARGET_LENS, length, True), 0.0, MASKED)
    views.cross_bias[...] = jnp.where(visible_pairs(place_ref, TARGET_LENS, SOURCE_LENS, length, False), 0.0, MASKED)
    views.prefetch_self_in.get()
    triple[:, :width] = scaled_query(dot_nn(own[...], weight_ref[:, :width]))
    triple[:, width:] = low(dot_nn(own[...], weight_ref[:, width:]))


def self_forward_body(scalars, views):
    place_ref, = scalars
    other_ref, weight_ref = views.other, views.self_in
    triple, mix = views.triple, views.mix
    half, width = other_ref.shape
    own_rows, other_rows = rows_at(place_ref[0], half), rows_at(1 - place_ref[0], half)
    triple.near[own_rows, :] = views.triple_own[...]
    triple.near[other_rows, :width] = scaled_query(dot_nn(other_ref[...], weight_ref[:, :width]))
    triple.near[other_rows, width:] = low(dot_nn(other_ref[...], weight_ref[:, width:]))
    triple.start()
    attend_all(
        triple.near.at[:, :width], triple.near.at[:, width : 2 * width], triple.near.at[:, 2 * width :],
        views.bias, views.attn, mix.near, views.work, True,
    )
    mix.start()
    centre_ref = views.centre_first
    for rows, part_ref in ((own_rows, views.own), (other_rows, other_ref)):
        summed = part_ref[...].astype(jnp.float32) + dot_nn(mix.near[rows, :], views.self_out[...])
        centre_ref[rows, :] = centred(summed)


def cross_forward_body(scalars, views):
    query, pairs, mix = views.query, views.pairs, views.mix
    width = mix.near.shape[1]
    bias_ref, centre_first_ref, vectors_ref = views.bias, views.centre_first, views.vectors
    views.centre_first_far.start()
    first = unit_of(centre_first_ref[...])[0] * gain_of(vectors_ref, 0) + shift_of(vectors_ref, 0)
    query.near[...] = scaled_query(dot_nn(low(first), views.cross_q[...]))
    query.start()
    pairs.near[...] = low(dot_nn(views.memory.get()[...], views.cross_kv[...]))
    pairs.start()
    attend_all(
        query.near, pairs.near.at[:, :width], pairs.near.at[:, width:], bias_ref, views.attn, mix.near, views.work, False
    )
    mix.start()
    first = unit_of(centre_first_ref[...])[0] * gain_of(vectors_ref, 0) + shift_of(vectors_ref, 0)
    views.centre_second[...] = centred(first + dot_nn(mix.near[...], views.cross_out[...]))


GELU_SCALE = math.sqrt(2.0 / math.pi)
GELU_CUBE = 0.044715


def gelu_both(values):
    square = values * values
    half = 0.5 * jnp.tanh(values * (GELU_SCALE + (GELU_SCALE * GELU_CUBE) * square)) + 0.5
    rise = values * (2.0 * GELU_SCALE + (6.0 * GELU_SCALE * GELU_CUBE) * square)
    return values * half, half + half * (1.0 - half) * rise


def feed_body(scalars, views):
    (place_ref,) = scalars
    length, width = views.centre_second.shape
    half = length // 2
    second_ref, active_ref, slope_ref = views.second, views.active, views.slope
    outer_ref, inner_ref, work_ref = views.outer, views.inner, views.grad_second
    vectors_ref = views.vectors
    second = unit_of(views.centre_second[...])[0] * gain_of(vectors_ref, 1) + shift_of(vectors_ref, 1)
    second_ref[...] = low(second)
    total = second + vectors_ref[6:7, :]
    in_ref, out_ref = views.ffn_in, views.ffn_out
    hidden = in_ref.shape[1]
    block = width
    for begin in range(0, hidden, block):
        cols = slice(begin, begin + block)
        inner = dot_nn(second_ref[...], in_ref[:, cols]) + vectors_ref[8 + begin // block : 9 + begin // block, :]
        active, slope_ref[:, cols] = gelu_both(inner)
        active_ref[:, cols] = low(active)
        total = total + dot_nn(active_ref[:, cols], out_ref[cols, :])
    unit, scale = unit_of(centred(total))
    work_ref[...] = unit * gain_of(vectors_ref, 2) + shift_of(vectors_ref, 2)
    views.output.near[...] = low(work_ref[pl.ds(pl.multiple_of(place_ref[0] * half, half), half), :])
    views.output.start()
    cotangent = views.cotangent.get()[...].astype(jnp.float32)
    sums_ref, wide_ref = views.sums, views.in_sums
    sums_ref[0:1, :] = jnp.sum(cotangent * unit, axis=0, keepdims=True)
    sums_ref[1:2, :] = jnp.sum(cotangent, axis=0, keepdims=True)
    grad_third = normalize_back(cotangent, gain_of(vectors_ref, 2), unit, scale)
    sums_ref[2:3, :] = jnp.sum(grad_third, axis=0, keepdims=True)
    outer_ref[...] = low(grad_third)
    work_ref[...] = grad_third
    keep, send = views.keep, views.send
    rows = keep.shape[0]
    groups = hidden // width
    for group in range(groups):
        cols = slice(group * width, (group + 1) * width)
        first = (place_ref[0] * groups + group) * 2 * rows
        for view, part in ((keep, place_ref[1]), (send, 1 - place_ref[1])):
            piece = own_columns(active_ref, first + part * rows, rows)
            view[:, cols] = dot_tn(piece, outer_ref[...]).astype(view.dtype)
    into_second = jnp.zeros((length, width), jnp.float32)
    for begin in range(0, hidden, block):
        cols = slice(begin, begin + block)
        grad_inner = dot_nt(outer_ref[...], out_ref[cols, :]) * slope_ref[:, cols]
        wide_ref[:, cols] = jnp.sum(grad_inner, axis=0, keepdims=True)
        inner_ref[:, cols] = low(grad_inner)
        into_second = into_second + dot_nt(inner_ref[:, cols], in_ref[:, cols])
    grad_rows(place_ref, second_ref, (inner_ref[...],), keep, send, hidden)
    work_ref[...] = work_ref[...] + into_second


def between_body(scalars, views):
    (place_ref,) = scalars
    length, width = views.grad.shape
    sums_ref, wide_ref, vectors_ref, small_ref = views.sums, views.in_sums, views.vectors, views.small
    work_ref = views.work
    grad = views.grad[...]
    unit_second, scale_second = unit_of(views.centre_second[...])
    grad_second = normalize_back(grad, gain_of(vectors_ref, 1), unit_second, scale_second)
    views.grad_second[...] = grad_second
    grad_low_ref = views.grad_low
    grad_low_ref[...] = low(grad_second)
    out_ref = views.cross_out
    seen = jnp.where(visible_pairs(place_ref, TARGET_LENS, SOURCE_LENS, length, False), 1.0, 0.0)
    seen = jnp.max(seen, axis=-1, keepdims=True)
    views.dmix[...] = low(dot_nt(grad_low_ref[...], out_ref[...]) * seen)
    views.dmix_t[...] = low(dot_nt(out_ref[...], grad_low_ref[...]))
    views.query_t[...] = views.query[...].T
    work_ref[0:3, :] = sums_ref[0:3, :]
    work_ref[3:4, :] = jnp.sum(grad * unit_second, axis=0, keepdims=True)
    work_ref[4:5, :] = jnp.sum(grad, axis=0, keepdims=True)
    columns = width // 2
    hidden = wide_ref.shape[1]
    small_ref[...] = jnp.zeros(small_ref.shape, jnp.float32)
    for row in range(5):
        small_ref[row : row + 1, :] = own_columns(work_ref.at[row : row + 1, :], place_ref[0] * columns, columns)
    for row in range(hidden // width):
        start = place_ref[0] * (hidden // 2) + row * columns
        small_ref[8 + row : 9 + row, :] = own_columns(wide_ref, start, columns)


def cross_back_body(scalars, views):
    (place_ref,) = scalars
    length, width = views.grad_second.shape
    half = length // 2
    first_ref, grad_ref, dmix_ref, dmix_t_ref = views.first, views.grad, views.dmix, views.dmix_t
    query_t_ref, dquery_ref, dpairs_t_ref = views.query_t, views.dquery, views.dpairs_t
    grad_second_ref = views.grad_second
    query_ref = views.query
    pairs_ref, mix_ref = views.pairs, views.mix
    attend_whole_back(
        query_ref, query_t_ref, pairs_ref.at[:, :width], pairs_ref.at[:, width:], views.attn, mix_ref,
        dmix_ref, dmix_t_ref, dquery_ref, dpairs_t_ref, views.work, views.dscores,
    )
    vectors_ref = views.vectors
    unit_first, scale_first = unit_of(views.centre_first.get()[...])
    first_ref[...] = low(unit_first * gain_of(vectors_ref, 0) + shift_of(vectors_ref, 0))
    memory_grad = views.memory_grad
    own_dpairs = own_columns(dpairs_t_ref, place_ref[0] * half, half).T
    memory_grad.near[...] = dot_nt(own_dpairs, views.cross_kv.get()[...])
    memory_grad.start()
    keep, send = views.keep, views.send
    grad_rows(place_ref, first_ref, (dquery_ref[...],), keep, send, 0)
    grad_rows(place_ref, views.memory.get(), (dpairs_t_ref[...].T,), keep, send, width)
    grad_rows(place_ref, mix_ref, (views.grad_low[...],), keep, send, 3 * width)
    grad = grad_second_ref[...] + dot_nt(dquery_ref[...], views.cross_q.get()[...])
    sums_ref, small_ref = views.sums, views.small
    sums_ref[0:1, :] = jnp.sum(grad * unit_first, axis=0, keepdims=True)
    sums_ref[1:2, :] = jnp.sum(grad, axis=0, keepdims=True)
    columns = width // 2
    turned_ref = views.turned
    turned_ref[...] = jnp.zeros(turned_ref.shape, jnp.float32)
    turned_ref[: small_ref.shape[0], :] = small_ref[...]
    for row in range(2):
        turned_ref[5 + row : 6 + row, :] = own_columns(sums_ref.at[row : row + 1, :], place_ref[0] * columns, columns)
    grad_first = normalize_back(grad, gain_of(vectors_ref, 0), unit_first, scale_first)
    views.grad_first[...] = grad_first
    grad_ref[...] = low(grad_first)
    grad_rows(place_ref, views.self_mix.get(), (grad_ref[...],), keep, send, 4 * width)
    rows = keep.shape[0]
    for ref, part in ((keep, place_ref[1]), (send, 1 - place_ref[1])):
        ref[:, 5 * width :] = own_columns(turned_ref, part * rows, rows).T.astype(ref.dtype)


def self_back_body(pairs, scalars, views):
    (place_ref,) = scalars
    length, width = views.grad_first.shape
    half = length // 2
    grad_ref, dmix_ref, dmix_t_ref = views.grad, views.dmix, views.dmix_t
    query_t_ref, dquery_ref, dpairs_t_ref = views.query_t, views.dquery, views.dpairs_t
    first, last = pairs[0] * PAIR, pairs[1] * PAIR
    span = last - first
    grad_ref[...] = low(views.grad_first[...])
    out_ref = views.self_out
    dmix_ref[...] = low(dot_nt(grad_ref[...], out_ref[first:last, :]))
    dmix_t_ref[...] = low(dot_nt(out_ref[first:last, :], grad_ref[...]))
    triple_ref = views.triple
    query_t_ref[...] = triple_ref[:, first:last].T
    attend_all_back(
        pairs, triple_ref.at[:, :width], query_t_ref, triple_ref.at[:, width : 2 * width], triple_ref.at[:, 2 * width :],
        views.attn, views.mix, dmix_ref, dmix_t_ref, dquery_ref, dpairs_t_ref, True,
    )
    own_rows = pl.ds(pl.multiple_of(place_ref[0] * half, half), half)
    own_dpairs = own_columns(dpairs_t_ref, place_ref[0] * half, half).T
    weight_ref = views.self_in.get()
    total = (
        dot_nt(dquery_ref[own_rows, :], weight_ref[:, first:last])
        + dot_nt(own_dpairs[:, :span], weight_ref[:, width + first : width + last])
        + dot_nt(own_dpairs[:, span:], weight_ref[:, 2 * width + first : 2 * width + last])
    )
    total = total + views.grad_first[own_rows, :]
    views.target_grad.near[...] = total
    views.target_grad.start()
    keep, send = views.keep, views.send
    grad_rows(place_ref, ref_of(views.target), (dquery_ref[...], dpairs_t_ref[...].T), keep, send, 0)


def send_wide(values, bit):
    count = lax.axis_size("wide")
    return lax.ppermute(values, "wide", [(i, i ^ (1 << bit)) for i in range(count)])


def bit_of(token_ref, bit):
    return (token_ref[0, 2] >> bit) & 1


def small_kernel(chain, body, arrays, outs):
    token = pltpu.with_memory_space_constraint(chain.token, pltpu.VMEM)

    def kernel(token_ref, *refs):
        *refs, last_ref = refs
        last_ref[...] = token_ref[...]
        body(token_ref, *refs)

    *results, chain.token = pl.pallas_call(
        kernel,
        out_shape=[jax.ShapeDtypeStruct(shape, dtype) for shape, dtype in outs] + [pltpu.VMEM(TOKEN, jnp.int32)],
        in_specs=[pl.BlockSpec(memory_space=pltpu.VMEM)] * (len(arrays) + 1),
        out_specs=[pl.BlockSpec(memory_space=pltpu.VMEM)] * (len(outs) + 1),
        compiler_params=pltpu.CompilerParams(vmem_limit_bytes=12 * 2**20),
        cost_estimate=pl.CostEstimate(flops=SMALL_COST, bytes_accessed=1, transcendentals=0),
    )(token, *arrays)
    return results


def rows_at(start, rows):
    return pl.ds(pl.multiple_of(start * rows, rows), rows)


def add_split(chain, keep, received, bit):
    rows = keep.shape[0] // 2
    shape = (rows,) + keep.shape[1:]

    def body(token_ref, keep_ref, came_ref, mine_ref, send_ref):
        mine = bit_of(token_ref, bit)
        for out, part in ((mine_ref, mine), (send_ref, 1 - mine)):
            where = rows_at(part, rows)
            out[...] = (keep_ref[where, :].astype(jnp.float32) + came_ref[where, :].astype(jnp.float32)).astype(out.dtype)

    outs = [(shape, jnp.float32), (shape, jnp.bfloat16)]
    return small_kernel(chain, body, (keep, received), outs)


def add_low(chain, keep, received):
    def body(token_ref, keep_ref, came_ref, out_ref):
        out_ref[...] = low(keep_ref[...].astype(jnp.float32) + came_ref[...].astype(jnp.float32))

    return small_kernel(chain, body, (keep, received), [(keep.shape, jnp.bfloat16)])[0]


def join_rows(chain, piece, received, bit):
    rows = piece.shape[0]

    def body(token_ref, own_ref, came_ref, out_ref):
        mine = bit_of(token_ref, bit)
        out_ref[rows_at(mine, rows), :] = own_ref[...]
        out_ref[rows_at(1 - mine, rows), :] = came_ref[...]

    shape = (2 * rows,) + piece.shape[1:]
    return small_kernel(chain, body, (piece, received), [(shape, piece.dtype)])[0]


def finish(chain, piece, received, cuts, outs, vectors=None):
    rows = piece.shape[0]

    def body(token_ref, *refs):
        core = token_ref[0, 1]
        for step in range(2):
            part = core ^ step
            for out, row, col, begin, size in cuts:
                where = pl.ds(pl.multiple_of(row + part * rows, rows), rows)
                refs[2 + out][where, col : col + size] = refs[step][:, begin : begin + size].astype(jnp.float32)
        if vectors:
            last = refs[0].shape[1] - 128
            turned = [refs[step][:, last:].astype(jnp.float32).T for step in range(2)]
            swap = core == 1
            turned = jnp.concatenate(
                [jnp.where(swap, turned[1], turned[0]), jnp.where(swap, turned[0], turned[1])], axis=1
            )
            for out, row, col, index in vectors:
                refs[2 + out][row : row + 1, col : col + 2 * rows] = turned[index : index + 1, :]

    return small_kernel(chain, body, (piece, received), outs)


HALVE, WHOLE, DOUBLE = range(3)


def rounds_of(bits):
    return [(HALVE, bit) for bit in bits[:-1]] + [(WHOLE, bits[-1])] + [(DOUBLE, bit) for bit in reversed(bits[:-1])]


class Chunk:
    def __init__(self, chain, keep, send, rounds):
        self.chain = chain
        self.kept, self.send = keep, send
        self.rounds, self.at = rounds, 0
        self.launch()

    def launch(self):
        self.received = send_wide(self.send, self.rounds[self.at][1])

    def advance(self):
        kind, bit = self.rounds[self.at]
        self.at += 1
        following, next_bit = self.rounds[self.at]
        if kind == DOUBLE:
            self.kept = self.send = join_rows(self.chain, self.kept, self.received, bit)
        elif following == HALVE:
            self.kept, self.send = add_split(self.chain, self.kept, self.received, next_bit)
        else:
            self.kept = self.send = add_low(self.chain, self.kept, self.received)
        self.launch()

    def left(self):
        return len(self.rounds) - 1 - self.at

    def finish(self, cuts, outs, vectors=None):
        return finish(self.chain, self.kept, self.received, cuts, outs, vectors)


def near_first(bits):
    return rounds_of(list(range(bits)))


def mid_first(bits):
    return rounds_of([0, 2, 1] + list(range(3, bits)))


def far_first(bits):
    return rounds_of([0] + list(range(2, bits)) + [1])


ORDER = dict(a=near_first, c=near_first, d=near_first)
SCHEDULE = ("a", "aca", "cadcadcdcdadcacdd")


def whole_rows(
    target, memory, target_lens, source_lens, self_in, self_out, cross_q, cross_kv, cross_out, ffn_in, ffn_in_bias,
    ffn_out, ffn_out_bias, norm_gain, norm_bias, cotangent,
):
    f32, bf16 = jnp.float32, jnp.bfloat16
    _, half, width = target.shape
    length = 2 * half
    hidden = ffn_in.shape[1]
    wide = lax.axis_index("wide")
    place = jnp.stack([lax.axis_index("narrow"), wide % 2, wide]).astype(jnp.int32)
    place = jnp.concatenate([place, target_lens[0], source_lens[0]])
    chain = Chain()

    def other_half(values):
        return lax.ppermute(values, "narrow", [(0, 1), (1, 0)])

    own_t, own_m, own_c = target[0], memory[0], cotangent[0]
    other_t, other_m, other_c = other_half(own_t), other_half(own_m), other_half(own_c)
    square = (length, width)
    attn_shape = (HEADS, length, length)
    macs = length * width * width
    rows = width // 4

    vectors = jnp.concatenate(
        [norm_gain, norm_bias, ffn_out_bias[None], jnp.zeros((1, width), f32), ffn_in_bias.reshape(-1, width)], axis=0
    )
    vectors = jnp.pad(vectors, ((0, -vectors.shape[0] % 8), (0, 0)))

    step = Kernel(chain, place)
    step.far(own=own_t)
    step.prefetch(self_in=self_in, self_out=self_out, cross_q=cross_q, cross_kv=cross_kv, cross_out=cross_out, own_t=own_t)
    step.near_out(
        triple_own=((half, 3 * width), bf16), self_bias=((length, length), f32), cross_bias=((length, length), f32)
    )
    (
        self_in_near, self_out_near, cross_q_near, cross_kv_near, cross_out_near, own_near, triple_own, self_bias, cross_bias,
    ) = step.run(first_body, 8 * macs, 12)

    step = Kernel(chain, place)
    step.near(other=other_t)
    step.near(self_in=self_in_near, self_out=self_out_near, own=own_near, triple_own=triple_own, bias=self_bias)
    step.far_out(triple=((length, 3 * width), bf16), mix=(square, bf16))
    step.heads_out(attn=(attn_shape, bf16))
    step.near_out(centre_first=(square, f32))
    step.hold(work=((2, length, length), f32))
    triple, self_mix, self_attn, centre_first = step.run(self_forward_body, 24 * macs, 16)

    step = Kernel(chain, place)
    step.halves(memory=(own_m, other_m))
    step.near(centre_first=centre_first, cross_q=cross_q_near, cross_kv=cross_kv_near, cross_out=cross_out_near)
    step.near(vectors=vectors, bias=cross_bias)
    step.copy_out(centre_first_far=("centre_first", square, f32))
    step.far_out(query=(square, bf16), pairs=((length, 2 * width), bf16), mix=(square, bf16))
    step.heads_out(attn=(attn_shape, bf16))
    step.near_out(centre_second=(square, f32))
    step.hold(work=((2, length, length), f32))
    step.prefetch(ffn_in=ffn_in, ffn_out=ffn_out)
    (
        centre_first, query, pairs, cross_mix, cross_attn, centre_second, ffn_in_near, ffn_out_near,
    ) = step.run(cross_forward_body, 24 * macs, 16)

    step = Kernel(chain, place)
    step.near(centre_second=centre_second, ffn_in=ffn_in_near, ffn_out=ffn_out_near, vectors=vectors)
    step.halves(cotangent=(own_c, other_c))
    step.far_out(output=((half, width), bf16))
    step.near_out(
        grad_second=(square, f32), sums=((8, width), f32), in_sums=((1, hidden), f32),
        keep=((rows, 2 * hidden), f32), send=((rows, 2 * hidden), bf16),
    )
    step.prefetch(cross_out=cross_out, query=query)
    step.hold(
        second=(square, bf16), active=((length, hidden), bf16), slope=((length, hidden), f32), outer=(square, bf16),
        inner=((length, hidden), bf16),
    )
    output, grad, sums, in_sums, feed_keep, feed_send, cross_out_near, query = step.run(feed_body, 40 * macs, 26)

    bits = lax.axis_size("wide").bit_length() - 1
    orders = {name: ORDER[name](bits) for name in ORDER}
    chunk_a = Chunk(chain, feed_keep, feed_send, orders["a"])
    chunks = dict(a=chunk_a)
    step = Kernel(chain, place)
    step.near(grad=grad, sums=sums, in_sums=in_sums, centre_second=centre_second, cross_out=cross_out_near, query=query)
    step.near(vectors=vectors)
    step.near_out(
        small=((16, half), f32), grad_second=(square, f32), grad_low=(square, bf16), dmix=(square, bf16),
        dmix_t=(square, bf16), query_t=(square, bf16),
    )
    step.prefetch(pairs=pairs, mix=cross_mix)
    step.hold(work=((8, width), f32))
    small, grad_second, grad_low, dmix, dmix_t, query_t, pairs, cross_mix = step.run(between_body, 24 * macs * 4, 8)
    for name in SCHEDULE[0]:
        chunks[name].advance()

    step = Kernel(chain, place)
    step.near(grad_second=grad_second, small=small, vectors=vectors, grad_low=grad_low, dmix=dmix, dmix_t=dmix_t)
    step.near(query_t=query_t, query=query, pairs=pairs, mix=cross_mix)
    step.heads("attn", cross_attn, 0, HEADS // 2)
    step.far(cross_kv=cross_kv)
    step.halves(memory=(own_m, other_m))
    step.far(centre_first=centre_first, cross_q=cross_q, self_mix=self_mix)
    step.far_out(memory_grad=((half, width), f32))
    step.near_out(
        grad_first=(square, f32), keep=((rows, 5 * width + 128), f32), send=((rows, 5 * width + 128), bf16)
    )
    step.prefetch(self_out=self_out, triple=triple, mix=self_mix)
    step.hold(
        work=((2, length, length), f32), dscores=((2, length, length), bf16),
        first=(square, bf16), grad=(square, bf16), dquery=(square, bf16), dpairs_t=((2 * width, length), bf16), sums=((8, width), f32), turned=((128, half), f32),
    )
    memory_grad, grad_first, cross_keep, cross_send, self_out_near, triple, self_mix = step.run(cross_back_body, 48 * macs * 4, 24)

    chunk_c = chunks["c"] = Chunk(chain, cross_keep, cross_send, orders["c"])
    for name in SCHEDULE[1]:
        chunks[name].advance()

    def self_part(first, last):
        span = (last - first) * PAIR
        step = Kernel(chain, place)
        step.near(grad_first=grad_first)
        step.near(self_out=self_out_near, triple=triple, mix=self_mix)
        step.heads("attn", self_attn, first, last)
        step.halves(target=(own_t, other_t))
        step.far(self_in=self_in)
        step.far_out(target_grad=((half, width), f32))
        step.near_out(keep=((rows, 3 * span), f32), send=((rows, 3 * span), bf16))
        step.hold(
            grad=(square, bf16), dmix=((length, span), bf16), dmix_t=((span, length), bf16),
            query_t=((span, length), bf16), dquery=((length, span), bf16), dpairs_t=((2 * span, length), bf16),
        )
        return step.run(functools.partial(self_back_body, (first, last)), 24 * macs * 12, 16)

    target_grad, keep, send = self_part(0, HEADS // 2)
    chunk_d = chunks["d"] = Chunk(chain, keep, send, orders["d"])
    groups = hidden // width
    endings = dict(
        a=(
            [(0, group * half, 0, group * width, width) for group in range(groups)] + [(1, 0, 0, hidden, hidden)],
            [((groups * half, width), f32), ((half, hidden), f32)],
        ),
        c=(
            [(0, 0, 0, 0, width), (1, 0, 0, width, 2 * width), (2, 0, 0, 3 * width, width), (3, 0, 0, 4 * width, width)],
            [
                ((half, width), f32), ((half, 2 * width), f32), ((half, width), f32), ((half, width), f32),
                ((3, half), f32), ((3, half), f32), ((1, half), f32), ((1, groups * half), f32),
            ],
            [(4, 0, 0, 5), (4, 1, 0, 3), (4, 2, 0, 0), (5, 0, 0, 6), (5, 1, 0, 4), (5, 2, 0, 1), (6, 0, 0, 2)]
            + [(7, 0, row * half, 8 + row) for row in range(groups)],
        ),
        d=([(0, 0, 0, 0, 3 * width)], [((half, 3 * width), f32)]),
    )
    finished = {}
    for name in SCHEDULE[2]:
        if chunks[name].left():
            chunks[name].advance()
        elif name not in finished:
            finished[name] = chunks[name].finish(*endings[name])
    ffn_out_g, ffn_in_g = finished["a"]
    cross_q_g, cross_kv_g, cross_out_g, self_out_g, gain_g, shift_g, out_bias_g, in_bias_g = finished["c"]
    (self_in_g,) = finished["d"]
    return (
        output[None],
        target_grad[None],
        memory_grad[None],
        self_in_g,
        self_out_g,
        cross_q_g,
        cross_kv_g,
        cross_out_g,
        ffn_in_g,
        in_bias_g[0],
        ffn_out_g,
        out_bias_g[0],
        gain_g,
        shift_g,
    )


def fits_whole_rows(mesh, target, lens):
    wide, narrow = mesh.shape["wide"], mesh.shape["narrow"]
    rows, length, width = target.shape
    documents = lens.shape[1]
    return (
        narrow == 2
        and rows == wide
        and wide >= 2
        and wide & (wide - 1) == 0
        and length <= 512
        and documents == DOCUMENTS
        and width == HEADS * HEAD_DIM
        and width % (32 * wide) == 0
    )


def solution(mesh):
    in_specs = (
        P("wide", "narrow", None),
        P("wide", "narrow", None),
        P("wide", None),
        P("wide", None),
        P(),
        P(),
        P(),
        P(),
        P(),
        P(),
        P(),
        P(),
        P(),
        P(),
        P(),
        P("wide", "narrow", None),
    )
    out_specs = (
        P("wide", "narrow", None),
        P("wide", "narrow", None),
        P("wide", "narrow", None),
        P("narrow", None),
        P("narrow", None),
        P("narrow", None),
        P("narrow", None),
        P("narrow", None),
        P("narrow", None),
        P("narrow"),
        P("narrow", None),
        P("narrow"),
        P(None, "narrow"),
        P(None, "narrow"),
    )

    def layer(*arrays):
        body = whole_rows if fits_whole_rows(mesh, arrays[0], arrays[2]) else local
        return jax.shard_map(body, mesh=mesh, in_specs=in_specs, out_specs=out_specs, check_vma=False)(*arrays)

    return layer
```

```python
import functools
import math
import types

import jax
import jax.numpy as jnp
from jax import lax
from jax.experimental import pallas as pl
from jax.experimental.pallas import tpu as pltpu
from jax.sharding import PartitionSpec as P

HEADS = 8
HEAD_DIM = 64


EPSILON = 1e-05
MASKED = -1e30


def segment_ids(doc_lens, length):
    ends = jnp.cumsum(doc_lens, axis=-1)
    places = jnp.arange(length, dtype=jnp.int32)
    return jnp.sum((places[:, None] >= ends[..., None, :]).astype(jnp.int32), axis=-1)


def layer_norm(values, gain, shift):
    centre = values - jnp.mean(values, axis=-1, keepdims=True)
    spread = jnp.mean(centre * centre, axis=-1, keepdims=True)
    return centre * lax.rsqrt(spread + EPSILON) * gain + shift


def gelu_tanh(values):
    return jax.nn.gelu(values, approximate=True)


def project(activity, weight):
    return jnp.einsum("rsd,de->rse", activity, weight, preferred_element_type=jnp.float32)


def project_back(gradient, weight):
    return jnp.einsum("rse,de->rsd", gradient, weight, preferred_element_type=jnp.float32)


def weight_grad(activity, gradient):
    return jnp.einsum("rsd,rse->de", activity, gradient, preferred_element_type=jnp.float32)


def split_heads(values):
    return values.reshape(values.shape[0], values.shape[1], HEADS, HEAD_DIM)


def join_heads(values):
    return values.reshape(values.shape[0], values.shape[1], HEADS * HEAD_DIM)


def block_scores(query_heads, key_heads, query_seg, key_seg, query_pos, key_pos, causal):
    raw_scores = jnp.einsum(
        "rqhd,rkhd->rhqk", query_heads, key_heads, preferred_element_type=jnp.float32
    )
    visible = query_seg[:, :, None] == key_seg[:, None, :]
    if causal:
        visible = visible & (key_pos[None, None, :] <= query_pos[None, :, None])
    return jnp.where(visible[:, None], raw_scores * HEAD_DIM ** (-0.5), MASKED)


def block_backward(query_heads, grad_heads, key_heads, value_heads, scores, log_norm, row_dot):
    attention = jnp.exp(scores - log_norm[..., None])
    grad_attn = jnp.einsum(
        "rqhd,rkhd->rhqk", grad_heads, value_heads, preferred_element_type=jnp.float32
    )
    grad_scores = (attention * (grad_attn - row_dot[..., None]) * HEAD_DIM ** (-0.5)).astype(
        jnp.bfloat16
    )
    grad_query = jnp.einsum(
        "rhqk,rkhd->rqhd", grad_scores, key_heads, preferred_element_type=jnp.float32
    )
    grad_key = jnp.einsum(
        "rhqk,rqhd->rkhd", grad_scores, query_heads, preferred_element_type=jnp.float32
    )
    grad_value = jnp.einsum(
        "rhqk,rqhd->rkhd",
        attention.astype(jnp.bfloat16),
        grad_heads,
        preferred_element_type=jnp.float32,
    )
    return (grad_query, jnp.concatenate([join_heads(grad_key), join_heads(grad_value)], axis=-1))


def make_key_fold(query_heads, query_seg, key_seg_full, query_pos, causal, running, portion):
    run_max, run_sum, stored = running
    span_len = portion.shape[1]
    key_pos = jnp.arange(span_len, dtype=jnp.int32)
    scores = block_scores(
        query_heads,
        split_heads(portion[:, :, : HEADS * HEAD_DIM]),
        query_seg,
        key_seg_full,
        query_pos,
        key_pos,
        causal,
    )
    new_max = jnp.maximum(run_max, jnp.max(scores, axis=-1))
    run_sum = jnp.sum(jnp.exp(scores - new_max[..., None]), axis=-1)
    stored = portion
    return (new_max, run_sum, stored)


def attend_stored(query_heads, stored, query_seg, key_seg_full, query_pos, causal, log_norm):
    total_len = stored.shape[1]
    pair_half = stored.shape[2] // 2
    block_len = math.gcd(total_len, max(query_heads.shape[1], 512))

    def advance(low_sum, block_idx):
        begin_at = block_idx * block_len
        portion = lax.dynamic_slice_in_dim(stored, begin_at, block_len, 1)
        key_seg = lax.dynamic_slice_in_dim(key_seg_full, begin_at, block_len, 1)
        key_pos = begin_at + jnp.arange(block_len, dtype=jnp.int32)
        value_heads = split_heads(portion[:, :, pair_half:])
        scores = block_scores(
            query_heads,
            split_heads(portion[:, :, :pair_half]),
            query_seg,
            key_seg,
            query_pos,
            key_pos,
            causal,
        )
        attention = jnp.exp(scores - log_norm[..., None])
        low_sum = low_sum + jnp.einsum(
            "rhqk,rkhd->rqhd",
            attention.astype(jnp.bfloat16),
            value_heads,
            preferred_element_type=jnp.float32,
        )
        return (low_sum, None)

    zeros_q = jnp.zeros(query_heads.shape, jnp.float32)
    low_sum, _ = lax.scan(advance, zeros_q, jnp.arange(total_len // block_len, dtype=jnp.int32))
    return low_sum


def attend_back_stored(
    query_heads, grad_heads, stored, query_seg, key_seg_full, query_pos, causal, log_norm, row_dot
):
    total_len = stored.shape[1]
    pair_half = stored.shape[2] // 2
    block_len = math.gcd(total_len, max(query_heads.shape[1], 512))

    def advance(block_idx, running):
        grad_query, grad_term = running
        begin_at = block_idx * block_len
        portion = lax.dynamic_slice_in_dim(stored, begin_at, block_len, 1)
        key_seg = lax.dynamic_slice_in_dim(key_seg_full, begin_at, block_len, 1)
        key_pos = begin_at + jnp.arange(block_len, dtype=jnp.int32)
        key_heads = split_heads(portion[:, :, :pair_half])
        value_heads = split_heads(portion[:, :, pair_half:])
        scores = block_scores(
            query_heads, key_heads, query_seg, key_seg, query_pos, key_pos, causal
        )
        block_dq, block_dkv = block_backward(
            query_heads, grad_heads, key_heads, value_heads, scores, log_norm, row_dot
        )
        grad_term = lax.dynamic_update_slice_in_dim(grad_term, block_dkv, begin_at, 1)
        return (grad_query + block_dq, grad_term)

    start_vals = (jnp.zeros(query_heads.shape, jnp.float32), jnp.zeros(stored.shape, jnp.float32))
    grad_query, grad_term = lax.fori_loop(0, total_len // block_len, advance, start_vals)
    return (join_heads(grad_query), grad_term)


def local(
    target,
    memory,
    target_lens,
    source_lens,
    self_in,
    self_out,
    cross_q,
    cross_kv,
    cross_out,
    ffn_in,
    ffn_in_bias,
    ffn_out,
    ffn_out_bias,
    norm_gain,
    norm_bias,
    cotangent,
):
    row_count, shard_len, feat_width = target.shape
    total_len = shard_len * lax.axis_size("narrow")
    own_start = lax.axis_index("narrow") * shard_len
    own_pos = own_start + jnp.arange(shard_len, dtype=jnp.int32)
    target_seg = segment_ids(target_lens, total_len)
    source_seg = segment_ids(source_lens, total_len)
    target_own = lax.dynamic_slice_in_dim(target_seg, own_start, shard_len, 1)
    start_state = (
        jnp.full((row_count, HEADS, shard_len), MASKED, jnp.float32),
        jnp.zeros((row_count, HEADS, shard_len), jnp.float32),
        jnp.zeros((row_count, total_len, 2 * feat_width), jnp.bfloat16),
    )
    triple = project(target, self_in).astype(jnp.bfloat16)
    self_query = split_heads(triple[:, :, :feat_width])
    self_pairs = triple[:, :, feat_width:]
    self_max, self_sum, self_store = make_key_fold(
        self_query,
        target_own,
        target_seg,
        own_pos,
        True,
        start_state,
        lax.all_gather(self_pairs, "narrow", axis=1, tiled=True),
    )
    self_norm = self_max + jnp.log(self_sum)
    self_low = attend_stored(
        self_query, self_store, target_own, target_seg, own_pos, True, self_norm
    )
    self_mix = join_heads(self_low).astype(jnp.bfloat16)
    first, first_pull = jax.vjp(
        layer_norm,
        target.astype(jnp.float32) + project(self_mix, self_out),
        norm_gain[0],
        norm_bias[0],
    )
    first_low = first.astype(jnp.bfloat16)
    cross_query = split_heads(project(first_low, cross_q).astype(jnp.bfloat16))
    cross_pairs = project(memory, cross_kv).astype(jnp.bfloat16)
    cross_max, cross_sum, cross_store = make_key_fold(
        cross_query,
        target_own,
        source_seg,
        own_pos,
        False,
        start_state,
        lax.all_gather(cross_pairs, "narrow", axis=1, tiled=True),
    )
    cross_norm = cross_max + jnp.log(cross_sum)
    cross_low = attend_stored(
        cross_query, cross_store, target_own, source_seg, own_pos, False, cross_norm
    )
    cross_mix = join_heads(cross_low).astype(jnp.bfloat16)
    second, second_pull = jax.vjp(
        layer_norm, first + project(cross_mix, cross_out), norm_gain[1], norm_bias[1]
    )
    second_low = second.astype(jnp.bfloat16)
    inner = project(second_low, ffn_in) + ffn_in_bias
    active, gelu_pull = jax.vjp(gelu_tanh, inner)
    active_low = active.astype(jnp.bfloat16)
    result, third_pull = jax.vjp(
        layer_norm, second + project(active_low, ffn_out) + ffn_out_bias, norm_gain[2], norm_bias[2]
    )
    grad_third, gain_third, shift_third = third_pull(cotangent.astype(jnp.float32))
    grad_outer = grad_third.astype(jnp.bfloat16)
    ffn_out_g = weight_grad(active_low, grad_outer)
    ffn_out_bias_g = jnp.sum(grad_third, axis=(0, 1))
    (grad_active,) = gelu_pull(project_back(grad_outer, ffn_out))
    grad_inner = grad_active.astype(jnp.bfloat16)
    ffn_in_g = weight_grad(second_low, grad_inner)
    ffn_in_bias_g = jnp.sum(grad_active, axis=(0, 1))
    grad_second, gain_second, shift_second = second_pull(
        grad_third + project_back(grad_inner, ffn_in)
    )
    grad_cross = grad_second.astype(jnp.bfloat16)
    cross_out_g = weight_grad(cross_mix, grad_cross)
    cross_dout = split_heads(project_back(grad_cross, cross_out).astype(jnp.bfloat16))
    cross_dot = jnp.swapaxes(jnp.sum(cross_dout.astype(jnp.float32) * cross_low, axis=-1), 1, 2)
    cross_dq, cross_term = attend_back_stored(
        cross_query,
        cross_dout,
        cross_store,
        target_own,
        source_seg,
        own_pos,
        False,
        cross_norm,
        cross_dot,
    )
    cross_dpairs = lax.psum_scatter(
        cross_term.astype(jnp.bfloat16), "narrow", scatter_dimension=1, tiled=True
    )
    cross_dq_low = cross_dq.astype(jnp.bfloat16)
    cross_q_g = weight_grad(first_low, cross_dq_low)
    cross_kv_g = weight_grad(memory, cross_dpairs)
    memory_grad = project_back(cross_dpairs, cross_kv)
    grad_first, gain_first, shift_first = first_pull(
        grad_second + project_back(cross_dq_low, cross_q)
    )
    grad_self = grad_first.astype(jnp.bfloat16)
    self_out_g = weight_grad(self_mix, grad_self)
    self_dout = split_heads(project_back(grad_self, self_out).astype(jnp.bfloat16))
    self_dot = jnp.swapaxes(jnp.sum(self_dout.astype(jnp.float32) * self_low, axis=-1), 1, 2)
    self_dq, self_term = attend_back_stored(
        self_query,
        self_dout,
        self_store,
        target_own,
        target_seg,
        own_pos,
        True,
        self_norm,
        self_dot,
    )
    self_dpairs = lax.psum_scatter(
        self_term.astype(jnp.bfloat16), "narrow", scatter_dimension=1, tiled=True
    ).astype(jnp.float32)
    grad_triple = jnp.concatenate([self_dq, self_dpairs], axis=-1).astype(jnp.bfloat16)
    self_in_g = weight_grad(target, grad_triple)
    target_grad = grad_first + project_back(grad_triple, self_in)
    gain_g = jnp.stack([gain_first, gain_second, gain_third])
    shift_g = jnp.stack([shift_first, shift_second, shift_third])
    sh_a, sh_b, sh_c, sh_d, sh_e, sh_f, sh_g, sh_h, sh_i, sh_j, sh_k = (
        lax.psum_scatter(
            self_in_g.astype(jnp.bfloat16), "narrow", scatter_dimension=0, tiled=True
        ).astype(jnp.float32),
        lax.psum_scatter(
            self_out_g.astype(jnp.bfloat16), "narrow", scatter_dimension=0, tiled=True
        ).astype(jnp.float32),
        lax.psum_scatter(
            cross_q_g.astype(jnp.bfloat16), "narrow", scatter_dimension=0, tiled=True
        ).astype(jnp.float32),
        lax.psum_scatter(
            cross_kv_g.astype(jnp.bfloat16), "narrow", scatter_dimension=0, tiled=True
        ).astype(jnp.float32),
        lax.psum_scatter(
            cross_out_g.astype(jnp.bfloat16), "narrow", scatter_dimension=0, tiled=True
        ).astype(jnp.float32),
        lax.psum_scatter(
            ffn_in_g.astype(jnp.bfloat16), "narrow", scatter_dimension=0, tiled=True
        ).astype(jnp.float32),
        lax.psum_scatter(
            ffn_in_bias_g.astype(jnp.bfloat16), "narrow", scatter_dimension=0, tiled=True
        ).astype(jnp.float32),
        lax.psum_scatter(
            ffn_out_g.astype(jnp.bfloat16), "narrow", scatter_dimension=0, tiled=True
        ).astype(jnp.float32),
        lax.psum_scatter(
            ffn_out_bias_g.astype(jnp.bfloat16), "narrow", scatter_dimension=0, tiled=True
        ).astype(jnp.float32),
        lax.psum_scatter(
            gain_g.astype(jnp.bfloat16), "narrow", scatter_dimension=1, tiled=True
        ).astype(jnp.float32),
        lax.psum_scatter(
            shift_g.astype(jnp.bfloat16), "narrow", scatter_dimension=1, tiled=True
        ).astype(jnp.float32),
    )
    summed = (
        lax.psum(sh_a.astype(jnp.bfloat16), "wide").astype(jnp.float32),
        lax.psum(sh_b.astype(jnp.bfloat16), "wide").astype(jnp.float32),
        lax.psum(sh_c.astype(jnp.bfloat16), "wide").astype(jnp.float32),
        lax.psum(sh_d.astype(jnp.bfloat16), "wide").astype(jnp.float32),
        lax.psum(sh_e.astype(jnp.bfloat16), "wide").astype(jnp.float32),
        lax.psum(sh_f.astype(jnp.bfloat16), "wide").astype(jnp.float32),
        lax.psum(sh_g.astype(jnp.bfloat16), "wide").astype(jnp.float32),
        lax.psum(sh_h.astype(jnp.bfloat16), "wide").astype(jnp.float32),
        lax.psum(sh_i.astype(jnp.bfloat16), "wide").astype(jnp.float32),
        lax.psum(sh_j.astype(jnp.bfloat16), "wide").astype(jnp.float32),
        lax.psum(sh_k.astype(jnp.bfloat16), "wide").astype(jnp.float32),
    )
    return (
        result.astype(jnp.bfloat16),
        target_grad,
        memory_grad,
        summed[0],
        summed[1],
        summed[2],
        summed[3],
        summed[4],
        summed[5],
        summed[6],
        summed[7],
        summed[8],
        summed[9],
        summed[10],
    )


def dot_nn(left, right):
    return jnp.dot(left, right, preferred_element_type=jnp.float32)


def dot_nt(left, right):
    return lax.dot_general(left, right, (((1,), (1,)), ((), ())), preferred_element_type=jnp.float32)


def dot_tn(left, right):
    return lax.dot_general(left, right, (((0,), (0,)), ((), ())), preferred_element_type=jnp.float32)


def low(values):
    return values.astype(jnp.bfloat16)


def centred(values):
    return values - jnp.mean(values, axis=-1, keepdims=True)


def unit_of(centre):
    scale = lax.rsqrt(jnp.mean(centre * centre, axis=-1, keepdims=True) + EPSILON)
    return centre * scale, scale


def normalize_back(grad, gain, unit, scale):
    inner = grad * gain
    return scale * (
        inner
        - jnp.mean(inner, axis=-1, keepdims=True)
        - unit * jnp.mean(inner * unit, axis=-1, keepdims=True)
    )


DOCUMENTS = 8
TARGET_LENS = range(3, 3 + DOCUMENTS)
SOURCE_LENS = range(3 + DOCUMENTS, 3 + 2 * DOCUMENTS)


def seg_along(place_ref, lens, shape, dim):
    places = lax.broadcasted_iota(jnp.int32, shape, dim)
    seg = jnp.zeros(shape, jnp.int32)
    end = jnp.int32(0)
    for doc in lens:
        end = end + place_ref[doc]
        seg = seg + (places >= end).astype(jnp.int32)
    return seg


def visible_pairs(place_ref, query_lens, key_lens, length, causal):
    query_seg = seg_along(place_ref, query_lens, (length, 1), 0)
    seen = query_seg == seg_along(place_ref, key_lens, (1, length), 1)
    if causal:
        rows = lax.broadcasted_iota(jnp.int32, (length, length), 0)
        cols = lax.broadcasted_iota(jnp.int32, (length, length), 1)
        seen = seen & (cols <= rows)
    return seen


class Far:
    def __init__(self, far_refs, near, sems, parts, inward):
        self.near, self.sems, self.inward, self.waited = near, sems, inward, set()
        self.far_refs, self.parts = far_refs, parts

    def copy(self, part):
        far, near = self.far_refs[0 if len(self.far_refs) == 1 else part], self.near
        if self.parts is not None:
            far_at, near_at = self.parts(part)
            far = far if far_at is None else far.at[far_at]
            near = near if near_at is None else near.at[near_at]
        ends = (far, near) if self.inward else (near, far)
        return pltpu.make_async_copy(*ends, self.sems.at[part])

    def start(self):
        for part in range(self.sems.shape[0]):
            self.copy(part).start()

    def wait(self):
        for part in range(self.sems.shape[0]):
            self.copy(part).wait()

    def get(self):
        if 0 not in self.waited:
            self.waited.add(0)
            self.wait()
        return self.near


TOKEN = (8, 128)
SMALL_COST = 25 * 10**9


def write_token(place_ref):
    lane = lax.broadcasted_iota(jnp.int32, TOKEN, 1)
    token = jnp.zeros(TOKEN, jnp.int32)
    for index in range(3):
        token = jnp.where(lane == index, place_ref[index], token)
    return token


class Chain:
    def __init__(self):
        self.token = None


class Kernel:
    def __init__(self, chain, place, *scalars):
        self.chain = chain
        self.scalars = (place, *scalars)
        self.operands, self.results, self.scratch, self.entries = [], [], [], {}
        self.place = place

    def _scratch(self, what):
        self.scratch.append(what)
        return ("scratch", len(self.scratch) - 1)

    def _operand(self, array, space):
        if space is not pl.ANY:
            array = pltpu.with_memory_space_constraint(array, space)
        self.operands.append((array, space))
        return ("operand", len(self.operands) - 1)

    def _result(self, shape, dtype, space):
        kept = jax.ShapeDtypeStruct(shape, dtype) if space is pl.ANY else space(shape, dtype)
        self.results.append((kept, space))
        return ("result", len(self.results) - 1)

    def near(self, **arrays):
        for name, array in arrays.items():
            self.entries[name] = ("plain", self._operand(array, pltpu.VMEM))

    def far(self, **arrays):
        for name, array in arrays.items():
            ref = self._operand(array, pltpu.HBM)
            near = self._scratch(pltpu.VMEM(array.shape, array.dtype))
            self.entries[name] = ("far", [ref], near, self._scratch(pltpu.SemaphoreType.DMA((1,))), "all", True)

    def halves(self, **pairs):
        for name, (own, other) in pairs.items():
            refs = [self._operand(own, pltpu.HBM), self._operand(other, pl.ANY)]
            near = self._scratch(pltpu.VMEM((2 * own.shape[0], own.shape[1]), own.dtype))
            self.entries[name] = ("far", refs, near, self._scratch(pltpu.SemaphoreType.DMA((2,))), "halves", True)

    def heads(self, name, array, first, last):
        ref = self._operand(array, pltpu.HBM)
        near = self._scratch(pltpu.VMEM((2 * (last - first),) + array.shape[1:], array.dtype))
        sems = self._scratch(pltpu.SemaphoreType.DMA((last - first,)))
        self.entries[name] = ("far", [ref], near, sems, ("heads", first), True)

    def near_out(self, **outs):
        for name, (shape, dtype) in outs.items():
            self.entries[name] = ("plain", self._result(shape, dtype, pltpu.VMEM))

    def free_out(self, **outs):
        for name, (shape, dtype) in outs.items():
            ref = self._result(shape, dtype, pl.ANY)
            near = self._scratch(pltpu.VMEM(shape, dtype))
            self.entries[name] = ("far", [ref], near, self._scratch(pltpu.SemaphoreType.DMA((1,))), "all", False)

    def far_out(self, **outs):
        for name, (shape, dtype) in outs.items():
            ref = self._result(shape, dtype, pltpu.HBM)
            near = self._scratch(pltpu.VMEM(shape, dtype))
            self.entries[name] = ("far", [ref], near, self._scratch(pltpu.SemaphoreType.DMA((1,))), "all", False)

    def heads_out(self, **outs):
        for name, (shape, dtype) in outs.items():
            ref = self._result(shape, dtype, pltpu.HBM)
            near = self._scratch(pltpu.VMEM(shape, dtype))
            sems = self._scratch(pltpu.SemaphoreType.DMA((shape[0] // 2,)))
            self.entries[name] = ("far", [ref], near, sems, ("heads", 0), False)

    def copy_out(self, **outs):
        for name, (source, shape, dtype) in outs.items():
            ref = self._result(shape, dtype, pltpu.HBM)
            near = self.entries[source][1]
            self.entries[name] = ("far", [ref], near, self._scratch(pltpu.SemaphoreType.DMA((1,))), "all", False)

    def prefetch(self, **arrays):
        for name, array in arrays.items():
            ref = self._operand(array, pltpu.HBM)
            near = self._result(array.shape, array.dtype, pltpu.VMEM)
            sems = self._scratch(pltpu.SemaphoreType.DMA((1,)))
            self.entries["prefetch_" + name] = ("far", [ref], near, sems, "all", True)

    def hold(self, **outs):
        for name, (shape, dtype) in outs.items():
            self.entries[name] = ("plain", self._scratch(pltpu.VMEM(shape, dtype)))

    def run(self, body, flops, vmem_mib):
        held = None if self.chain.token is None else self._operand(self.chain.token, pltpu.VMEM)[1]
        last = self._result(TOKEN, jnp.int32, pltpu.VMEM)[1]

        def kernel(*refs):
            count = len(self.scalars)
            bounds = (count, count + len(self.operands), count + len(self.operands) + len(self.results))
            groups = {
                "operand": refs[bounds[0] : bounds[1]],
                "result": refs[bounds[1] : bounds[2]],
                "scratch": refs[bounds[2] :],
            }
            mine = refs[0][0]
            views = types.SimpleNamespace()
            for name, entry in self.entries.items():
                if entry[0] == "plain":
                    setattr(views, name, groups[entry[1][0]][entry[1][1]])
                    continue
                _, far, near, sems, cut, inward = entry
                near = groups[near[0]][near[1]]
                half = near.shape[0] // 2
                parts = None
                if cut == "halves":

                    def parts(part, half=half):
                        place = mine if part == 0 else 1 - mine
                        return (None, pl.ds(pl.multiple_of(place * half, half), half))

                if isinstance(cut, tuple):

                    def parts(part, skip=cut[1]):
                        return (pl.ds((skip + part) * 2, 2), pl.ds(part * 2, 2))

                setattr(views, name, Far([groups[g][i] for g, i in far], near, groups[sems[0]][sems[1]], parts, inward))
            groups["result"][last][...] = write_token(refs[0]) if held is None else groups["operand"][held][...]
            for view in vars(views).values():
                if isinstance(view, Far) and view.inward:
                    view.start()
            body(refs[:count], views)
            for name, view in vars(views).items():
                if isinstance(view, Far) and (not view.inward or name.startswith("prefetch_")):
                    view.get()

        arrays = [array for array, _ in self.operands]
        shapes = [kept for kept, _ in self.results]
        moved = sum(math.prod(a.shape) * a.dtype.itemsize for a in arrays)
        *results, self.chain.token = pl.pallas_call(
            kernel,
            out_shape=shapes,
            in_specs=[pl.BlockSpec(memory_space=pltpu.SMEM)] * len(self.scalars)
            + [pl.BlockSpec(memory_space=space) for _, space in self.operands],
            out_specs=[pl.BlockSpec(memory_space=space) for _, space in self.results],
            scratch_shapes=self.scratch,
            compiler_params=pltpu.CompilerParams(vmem_limit_bytes=vmem_mib * 2**20),
            cost_estimate=pl.CostEstimate(flops=flops, bytes_accessed=moved, transcendentals=0),
        )(*self.scalars, *arrays)
        return results


def ref_of(view):
    return view.get() if isinstance(view, Far) else view


def near_of(view):
    return view.near if isinstance(view, Far) else view


def own_columns(ref, start, width):
    return ref[:, pl.ds(pl.multiple_of(start, 128), width)]


def grad_rows(place_ref, activity_ref, grads, keep_ref, send_ref, col):
    rows = keep_ref.shape[0]
    first = place_ref[0] * 2 * rows
    for ref, part in ((keep_ref, place_ref[1]), (send_ref, 1 - place_ref[1])):
        piece = own_columns(activity_ref, first + part * rows, rows)
        at = col
        for grad in grads:
            ref[:, at : at + grad.shape[1]] = dot_tn(piece, grad).astype(ref.dtype)
            at += grad.shape[1]


def query_blocks(length, causal):
    if causal:
        return ((0, length // 2, length // 2), (length // 2, length, length))
    return ((0, length // 2, length), (length // 2, length, length))


PAIR = 2 * HEAD_DIM


def head_lanes():
    lane = lax.broadcasted_iota(jnp.int32, (1, PAIR), 1)
    return (lane < HEAD_DIM, lane >= HEAD_DIM)


SPAN = 32


def attend_all(query_ref, key_ref, value_ref, bias_ref, attn, mix_ref, work_ref, causal):
    length = query_ref.shape[0]

    def one_pair(pair, carry):
        lanes = pl.ds(pl.multiple_of(pair * PAIR, PAIR), PAIR)
        keys, values = key_ref[:, lanes], value_ref[:, lanes]
        zero = jnp.zeros_like(keys)
        total = jnp.zeros((length, PAIR), jnp.float32)
        for sub, inside in enumerate(head_lanes()):
            work_ref[sub] = dot_nt(query_ref[:, lanes], jnp.where(inside, keys, zero))
            for begin in range(0, length, SPAN):
                rows = slice(begin, begin + SPAN)
                reach = length // 2 if causal and begin + SPAN <= length // 2 else length
                scores = work_ref[sub, rows, :reach] + bias_ref[rows, :reach]
                weights = jnp.exp(scores - jnp.max(scores, axis=-1, keepdims=True))
                weights = low(weights * (1.0 / jnp.sum(weights, axis=-1, keepdims=True)))
                attn.near[pair * 2 + sub, rows, :reach] = weights
                if reach < length:
                    attn.near[pair * 2 + sub, rows, reach:] = jnp.zeros((SPAN, length - reach), weights.dtype)
            total = total + dot_nn(attn.near[pair * 2 + sub], jnp.where(inside, values, zero))
        mix_ref[:, lanes] = low(total)
        attn.copy(pair).start()
        return carry

    lax.fori_loop(0, HEADS // 2, one_pair, 0, unroll=True)


def attend_whole_back(
    query_ref, query_t_ref, key_ref, value_ref, attn, mix_ref, grad_ref, grad_t_ref, dquery_ref, dpairs_t_ref,
    work_ref, dscores_ref,
):
    length, width = query_ref.shape

    def one_pair(pair, carry):
        lanes = pl.ds(pl.multiple_of(pair * PAIR, PAIR), PAIR)
        attn.copy(pair).wait()
        keys, values = key_ref[:, lanes], value_ref[:, lanes]
        zero = jnp.zeros_like(keys)
        dquery = jnp.zeros((length, PAIR), jnp.float32)
        dots = grad_ref[:, lanes].astype(jnp.float32) * mix_ref[:, lanes].astype(jnp.float32)
        for sub, inside in enumerate(head_lanes()):
            row_dot = jnp.sum(jnp.where(inside, dots, 0.0), axis=-1, keepdims=True)
            work_ref[sub] = dot_nt(grad_ref[:, lanes], jnp.where(inside, values, zero))
            for begin in range(0, length, SPAN):
                rows = slice(begin, begin + SPAN)
                weights = attn.near[pair * 2 + sub, rows, :].astype(jnp.float32)
                dscores_ref[sub, rows, :] = low(weights * (work_ref[sub, rows, :] - row_dot[rows]))
            dquery = dquery + dot_nn(dscores_ref[sub], jnp.where(inside, keys, zero))
            first = pair * PAIR + sub * HEAD_DIM
            rows = pl.ds(pl.multiple_of(first, HEAD_DIM), HEAD_DIM)
            dpairs_t_ref[rows, :] = low(dot_nn(query_t_ref[rows, :], dscores_ref[sub]))
            where = pl.ds(pl.multiple_of(width + first, HEAD_DIM), HEAD_DIM)
            dpairs_t_ref[where, :] = low(dot_nn(grad_t_ref[rows, :], attn.near[pair * 2 + sub]))
        dquery_ref[:, lanes] = low(dquery * HEAD_DIM ** (-0.5))
        return carry

    lax.fori_loop(0, HEADS // 2, one_pair, 0)


def attend_all_back(
    pairs, query_ref, query_t_ref, key_ref, value_ref, attn, mix_ref, grad_ref, grad_t_ref, dquery_ref, dpairs_t_ref, causal
):
    length = query_ref.shape[0]
    width = grad_ref.shape[1]

    def one_pair(pair, carry):
        place = pair - pairs[0]
        lanes = pl.ds(pl.multiple_of(pair * PAIR, PAIR), PAIR)
        near_lanes = pl.ds(pl.multiple_of(place * PAIR, PAIR), PAIR)
        attn.copy(place).wait()
        keys, values = key_ref[:, lanes], value_ref[:, lanes]
        zero = jnp.zeros_like(keys)
        blocks = query_blocks(length, causal)
        dquery = [jnp.zeros((end - begin, PAIR), jnp.float32) for begin, end, _ in blocks]
        for sub, inside in enumerate(head_lanes()):
            head_keys = jnp.where(inside, keys, zero)
            head_values = jnp.where(inside, values, zero)
            rows = pl.ds(pl.multiple_of(place * PAIR + sub * HEAD_DIM, HEAD_DIM), HEAD_DIM)
            parts = []
            for idx, (begin, end, reach) in enumerate(blocks):
                grads = grad_ref[begin:end, near_lanes]
                dots = grads.astype(jnp.float32) * mix_ref[begin:end, lanes].astype(jnp.float32)
                row_dot = jnp.sum(jnp.where(inside, dots, 0.0), axis=-1, keepdims=True)
                weights = attn.near[place * 2 + sub, begin:end, :reach]
                dattn = dot_nt(grads, head_values[:reach])
                dscores = low(weights.astype(jnp.float32) * (dattn - row_dot))
                dquery[idx] = dquery[idx] + dot_nn(dscores, head_keys[:reach])
                dkey_t = dot_nn(query_t_ref[rows, begin:end], dscores)
                dvalue_t = dot_nn(grad_t_ref[rows, begin:end], weights)
                parts.append((reach, dkey_t, dvalue_t))
            (reach, dkey_t, dvalue_t), (_, dkey_more, dvalue_more) = parts
            rows_v = pl.ds(pl.multiple_of(width + place * PAIR + sub * HEAD_DIM, HEAD_DIM), HEAD_DIM)
            for where, less, more in ((rows, dkey_t, dkey_more), (rows_v, dvalue_t, dvalue_more)):
                dpairs_t_ref[where, :reach] = low(less + more[:, :reach])
                if reach < length:
                    dpairs_t_ref[where, reach:] = low(more[:, reach:])
        for (begin, end, _), dq in zip(blocks, dquery):
            dquery_ref[begin:end, near_lanes] = low(dq * HEAD_DIM ** (-0.5))
        return carry

    lax.fori_loop(pairs[0], pairs[1], one_pair, 0)


def scaled_query(values):
    return low(low(values) * jnp.bfloat16(HEAD_DIM ** (-0.5)))


def gain_of(vectors_ref, layer):
    return vectors_ref[layer : layer + 1, :]


def shift_of(vectors_ref, layer):
    return vectors_ref[3 + layer : 4 + layer, :]


def first_body(scalars, views):
    (place_ref,) = scalars
    length = views.self_bias.shape[0]
    own, triple = views.own.get(), views.triple_own
    width = own.shape[1]
    weight_ref = views.prefetch_self_in.near
    views.self_bias[...] = jnp.where(visible_pairs(place_ref, TARGET_LENS, TARGET_LENS, length, True), 0.0, MASKED)
    views.cross_bias[...] = jnp.where(visible_pairs(place_ref, TARGET_LENS, SOURCE_LENS, length, False), 0.0, MASKED)
    views.prefetch_self_in.get()
    triple[:, :width] = scaled_query(dot_nn(own[...], weight_ref[:, :width]))
    triple[:, width:] = low(dot_nn(own[...], weight_ref[:, width:]))


def self_forward_body(scalars, views):
    place_ref, = scalars
    other_ref, weight_ref = views.other, views.self_in
    triple, mix = views.triple, views.mix
    half, width = other_ref.shape
    own_rows, other_rows = rows_at(place_ref[0], half), rows_at(1 - place_ref[0], half)
    triple.near[own_rows, :] = views.triple_own[...]
    triple.near[other_rows, :width] = scaled_query(dot_nn(other_ref[...], weight_ref[:, :width]))
    triple.near[other_rows, width:] = low(dot_nn(other_ref[...], weight_ref[:, width:]))
    triple.start()
    attend_all(
        triple.near.at[:, :width], triple.near.at[:, width : 2 * width], triple.near.at[:, 2 * width :],
        views.bias, views.attn, mix.near, views.work, True,
    )
    mix.start()
    centre_ref = views.centre_first
    for rows, part_ref in ((own_rows, views.own), (other_rows, other_ref)):
        summed = part_ref[...].astype(jnp.float32) + dot_nn(mix.near[rows, :], views.self_out[...])
        centre_ref[rows, :] = centred(summed)


def cross_forward_body(scalars, views):
    query, pairs, mix = views.query, views.pairs, views.mix
    width = mix.near.shape[1]
    bias_ref, centre_first_ref, vectors_ref = views.bias, views.centre_first, views.vectors
    views.centre_first_far.start()
    first = unit_of(centre_first_ref[...])[0] * gain_of(vectors_ref, 0) + shift_of(vectors_ref, 0)
    query.near[...] = scaled_query(dot_nn(low(first), views.cross_q[...]))
    query.start()
    pairs.near[...] = low(dot_nn(views.memory.get()[...], views.cross_kv[...]))
    pairs.start()
    attend_all(
        query.near, pairs.near.at[:, :width], pairs.near.at[:, width:], bias_ref, views.attn, mix.near, views.work, False
    )
    mix.start()
    first = unit_of(centre_first_ref[...])[0] * gain_of(vectors_ref, 0) + shift_of(vectors_ref, 0)
    views.centre_second[...] = centred(first + dot_nn(mix.near[...], views.cross_out[...]))


GELU_SCALE = math.sqrt(2.0 / math.pi)
GELU_CUBE = 0.044715


def gelu_both(values):
    square = values * values
    half = 0.5 * jnp.tanh(values * (GELU_SCALE + (GELU_SCALE * GELU_CUBE) * square)) + 0.5
    rise = values * (2.0 * GELU_SCALE + (6.0 * GELU_SCALE * GELU_CUBE) * square)
    return values * half, half + half * (1.0 - half) * rise


STRIP = 16


def feed_body(scalars, views):
    (place_ref,) = scalars
    length, width = views.centre_second.shape
    half = length // 2
    second_ref, active_ref, slope_ref = views.second, views.active, views.slope
    outer_ref, inner_ref, work_ref = views.outer, views.inner, views.grad_second
    vectors_ref = views.vectors
    second = unit_of(views.centre_second[...])[0] * gain_of(vectors_ref, 1) + shift_of(vectors_ref, 1)
    second_ref[...] = low(second)
    total = second + vectors_ref[6:7, :]
    in_ref, out_ref = views.ffn_in, views.ffn_out
    hidden = in_ref.shape[1]
    block = width
    for begin in range(0, hidden, block):
        cols = slice(begin, begin + block)
        index = begin // block
        held_ref = views.held.at[index % 2]
        held_ref[...] = dot_nn(second_ref[...], in_ref[:, cols])
        shift = vectors_ref[8 + index : 9 + index, :]
        for first in range(0, length, STRIP):
            rows = slice(first, first + STRIP)
            active, slope_ref[rows, cols] = gelu_both(held_ref[rows, :] + shift)
            active_ref[rows, cols] = low(active)
        total = total + dot_nn(active_ref[:, cols], out_ref[cols, :])
    unit, scale = unit_of(centred(total))
    work_ref[...] = unit * gain_of(vectors_ref, 2) + shift_of(vectors_ref, 2)
    views.output.near[...] = low(work_ref[pl.ds(pl.multiple_of(place_ref[0] * half, half), half), :])
    views.output.start()
    cotangent = views.cotangent.get()[...].astype(jnp.float32)
    sums_ref, wide_ref = views.sums, views.in_sums
    sums_ref[0:1, :] = jnp.sum(cotangent * unit, axis=0, keepdims=True)
    sums_ref[1:2, :] = jnp.sum(cotangent, axis=0, keepdims=True)
    grad_third = normalize_back(cotangent, gain_of(vectors_ref, 2), unit, scale)
    sums_ref[2:3, :] = jnp.sum(grad_third, axis=0, keepdims=True)
    outer_ref[...] = low(grad_third)
    work_ref[...] = grad_third
    keep, send = views.keep, views.send
    rows = keep.shape[0]
    groups = hidden // width
    for group in range(groups):
        cols = slice(group * width, (group + 1) * width)
        first = (place_ref[0] * groups + group) * 2 * rows
        for view, part in ((keep, place_ref[1]), (send, 1 - place_ref[1])):
            piece = own_columns(active_ref, first + part * rows, rows)
            view[:, cols] = dot_tn(piece, outer_ref[...]).astype(view.dtype)
    into_second = jnp.zeros((length, width), jnp.float32)
    for begin in range(0, hidden, block):
        cols = slice(begin, begin + block)
        held_ref = views.held.at[begin // block % 2]
        held_ref[...] = dot_nt(outer_ref[...], out_ref[cols, :])
        summed = jnp.zeros((STRIP, block), jnp.float32)
        for first in range(0, length, STRIP):
            rows = slice(first, first + STRIP)
            grad_inner = held_ref[rows, :] * slope_ref[rows, cols]
            summed = summed + grad_inner
            inner_ref[rows, cols] = low(grad_inner)
        wide_ref[:, cols] = jnp.sum(summed, axis=0, keepdims=True)
        into_second = into_second + dot_nt(inner_ref[:, cols], in_ref[:, cols])
    grad_rows(place_ref, second_ref, (inner_ref[...],), keep, send, hidden)
    work_ref[...] = work_ref[...] + into_second


def between_body(scalars, views):
    (place_ref,) = scalars
    length, width = views.grad.shape
    sums_ref, wide_ref, vectors_ref, small_ref = views.sums, views.in_sums, views.vectors, views.small
    work_ref = views.work
    grad = views.grad[...]
    unit_second, scale_second = unit_of(views.centre_second[...])
    grad_second = normalize_back(grad, gain_of(vectors_ref, 1), unit_second, scale_second)
    views.grad_second[...] = grad_second
    grad_low_ref = views.grad_low
    grad_low_ref[...] = low(grad_second)
    out_ref = views.cross_out
    seen = jnp.where(visible_pairs(place_ref, TARGET_LENS, SOURCE_LENS, length, False), 1.0, 0.0)
    seen = jnp.max(seen, axis=-1, keepdims=True)
    views.dmix[...] = low(dot_nt(grad_low_ref[...], out_ref[...]) * seen)
    views.dmix_t[...] = low(dot_nt(out_ref[...], grad_low_ref[...]))
    views.query_t[...] = views.query[...].T
    work_ref[0:3, :] = sums_ref[0:3, :]
    work_ref[3:4, :] = jnp.sum(grad * unit_second, axis=0, keepdims=True)
    work_ref[4:5, :] = jnp.sum(grad, axis=0, keepdims=True)
    columns = width // 2
    hidden = wide_ref.shape[1]
    small_ref[...] = jnp.zeros(small_ref.shape, jnp.float32)
    for row in range(5):
        small_ref[row : row + 1, :] = own_columns(work_ref.at[row : row + 1, :], place_ref[0] * columns, columns)
    for row in range(hidden // width):
        start = place_ref[0] * (hidden // 2) + row * columns
        small_ref[8 + row : 9 + row, :] = own_columns(wide_ref, start, columns)


def cross_back_body(scalars, views):
    (place_ref,) = scalars
    length, width = views.grad_second.shape
    half = length // 2
    first_ref, grad_ref, dmix_ref, dmix_t_ref = views.first, views.grad, views.dmix, views.dmix_t
    query_t_ref, dquery_ref, dpairs_t_ref = views.query_t, views.dquery, views.dpairs_t
    grad_second_ref = views.grad_second
    query_ref = views.query
    pairs_ref, mix_ref = views.pairs, views.mix
    attend_whole_back(
        query_ref, query_t_ref, pairs_ref.at[:, :width], pairs_ref.at[:, width:], views.attn, mix_ref,
        dmix_ref, dmix_t_ref, dquery_ref, dpairs_t_ref, views.work, views.dscores,
    )
    vectors_ref = views.vectors
    unit_first, scale_first = unit_of(views.centre_first.get()[...])
    first_ref[...] = low(unit_first * gain_of(vectors_ref, 0) + shift_of(vectors_ref, 0))
    memory_grad = views.memory_grad
    own_dpairs = own_columns(dpairs_t_ref, place_ref[0] * half, half).T
    memory_grad.near[...] = dot_nt(own_dpairs, views.cross_kv.get()[...])
    memory_grad.start()
    keep, send = views.keep, views.send
    grad_rows(place_ref, first_ref, (dquery_ref[...],), keep, send, 0)
    grad_rows(place_ref, views.memory.get(), (dpairs_t_ref[...].T,), keep, send, width)
    grad_rows(place_ref, mix_ref, (views.grad_low[...],), keep, send, 3 * width)
    grad = grad_second_ref[...] + dot_nt(dquery_ref[...], views.cross_q.get()[...])
    sums_ref, small_ref = views.sums, views.small
    sums_ref[0:1, :] = jnp.sum(grad * unit_first, axis=0, keepdims=True)
    sums_ref[1:2, :] = jnp.sum(grad, axis=0, keepdims=True)
    columns = width // 2
    turned_ref = views.turned
    turned_ref[...] = jnp.zeros(turned_ref.shape, jnp.float32)
    turned_ref[: small_ref.shape[0], :] = small_ref[...]
    for row in range(2):
        turned_ref[5 + row : 6 + row, :] = own_columns(sums_ref.at[row : row + 1, :], place_ref[0] * columns, columns)
    grad_first = normalize_back(grad, gain_of(vectors_ref, 0), unit_first, scale_first)
    views.grad_first[...] = grad_first
    grad_ref[...] = low(grad_first)
    grad_rows(place_ref, views.self_mix.get(), (grad_ref[...],), keep, send, 4 * width)
    rows = keep.shape[0]
    for ref, part in ((keep, place_ref[1]), (send, 1 - place_ref[1])):
        ref[:, 5 * width :] = own_columns(turned_ref, part * rows, rows).T.astype(ref.dtype)


def self_back_body(pairs, scalars, views):
    (place_ref,) = scalars
    length, width = views.grad_first.shape
    half = length // 2
    grad_ref, dmix_ref, dmix_t_ref = views.grad, views.dmix, views.dmix_t
    query_t_ref, dquery_ref, dpairs_t_ref = views.query_t, views.dquery, views.dpairs_t
    first, last = pairs[0] * PAIR, pairs[1] * PAIR
    span = last - first
    grad_ref[...] = low(views.grad_first[...])
    out_ref = views.self_out
    dmix_ref[...] = low(dot_nt(grad_ref[...], out_ref[first:last, :]))
    dmix_t_ref[...] = low(dot_nt(out_ref[first:last, :], grad_ref[...]))
    triple_ref = views.triple
    query_t_ref[...] = triple_ref[:, first:last].T
    attend_all_back(
        pairs, triple_ref.at[:, :width], query_t_ref, triple_ref.at[:, width : 2 * width], triple_ref.at[:, 2 * width :],
        views.attn, views.mix, dmix_ref, dmix_t_ref, dquery_ref, dpairs_t_ref, True,
    )
    own_rows = pl.ds(pl.multiple_of(place_ref[0] * half, half), half)
    own_dpairs = own_columns(dpairs_t_ref, place_ref[0] * half, half).T
    weight_ref = views.self_in.get()
    total = (
        dot_nt(dquery_ref[own_rows, :], weight_ref[:, first:last])
        + dot_nt(own_dpairs[:, :span], weight_ref[:, width + first : width + last])
        + dot_nt(own_dpairs[:, span:], weight_ref[:, 2 * width + first : 2 * width + last])
    )
    total = total + views.grad_first[own_rows, :]
    views.target_grad.near[...] = total
    views.target_grad.start()
    keep, send = views.keep, views.send
    grad_rows(place_ref, ref_of(views.target), (dquery_ref[...], dpairs_t_ref[...].T), keep, send, 0)


def send_wide(values, bit):
    count = lax.axis_size("wide")
    return lax.ppermute(values, "wide", [(i, i ^ (1 << bit)) for i in range(count)])


def bit_of(token_ref, bit):
    return (token_ref[0, 2] >> bit) & 1


def small_kernel(chain, body, arrays, outs):
    token = pltpu.with_memory_space_constraint(chain.token, pltpu.VMEM)

    def kernel(token_ref, *refs):
        *refs, last_ref = refs
        last_ref[...] = token_ref[...]
        body(token_ref, *refs)

    *results, chain.token = pl.pallas_call(
        kernel,
        out_shape=[jax.ShapeDtypeStruct(shape, dtype) for shape, dtype in outs] + [pltpu.VMEM(TOKEN, jnp.int32)],
        in_specs=[pl.BlockSpec(memory_space=pltpu.VMEM)] * (len(arrays) + 1),
        out_specs=[pl.BlockSpec(memory_space=pltpu.VMEM)] * (len(outs) + 1),
        compiler_params=pltpu.CompilerParams(vmem_limit_bytes=12 * 2**20),
        cost_estimate=pl.CostEstimate(flops=SMALL_COST, bytes_accessed=1, transcendentals=0),
    )(token, *arrays)
    return results


def rows_at(start, rows):
    return pl.ds(pl.multiple_of(start * rows, rows), rows)


def add_split(chain, keep, received, bit):
    rows = keep.shape[0] // 2
    shape = (rows,) + keep.shape[1:]

    def body(token_ref, keep_ref, came_ref, mine_ref, send_ref):
        mine = bit_of(token_ref, bit)
        for out, part in ((mine_ref, mine), (send_ref, 1 - mine)):
            where = rows_at(part, rows)
            out[...] = (keep_ref[where, :].astype(jnp.float32) + came_ref[where, :].astype(jnp.float32)).astype(out.dtype)

    outs = [(shape, jnp.float32), (shape, jnp.bfloat16)]
    return small_kernel(chain, body, (keep, received), outs)


def add_low(chain, keep, received):
    def body(token_ref, keep_ref, came_ref, out_ref):
        out_ref[...] = low(keep_ref[...].astype(jnp.float32) + came_ref[...].astype(jnp.float32))

    return small_kernel(chain, body, (keep, received), [(keep.shape, jnp.bfloat16)])[0]


def join_rows(chain, piece, received, bit):
    rows = piece.shape[0]

    def body(token_ref, own_ref, came_ref, out_ref):
        mine = bit_of(token_ref, bit)
        out_ref[rows_at(mine, rows), :] = own_ref[...]
        out_ref[rows_at(1 - mine, rows), :] = came_ref[...]

    shape = (2 * rows,) + piece.shape[1:]
    return small_kernel(chain, body, (piece, received), [(shape, piece.dtype)])[0]


def finish(chain, piece, received, cuts, outs, vectors=None):
    rows = piece.shape[0]

    def body(token_ref, *refs):
        core = token_ref[0, 1]
        for step in range(2):
            part = core ^ step
            for out, row, col, begin, size in cuts:
                where = pl.ds(pl.multiple_of(row + part * rows, rows), rows)
                refs[2 + out][where, col : col + size] = refs[step][:, begin : begin + size].astype(jnp.float32)
        if vectors:
            last = refs[0].shape[1] - 128
            turned = [refs[step][:, last:].astype(jnp.float32).T for step in range(2)]
            swap = core == 1
            turned = jnp.concatenate(
                [jnp.where(swap, turned[1], turned[0]), jnp.where(swap, turned[0], turned[1])], axis=1
            )
            for out, row, col, index in vectors:
                refs[2 + out][row : row + 1, col : col + 2 * rows] = turned[index : index + 1, :]

    return small_kernel(chain, body, (piece, received), outs)


HALVE, WHOLE, DOUBLE = range(3)


def rounds_of(bits):
    return [(HALVE, bit) for bit in bits[:-1]] + [(WHOLE, bits[-1])] + [(DOUBLE, bit) for bit in reversed(bits[:-1])]


class Chunk:
    def __init__(self, chain, keep, send, rounds):
        self.chain = chain
        self.kept, self.send = keep, send
        self.rounds, self.at = rounds, 0
        self.launch()

    def launch(self):
        self.received = send_wide(self.send, self.rounds[self.at][1])

    def advance(self):
        kind, bit = self.rounds[self.at]
        self.at += 1
        following, next_bit = self.rounds[self.at]
        if kind == DOUBLE:
            self.kept = self.send = join_rows(self.chain, self.kept, self.received, bit)
        elif following == HALVE:
            self.kept, self.send = add_split(self.chain, self.kept, self.received, next_bit)
        else:
            self.kept = self.send = add_low(self.chain, self.kept, self.received)
        self.launch()

    def left(self):
        return len(self.rounds) - 1 - self.at

    def finish(self, cuts, outs, vectors=None):
        return finish(self.chain, self.kept, self.received, cuts, outs, vectors)


def near_first(bits):
    return rounds_of(list(range(bits)))


def mid_first(bits):
    return rounds_of([0, 2, 1] + list(range(3, bits)))


def far_first(bits):
    return rounds_of([0] + list(range(2, bits)) + [1])


ORDER = dict(a=near_first, c=near_first, d=near_first)
SCHEDULE = ("a", "acac", "acdadcdcdadcadcd")


def whole_rows(
    target, memory, target_lens, source_lens, self_in, self_out, cross_q, cross_kv, cross_out, ffn_in, ffn_in_bias,
    ffn_out, ffn_out_bias, norm_gain, norm_bias, cotangent,
):
    f32, bf16 = jnp.float32, jnp.bfloat16
    _, half, width = target.shape
    length = 2 * half
    hidden = ffn_in.shape[1]
    wide = lax.axis_index("wide")
    place = jnp.stack([lax.axis_index("narrow"), wide % 2, wide]).astype(jnp.int32)
    place = jnp.concatenate([place, target_lens[0], source_lens[0]])
    chain = Chain()

    def other_half(values):
        return lax.ppermute(values, "narrow", [(0, 1), (1, 0)])

    own_t, own_m, own_c = target[0], memory[0], cotangent[0]
    other_t, other_m, other_c = other_half(own_t), other_half(own_m), other_half(own_c)
    square = (length, width)
    attn_shape = (HEADS, length, length)
    macs = length * width * width
    rows = width // 4

    vectors = jnp.concatenate(
        [norm_gain, norm_bias, ffn_out_bias[None], jnp.zeros((1, width), f32), ffn_in_bias.reshape(-1, width)], axis=0
    )
    vectors = jnp.pad(vectors, ((0, -vectors.shape[0] % 8), (0, 0)))

    step = Kernel(chain, place)
    step.far(own=own_t)
    step.prefetch(self_in=self_in, self_out=self_out, cross_q=cross_q, cross_kv=cross_kv, cross_out=cross_out, own_t=own_t)
    step.near_out(
        triple_own=((half, 3 * width), bf16), self_bias=((length, length), f32), cross_bias=((length, length), f32)
    )
    (
        self_in_near, self_out_near, cross_q_near, cross_kv_near, cross_out_near, own_near, triple_own, self_bias, cross_bias,
    ) = step.run(first_body, 8 * macs, 12)

    step = Kernel(chain, place)
    step.near(other=other_t)
    step.near(self_in=self_in_near, self_out=self_out_near, own=own_near, triple_own=triple_own, bias=self_bias)
    step.far_out(triple=((length, 3 * width), bf16), mix=(square, bf16))
    step.heads_out(attn=(attn_shape, bf16))
    step.near_out(centre_first=(square, f32))
    step.hold(work=((2, length, length), f32))
    triple, self_mix, self_attn, centre_first = step.run(self_forward_body, 24 * macs, 16)

    step = Kernel(chain, place)
    step.halves(memory=(own_m, other_m))
    step.near(centre_first=centre_first, cross_q=cross_q_near, cross_kv=cross_kv_near, cross_out=cross_out_near)
    step.near(vectors=vectors, bias=cross_bias)
    step.copy_out(centre_first_far=("centre_first", square, f32))
    step.far_out(query=(square, bf16), pairs=((length, 2 * width), bf16), mix=(square, bf16))
    step.heads_out(attn=(attn_shape, bf16))
    step.near_out(centre_second=(square, f32))
    step.hold(work=((2, length, length), f32))
    step.prefetch(ffn_in=ffn_in, ffn_out=ffn_out)
    (
        centre_first, query, pairs, cross_mix, cross_attn, centre_second, ffn_in_near, ffn_out_near,
    ) = step.run(cross_forward_body, 24 * macs, 16)

    step = Kernel(chain, place)
    step.near(centre_second=centre_second, ffn_in=ffn_in_near, ffn_out=ffn_out_near, vectors=vectors)
    step.halves(cotangent=(own_c, other_c))
    step.far_out(output=((half, width), bf16))
    step.near_out(
        grad_second=(square, f32), sums=((8, width), f32), in_sums=((1, hidden), f32),
        keep=((rows, 2 * hidden), f32), send=((rows, 2 * hidden), bf16),
    )
    step.prefetch(cross_out=cross_out, query=query)
    step.hold(
        second=(square, bf16), active=((length, hidden), bf16), slope=((length, hidden), f32), outer=(square, bf16),
        inner=((length, hidden), bf16), held=((2, length, width), f32),
    )
    output, grad, sums, in_sums, feed_keep, feed_send, cross_out_near, query = step.run(feed_body, 40 * macs, 26)

    bits = lax.axis_size("wide").bit_length() - 1
    orders = {name: ORDER[name](bits) for name in ORDER}
    chunk_a = Chunk(chain, feed_keep, feed_send, orders["a"])
    chunks = dict(a=chunk_a)
    step = Kernel(chain, place)
    step.near(grad=grad, sums=sums, in_sums=in_sums, centre_second=centre_second, cross_out=cross_out_near, query=query)
    step.near(vectors=vectors)
    step.near_out(
        small=((16, half), f32), grad_second=(square, f32), grad_low=(square, bf16), dmix=(square, bf16),
        dmix_t=(square, bf16), query_t=(square, bf16),
    )
    step.prefetch(pairs=pairs, mix=cross_mix)
    step.hold(work=((8, width), f32))
    small, grad_second, grad_low, dmix, dmix_t, query_t, pairs, cross_mix = step.run(between_body, 24 * macs * 4, 8)
    for name in SCHEDULE[0]:
        chunks[name].advance()

    step = Kernel(chain, place)
    step.near(grad_second=grad_second, small=small, vectors=vectors, grad_low=grad_low, dmix=dmix, dmix_t=dmix_t)
    step.near(query_t=query_t, query=query, pairs=pairs, mix=cross_mix)
    step.heads("attn", cross_attn, 0, HEADS // 2)
    step.far(cross_kv=cross_kv)
    step.halves(memory=(own_m, other_m))
    step.far(centre_first=centre_first, cross_q=cross_q, self_mix=self_mix)
    step.far_out(memory_grad=((half, width), f32))
    step.near_out(
        grad_first=(square, f32), keep=((rows, 5 * width + 128), f32), send=((rows, 5 * width + 128), bf16)
    )
    step.prefetch(self_out=self_out, triple=triple, mix=self_mix)
    step.hold(
        work=((2, length, length), f32), dscores=((2, length, length), bf16),
        first=(square, bf16), grad=(square, bf16), dquery=(square, bf16), dpairs_t=((2 * width, length), bf16), sums=((8, width), f32), turned=((128, half), f32),
    )
    memory_grad, grad_first, cross_keep, cross_send, self_out_near, triple, self_mix = step.run(cross_back_body, 48 * macs * 4, 24)

    chunk_c = chunks["c"] = Chunk(chain, cross_keep, cross_send, orders["c"])
    for name in SCHEDULE[1]:
        chunks[name].advance()

    def self_part(first, last):
        span = (last - first) * PAIR
        step = Kernel(chain, place)
        step.near(grad_first=grad_first)
        step.near(self_out=self_out_near, triple=triple, mix=self_mix)
        step.heads("attn", self_attn, first, last)
        step.halves(target=(own_t, other_t))
        step.far(self_in=self_in)
        step.far_out(target_grad=((half, width), f32))
        step.near_out(keep=((rows, 3 * span), f32), send=((rows, 3 * span), bf16))
        step.hold(
            grad=(square, bf16), dmix=((length, span), bf16), dmix_t=((span, length), bf16),
            query_t=((span, length), bf16), dquery=((length, span), bf16), dpairs_t=((2 * span, length), bf16),
        )
        return step.run(functools.partial(self_back_body, (first, last)), 24 * macs * 12, 16)

    target_grad, keep, send = self_part(0, HEADS // 2)
    chunk_d = chunks["d"] = Chunk(chain, keep, send, orders["d"])
    groups = hidden // width
    endings = dict(
        a=(
            [(0, group * half, 0, group * width, width) for group in range(groups)] + [(1, 0, 0, hidden, hidden)],
            [((groups * half, width), f32), ((half, hidden), f32)],
        ),
        c=(
            [(0, 0, 0, 0, width), (1, 0, 0, width, 2 * width), (2, 0, 0, 3 * width, width), (3, 0, 0, 4 * width, width)],
            [
                ((half, width), f32), ((half, 2 * width), f32), ((half, width), f32), ((half, width), f32),
                ((3, half), f32), ((3, half), f32), ((1, half), f32), ((1, groups * half), f32),
            ],
            [(4, 0, 0, 5), (4, 1, 0, 3), (4, 2, 0, 0), (5, 0, 0, 6), (5, 1, 0, 4), (5, 2, 0, 1), (6, 0, 0, 2)]
            + [(7, 0, row * half, 8 + row) for row in range(groups)],
        ),
        d=([(0, 0, 0, 0, 3 * width)], [((half, 3 * width), f32)]),
    )
    finished = {}
    for name in SCHEDULE[2]:
        if chunks[name].left():
            chunks[name].advance()
        elif name not in finished:
            finished[name] = chunks[name].finish(*endings[name])
    ffn_out_g, ffn_in_g = finished["a"]
    cross_q_g, cross_kv_g, cross_out_g, self_out_g, gain_g, shift_g, out_bias_g, in_bias_g = finished["c"]
    (self_in_g,) = finished["d"]
    return (
        output[None],
        target_grad[None],
        memory_grad[None],
        self_in_g,
        self_out_g,
        cross_q_g,
        cross_kv_g,
        cross_out_g,
        ffn_in_g,
        in_bias_g[0],
        ffn_out_g,
        out_bias_g[0],
        gain_g,
        shift_g,
    )


def fits_whole_rows(mesh, target, lens):
    wide, narrow = mesh.shape["wide"], mesh.shape["narrow"]
    rows, length, width = target.shape
    documents = lens.shape[1]
    return (
        narrow == 2
        and rows == wide
        and wide >= 2
        and wide & (wide - 1) == 0
        and length <= 512
        and documents == DOCUMENTS
        and width == HEADS * HEAD_DIM
        and width % (32 * wide) == 0
    )


def solution(mesh):
    in_specs = (
        P("wide", "narrow", None),
        P("wide", "narrow", None),
        P("wide", None),
        P("wide", None),
        P(),
        P(),
        P(),
        P(),
        P(),
        P(),
        P(),
        P(),
        P(),
        P(),
        P(),
        P("wide", "narrow", None),
    )
    out_specs = (
        P("wide", "narrow", None),
        P("wide", "narrow", None),
        P("wide", "narrow", None),
        P("narrow", None),
        P("narrow", None),
        P("narrow", None),
        P("narrow", None),
        P("narrow", None),
        P("narrow", None),
        P("narrow"),
        P("narrow", None),
        P("narrow"),
        P(None, "narrow"),
        P(None, "narrow"),
    )

    def layer(*arrays):
        body = whole_rows if fits_whole_rows(mesh, arrays[0], arrays[2]) else local
        return jax.shard_map(body, mesh=mesh, in_specs=in_specs, out_specs=out_specs, check_vma=False)(*arrays)

    return layer
```
